32 devices in a mesh: rep: 16 (over z, y, x), fsdp: 2 (over core).
Axes of the slice: x: 2, y: 2, z: 4, core: 2. Of those that a mesh axis runs over, the one named last changes fastest.
Arguments:
- tokens: bfloat16 [16384, 768], P(('rep', 'fsdp')), may hold values from -6 to 6
- attn_gain: bfloat16 [768], P('fsdp'), may hold values from 0.5 to 1.5
- qkv_weight: bfloat16 [768, 2304], P('fsdp'), may hold values from -0.21875 to 0.21875
- out_weight: bfloat16 [768, 768], P('fsdp'), may hold values from -1.75 to 1.75
- mlp_gain: bfloat16 [768], P('fsdp'), may hold values from 0.5 to 1.5
- in_weight: bfloat16 [768, 2304], P('fsdp'), may hold values from -0.21875 to 0.21875
- down_weight: bfloat16 [1152, 768], P('fsdp'), may hold values from -0.25 to 0.25
- seq_len: int32 [16, 4], P('rep'), may hold values from 0 to 1024, as said below
- cotangent: bfloat16 [16384, 768], P(('rep', 'fsdp')), may hold values from -6 to 6
Outputs:
- result: bfloat16 [16384, 768], P(('rep', 'fsdp'))
- grad_tokens: bfloat16 [16384, 768], P(('rep', 'fsdp'))
- grad_attn_gain: float32 [768], P('fsdp')
- grad_qkv_weight: float32 [768, 2304], P('fsdp')
- grad_out_weight: float32 [768, 768], P('fsdp')
- grad_mlp_gain: float32 [768], P('fsdp')
- grad_in_weight: float32 [768, 2304], P('fsdp')
- grad_down_weight: float32 [1152, 768], P('fsdp')
The draws below stay inside these ranges and needn't reach their ends.
Inputs may be any that keep to these rules, and one draw needn't show every extreme that they name: `seq_len`: each group's row sums to 1024; its first 1 to 4 entries are positive and the rest zero; in each group one sequence covers slots 512 - 1 and 512; some group holds a single sequence of 1024.
All inputs are finite; a program needn't handle non-finite values.
Results may differ from the reference program's by a relative error of at most 0.018.
Values may be sent and summed in bfloat16 or wider, within the bound.
No kernel may reach another device: no remote copies, remote signals or barrier semaphores. Data moves between devices by JAX's collectives and lax.ppermute only.
A program may use at most 128 MiB of HBM per device.

```python
import jax
import jax.numpy as jnp
from jax import lax

D = 768
HEADS = 12
HEAD_DIM = 64
FF = 1152
TOK_DEV = 512
SLOTS = 4
GROUP_TOK = 1024
TOKENS = 16384
N_REP = 16


def draw_seq_len(key, part):
    key = jax.random.fold_in(key, 7)
    keys = jax.random.split(key, 3)
    counts = jax.random.randint(keys[0], (N_REP,), 1, SLOTS + 1)
    lone_group = jax.random.randint(keys[1], (), 0, N_REP)
    counts = jnp.where(jnp.arange(N_REP) == lone_group, 1, counts)

    def lengths_for(group_key, seq_count):
        cuts = jax.random.permutation(group_key, GROUP_TOK - 2)[:SLOTS - 1].astype(jnp.int32) + 1
        cuts = jnp.where(cuts >= TOK_DEV, cuts + 1, cuts)
        used = jnp.arange(SLOTS - 1) < seq_count - 1
        cuts = jnp.sort(jnp.where(used, cuts, GROUP_TOK)).astype(jnp.int32)
        ends = jnp.concatenate([cuts, jnp.full((1,), GROUP_TOK, jnp.int32)])
        begins = jnp.concatenate([jnp.zeros((1,), jnp.int32), cuts])
        return ends - begins
    return jax.vmap(lengths_for)(jax.random.split(keys[2], N_REP), counts).astype(jnp.int32)


def spiked(entries, own_key, source, target, blocks, factor):
    def block_of(axis_at):
        return (jnp.arange(entries.shape[axis_at]) // (entries.shape[axis_at] // blocks)).reshape((-1,) + (1,) * (entries.ndim - 1 - axis_at))

    first = jax.random.permutation(own_key, blocks)[block_of(target)]
    second = (block_of(target) + blocks // 2) % blocks
    return jnp.where((block_of(source) == first) | (block_of(source) == second), factor * entries, entries)


def shard_levels(key, shape, cuts, smallest, top_value):
    level = 1.0
    for position, shards_of in cuts:
        draws = jax.random.uniform(jax.random.fold_in(jax.random.fold_in(key, 6), position), (shards_of,), jnp.float32, smallest / len(cuts), top_value / len(cuts))
        level = level * jnp.repeat(jnp.exp(draws), shape[position] // shards_of).reshape((-1,) + (1,) * (len(shape) - 1 - position))
    return level


def bell_draw(rng, shape, deviation, most, shards=(), kind=jnp.bfloat16):
    drawn = jax.random.normal(rng, shape, jnp.float32) * deviation
    if len(shards) > 0:
        drawn = shard_levels(rng, shape, shards, -0.22, 0.18) * drawn
    return jnp.clip(drawn, min=-most, max=most).astype(kind)


def bell_draw_with(stream_key, extent, spread, reach, pieces, heavy, kind=jnp.bfloat16):
    result = spread * jax.random.normal(stream_key, extent, jnp.float32)
    if pieces:
        result = result * shard_levels(stream_key, extent, pieces, -0.22, 0.18)
    return jnp.clip(spiked(result, jax.random.fold_in(stream_key, 3), *heavy), -reach, reach).astype(kind)


def setup_inputs(seed: int = 0) -> dict:
    key_of = jax.random.split(jax.random.key(seed), 10)
    tokens = bell_draw(key_of[0], (TOKENS, D), 1.0, 6.0, ((0, 32),))
    attn_gain = jnp.clip(1.0 + 0.1 * jax.random.normal(key_of[1], (D,), jnp.float32), 0.5, 1.5).astype(jnp.bfloat16)
    qkv_weight = bell_draw(key_of[2], (D, 3 * D), D ** -0.5, 0.21875, ((0, 2),))
    out_weight = bell_draw(key_of[3], (D, D), (D // 64) ** -0.5, 1.75, ((0, 2),))
    mlp_gain = jnp.clip(1.0 + 0.1 * jax.random.normal(key_of[4], (D,), jnp.float32), 0.5, 1.5).astype(jnp.bfloat16)
    in_weight = bell_draw(key_of[5], (D, 2 * FF), D ** -0.5, 0.21875, ((0, 2),))
    down_weight = bell_draw(key_of[6], (FF, D), (FF // 2) ** -0.5, 0.25, ((0, 2),))
    seq_len = draw_seq_len(jax.random.fold_in(key_of[9], 71), 0)
    cotangent = bell_draw_with(key_of[8], (TOKENS, D), 1.0, 6.0, ((0, 32),), (0, 1, 32, 2.75))
    return {"tokens": tokens, "attn_gain": attn_gain, "qkv_weight": qkv_weight, "out_weight": out_weight, "mlp_gain": mlp_gain, "in_weight": in_weight, "down_weight": down_weight, "seq_len": seq_len, "cotangent": cotangent}


epsilon = 1e-05
rope_base = 160000.0

@jax.custom_vjp
def low(v):
    return lax.optimization_barrier(v.astype(jnp.bfloat16)).astype(jnp.float32)

@jax.custom_vjp
def low_back(v):
    return v

def low_keep(v):
    return (low(v), None)

def low_pass(kept, grad):
    return (grad,)

def back_keep(v):
    return (v, None)

def back_low(kept, grad):
    return (low(grad),)
low.defvjp(low_keep, low_pass)
low_back.defvjp(back_keep, back_low)

def layout(lengths, slot_count):
    slots = jnp.arange(slot_count, dtype=jnp.int32)
    ends = jnp.cumsum(lengths).astype(jnp.int32)
    segment = lax.optimization_barrier(jnp.sum((slots[:, None] >= ends[None, :]).astype(jnp.int32), axis=1)).astype(jnp.int32)
    begins = lax.optimization_barrier(jnp.max(jnp.where(ends[None, :] <= slots[:, None], ends[None, :], 0), axis=1)).astype(jnp.int32)
    return (segment, (slots - begins).astype(jnp.int32))

def rope_angles(places):
    half_dim = HEAD_DIM // 2
    freq = jnp.exp(-jnp.log(rope_base) * (2.0 * jnp.arange(half_dim, dtype=jnp.float32) / HEAD_DIM))
    return places.astype(jnp.float32)[:, None] * freq[None, :]

def rotate(values, angles):
    half_dim = values.shape[-1] // 2
    first_half = values[..., :half_dim]
    second_half = values[..., half_dim:]
    cosine = jnp.cos(angles)[:, None, :]
    sine_part = jnp.sin(angles)[:, None, :]
    return jnp.concatenate([first_half * cosine - second_half * sine_part, second_half * cosine + first_half * sine_part], axis=-1)

def norm_rows(values, gain_vec):
    row_mean = lax.optimization_barrier(jnp.mean(values, axis=-1, keepdims=True))
    centred = values - row_mean
    row_var = lax.optimization_barrier(jnp.mean(centred * centred, axis=-1, keepdims=True))
    return centred * lax.rsqrt(row_var + epsilon) * gain_vec

def attend_group(inputs):
    query, key, value, segment = inputs
    raw = jnp.einsum('qhd,khd->hqk', query, key, precision=lax.Precision.HIGHEST) * HEAD_DIM ** (-0.5)
    scores = low_back(raw)
    allowed = (segment[:, None] == segment[None, :])[None]
    scores = jnp.where(allowed, scores, -1e+30)
    probabilities = low(jax.nn.softmax(scores, axis=-1))
    return jnp.einsum('hqk,khd->qhd', probabilities, value, precision=lax.Precision.HIGHEST)

def reference(tokens, attn_gain, qkv_weight, out_weight, mlp_gain, in_weight, down_weight, seq_len, cotangent):
    segments, places = jax.vmap(lambda lengths: layout(lengths, GROUP_TOK))(seq_len)
    angles = rope_angles(places.reshape(-1))
    highest = lax.Precision.HIGHEST

    def forward(inputs, gain_one, w_qkv, w_out, gain_two, w_in, w_down):
        row_count = inputs.shape[0]
        normed_one = low(norm_rows(inputs, gain_one))
        qkv = low_back(jnp.dot(normed_one, w_qkv, precision=highest))
        query = low(rotate(qkv[:, :D].reshape(row_count, HEADS, HEAD_DIM), angles))
        key = low(rotate(qkv[:, D:2 * D].reshape(row_count, HEADS, HEAD_DIM), angles))
        value = low(qkv[:, 2 * D:].reshape(row_count, HEADS, HEAD_DIM))

        def grouped(array):
            return array.reshape(N_REP, GROUP_TOK, HEADS, HEAD_DIM)
        attended = lax.map(jax.checkpoint(attend_group), (grouped(query), grouped(key), grouped(value), segments))
        merged = low(low_back(attended.reshape(row_count, D)))
        resid = inputs + low_back(jnp.dot(merged, w_out, precision=highest))
        normed_two = low(norm_rows(resid, gain_two))
        lifted = low_back(jnp.dot(normed_two, w_in, precision=highest))
        act = low(jax.nn.gelu(lifted[:, :FF], approximate=False) * lifted[:, FF:])
        return resid + low_back(jnp.dot(act, w_down, precision=highest))
    primals = (tokens.astype(jnp.float32), attn_gain.astype(jnp.float32), qkv_weight.astype(jnp.float32), out_weight.astype(jnp.float32), mlp_gain.astype(jnp.float32), in_weight.astype(jnp.float32), down_weight.astype(jnp.float32))
    output, backward = jax.vjp(forward, *primals)
    grads = backward(cotangent.astype(jnp.float32))
    return (output.astype(jnp.bfloat16), grads[0].astype(jnp.bfloat16), grads[1], grads[2], grads[3], grads[4], grads[5], grads[6])
```

```python
import functools

import jax
import jax.numpy as jnp
from jax import lax
from jax.experimental import pallas as pl
from jax.experimental.pallas import tpu as pltpu
from jax.sharding import PartitionSpec as P

D = 768
HEADS = 12
HEAD_DIM = 64
FF = 1152
HALF = D // 2
LANES = 128
PAIRS = D // LANES
QKV = 3 * D
PACK = 2 * FF + FF + D

epsilon = 1e-05
rope_base = 160000.0
BLOCKED = -(2.0**100)
F32 = jnp.float32
BF16 = jnp.bfloat16
MIB = 1 << 20

NN = (((1,), (0,)), ((), ()))
NT = (((1,), (1,)), ((), ()))
TN = (((0,), (0,)), ((), ()))


def mm(a, b, dims=NN):
    return lax.dot_general(a, b, dims, preferred_element_type=F32)


def vmem():
    return pl.BlockSpec(memory_space=pltpu.VMEM)


def anywhere():
    return pl.BlockSpec(memory_space=pl.ANY)


def smem():
    return pl.BlockSpec(memory_space=pltpu.SMEM)


def params(mib):
    return pltpu.CompilerParams(vmem_limit_bytes=mib * MIB)


def cost(flops, nbytes):
    return pl.CostEstimate(flops=int(flops), bytes_accessed=int(nbytes), transcendentals=0)


def halves_in(own_ref, peer_ref, whole, sems, slot, core):
    rows = own_ref.shape[0]
    mine = pl.multiple_of(core * rows, 16)
    other = pl.multiple_of((1 - core) * rows, 16)
    return (
        pltpu.make_async_copy(own_ref, whole.at[pl.ds(mine, rows), :], sems.at[slot]),
        pltpu.make_async_copy(peer_ref, whole.at[pl.ds(other, rows), :], sems.at[slot + 1]),
    )


def lane_in_head(shape):
    return lax.broadcasted_iota(jnp.int32, shape, 1) % HEAD_DIM


def swap_halves(values):
    place = lane_in_head(values.shape)
    return jnp.where(
        place < HEAD_DIM // 2,
        pltpu.roll(values, LANES - HEAD_DIM // 2, 1),
        pltpu.roll(values, HEAD_DIM // 2, 1),
    )


def normalize(values):
    row_mean = jnp.mean(values, axis=-1, keepdims=True)
    centred = values - row_mean
    row_var = jnp.mean(centred * centred, axis=-1, keepdims=True)
    inverse = lax.rsqrt(row_var + epsilon)
    return centred * inverse, inverse


def project_kernel(core_ref, x_ref, gain_ref, own_ref, peer_ref, cos_ref, sin_ref, n_ref, q_ref, kv_ref, w_ref, sems):
    core = core_ref[0]
    copies = halves_in(own_ref, peer_ref, w_ref, sems, 0, core)
    for copy in copies:
        copy.start()
    rows = 256
    for r in range(x_ref.shape[0] // rows):
        part = pl.ds(r * rows, rows)
        hat, _ = normalize(x_ref[part, :].astype(F32))
        n_ref[part, :] = (hat * gain_ref[...]).astype(BF16)
    for copy in copies:
        copy.wait()
    scale = HEAD_DIM**-0.5
    for r in range(x_ref.shape[0] // rows):
        part = pl.ds(r * rows, rows)
        normed = n_ref[part, :]
        cosine, sine = cos_ref[part, :], sin_ref[part, :]
        for which in range(3):
            for half in range(2):
                at = which * D + half * HALF
                out = mm(normed, w_ref[:, at : at + HALF])
                for tile in range(HALF // LANES):
                    piece = out[:, tile * LANES : (tile + 1) * LANES]
                    cols = pl.ds(half * HALF + tile * LANES, LANES)
                    if which < 2:
                        piece = piece * cosine + swap_halves(piece) * sine
                    if which == 0:
                        q_ref[part, cols] = (piece * scale).astype(BF16)
                    else:
                        kv_ref[which - 1, part, cols] = piece.astype(BF16)


def project(core, x, gain, own, peer, cosine, sine):
    rows = x.shape[0]
    return pl.pallas_call(
        project_kernel,
        out_shape=(
            jax.ShapeDtypeStruct((rows, D), BF16),
            jax.ShapeDtypeStruct((rows, D), BF16),
            jax.ShapeDtypeStruct((2, rows, D), BF16),
        ),
        in_specs=[smem(), vmem(), vmem(), anywhere(), anywhere(), vmem(), vmem()],
        out_specs=(vmem(), vmem(), vmem()),
        scratch_shapes=[pltpu.VMEM((D, QKV), BF16), pltpu.SemaphoreType.DMA((2,))],
        compiler_params=params(40),
        cost_estimate=cost(2 * rows * D * QKV, 8 * MIB),
        name="project",
    )(core, x, gain, own, peer, cosine, sine)


def attend_kernel(q_ref, ko_ref, vo_ref, kp_ref, vp_ref, mq_ref, mk_ref, att_ref, low_ref, lse_ref):
    rows = q_ref.shape[0]
    tile = 256
    keys = jnp.concatenate([ko_ref[0], kp_ref[0]], axis=0)
    values = jnp.concatenate([vo_ref[0], vp_ref[0]], axis=0)
    key_first = lax.broadcasted_iota(jnp.int32, keys.shape, 1) < HEAD_DIM
    one = jnp.ones_like(values)
    mask_keys = mk_ref[...]
    k_both = (jnp.where(key_first, keys, mask_keys), jnp.where(key_first, mask_keys, keys))
    v_both = (jnp.where(key_first, values, one), jnp.where(key_first, one, values))
    first = lax.broadcasted_iota(jnp.int32, (tile, LANES), 1) < HEAD_DIM
    for t in range(rows // tile):
        part = pl.ds(t * tile, tile)
        query, mask_q = q_ref[part, :], mq_ref[part, :]
        sums, peaks = [], []
        for head in range(2):
            side = first if head == 0 else jnp.logical_not(first)
            scores = mm(jnp.where(side, query, mask_q), k_both[head], NT)
            peak = jnp.max(scores, axis=-1, keepdims=True)
            weights = jnp.exp(scores - peak).astype(BF16)
            sums.append(mm(weights, v_both[head]))
            peaks.append(peak)
        numer = jnp.where(first, sums[0], sums[1])
        denom = jnp.where(first, pltpu.roll(sums[0], HEAD_DIM, 1), pltpu.roll(sums[1], HEAD_DIM, 1))
        out = numer / denom
        att_ref[part, :] = out
        low_ref[part, :] = out.astype(BF16)
        lse_ref[part, :] = jnp.where(first, peaks[0], peaks[1]) + jnp.log(denom)


def kv_specs(rows):
    return [
        pl.BlockSpec((1, rows, LANES), lambda i: (0, 0, i)),
        pl.BlockSpec((1, rows, LANES), lambda i: (1, 0, i)),
    ]


def attend(query, kv_own, kv_peer, mask_q, mask_k):
    rows = query.shape[0]
    keys = mask_k.shape[0]
    pair = pl.BlockSpec((rows, LANES), lambda i: (0, i))
    whole = lambda n: pl.BlockSpec((n, LANES), lambda i: (0, 0))
    return pl.pallas_call(
        attend_kernel,
        grid=(PAIRS,),
        out_shape=(
            jax.ShapeDtypeStruct((rows, D), F32),
            jax.ShapeDtypeStruct((rows, D), BF16),
            jax.ShapeDtypeStruct((rows, D), F32),
        ),
        in_specs=[pair] + kv_specs(rows) + kv_specs(rows) + [whole(rows), whole(keys)],
        out_specs=(pair, pair, pair),
        compiler_params=params(40),
        cost_estimate=cost(16 * rows * keys * D, 8 * MIB),
        name="attend",
    )(query, kv_own, kv_own, kv_peer, kv_peer, mask_q, mask_k)


def middle_kernel(
    core_ref, x_ref, low_ref, dy_ref, gain_ref,
    oo_ref, op_ref, io_ref, ip_ref, do_ref, dp_ref,
    result_ref, n2_ref, act_ref, dl_ref, dres_ref, dproj_ref, datt_ref, dgain_ref,
    wo_ref, wi_ref, wd_ref, sems,
):
    core = core_ref[0]
    copies = (
        halves_in(oo_ref, op_ref, wo_ref, sems, 0, core),
        halves_in(io_ref, ip_ref, wi_ref, sems, 2, core),
        halves_in(do_ref, dp_ref, wd_ref, sems, 4, core),
    )
    for pair in copies:
        for copy in pair:
            copy.start()
    for pair in copies:
        for copy in pair:
            copy.wait()
    gain = gain_ref[...]
    rows = 256
    block = 384
    total = jnp.zeros((1, D), F32)
    for r in range(x_ref.shape[0] // rows):
        part = pl.ds(r * rows, rows)
        resid = x_ref[part, :].astype(F32) + mm(low_ref[part, :], wo_ref[...])
        hat, inverse = normalize(resid)
        n2 = (hat * gain).astype(BF16)
        n2_ref[part, :] = n2
        dy = dy_ref[part, :]
        for b in range(FF // block):
            cols = slice(b * block, (b + 1) * block)
            gate_cols = slice(FF + b * block, FF + (b + 1) * block)
            lift = mm(n2, wi_ref[:, cols])
            gate = mm(n2, wi_ref[:, gate_cols])
            d_act = mm(dy, wd_ref[cols, :], NT)
            cdf = 0.5 + 0.5 * lax.erf(lift * (0.5**0.5))
            bell = jnp.exp(-0.5 * lift * lift) * 0.3989422804014327
            gelu = lift * cdf
            act_ref[part, cols] = (gelu * gate).astype(BF16)
            dl_ref[part, cols] = (d_act * gate * (cdf + lift * bell)).astype(BF16)
            dl_ref[part, gate_cols] = (d_act * gelu).astype(BF16)
        result_ref[part, :] = (resid + mm(act_ref[part, :], wd_ref[...])).astype(BF16)
        d_normed = mm(dl_ref[part, :], wi_ref[...], NT)
        total = total + jnp.sum(d_normed * hat, axis=0, keepdims=True)
        d_hat = d_normed * gain
        d_resid = dy.astype(F32) + inverse * (
            d_hat
            - jnp.mean(d_hat, axis=-1, keepdims=True)
            - hat * jnp.mean(d_hat * hat, axis=-1, keepdims=True)
        )
        dres_ref[part, :] = d_resid
        d_proj = d_resid.astype(BF16)
        dproj_ref[part, :] = d_proj
        datt_ref[part, :] = mm(d_proj, wo_ref[...], NT).astype(BF16)
    dgain_ref[...] = total


def middle(core, x, low, dy, gain, w_out, w_in, w_down):
    rows = x.shape[0]
    low_shape = lambda n: jax.ShapeDtypeStruct((rows, n), BF16)
    return pl.pallas_call(
        middle_kernel,
        out_shape=(
            low_shape(D), low_shape(D), low_shape(FF), low_shape(2 * FF),
            jax.ShapeDtypeStruct((rows, D), F32), low_shape(D), low_shape(D),
            jax.ShapeDtypeStruct((1, D), F32),
        ),
        in_specs=[smem()] + [vmem()] * 4 + [anywhere()] * 6,
        out_specs=(vmem(),) * 8,
        scratch_shapes=[
            pltpu.VMEM((D, D), BF16),
            pltpu.VMEM((D, 2 * FF), BF16),
            pltpu.VMEM((FF, D), BF16),
            pltpu.SemaphoreType.DMA((6,)),
        ],
        compiler_params=params(48),
        cost_estimate=cost(2 * rows * D * (2 * D + 6 * FF), 16 * MIB),
        name="middle",
    )(core, x, low, dy, gain, *w_out, *w_in, *w_down)


def store_down(ref, block):
    rest = block.shape[0] - HALF
    ref[:, 2 * FF : 2 * FF + D] = block[:HALF]
    ref[0:rest, 2 * FF + D : 3 * FF] = block[HALF:, :HALF]
    ref[rest : 2 * rest, 2 * FF + D : 3 * FF] = block[HALF:, HALF:]


def terms_kernel(core_ref, n2_ref, dl_ref, act_ref, dy_ref, low_ref, dproj_ref, peer_ref, down_ref, whole):
    other = pl.ds(pl.multiple_of((1 - core_ref[0]) * HALF, LANES), HALF)
    n2 = n2_ref[:, other]
    for b in range(2 * FF // 384):
        cols = slice(b * 384, (b + 1) * 384)
        peer_ref[:, cols] = mm(n2, dl_ref[:, cols], TN).astype(BF16)
    peer_ref[:, 3 * FF :] = mm(low_ref[:, other], dproj_ref[...], TN).astype(BF16)
    for b in range(FF // 384):
        rows = slice(b * 384, (b + 1) * 384)
        whole[rows, :] = mm(act_ref[:, rows], dy_ref[...], TN).astype(BF16)
    size = FF // 2
    store_down(peer_ref, whole[pl.ds(pl.multiple_of((1 - core_ref[0]) * size, 16), size), :])
    down_ref[...] = whole[pl.ds(pl.multiple_of(core_ref[0] * size, 16), size), :]


def terms_peer(core, n2, dl, act, dy, low, dproj):
    rows = n2.shape[0]
    return pl.pallas_call(
        terms_kernel,
        out_shape=(jax.ShapeDtypeStruct((HALF, PACK), BF16), jax.ShapeDtypeStruct((FF // 2, D), BF16)),
        in_specs=[smem()] + [vmem()] * 6,
        out_specs=(vmem(), vmem()),
        scratch_shapes=[pltpu.VMEM((FF, D), BF16)],
        compiler_params=params(40),
        cost_estimate=cost(2 * rows * D * (FF * 2 + D // 2), 10 * MIB),
        name="terms_peer",
    )(core, n2, dl, act, dy, low, dproj)


def terms_own_kernel(core_ref, n2_ref, dl_ref, low_ref, dproj_ref, down_ref, own_ref):
    mine = pl.ds(pl.multiple_of(core_ref[0] * HALF, LANES), HALF)
    n2 = n2_ref[:, mine]
    for b in range(2 * FF // 384):
        cols = slice(b * 384, (b + 1) * 384)
        own_ref[:, cols] = mm(n2, dl_ref[:, cols], TN).astype(BF16)
    own_ref[:, 3 * FF :] = mm(low_ref[:, mine], dproj_ref[...], TN).astype(BF16)
    store_down(own_ref, down_ref[...])


def terms_own(core, n2, dl, low, dproj, down):
    rows = n2.shape[0]
    return pl.pallas_call(
        terms_own_kernel,
        out_shape=jax.ShapeDtypeStruct((HALF, PACK), BF16),
        in_specs=[smem()] + [vmem()] * 5,
        out_specs=vmem(),
        compiler_params=params(40),
        cost_estimate=cost(2 * rows * D * (FF + D // 2), 10 * MIB),
        name="terms_own",
    )(core, n2, dl, low, dproj, down)


def split_three(values):
    high = values.astype(BF16)
    rest = values - high.astype(F32)
    mid = rest.astype(BF16)
    return high, mid, (rest - mid.astype(F32)).astype(BF16)


def place_three(values, place, others):
    high, mid, tail = split_three(-values)
    at = HEAD_DIM // 2
    out = jnp.where(place == at, high.astype(F32), others)
    out = jnp.where(place == at + 1, mid.astype(F32), out)
    return jnp.where(place == at + 2, tail.astype(F32), out)


def attend_back_kernel(
    q_ref, ko_ref, vo_ref, kp_ref, vp_ref, mq_ref, mk_ref, do_ref, att_ref, lse_ref, cos_ref, sin_ref,
    dq_ref, own_ref, peer_ref,
):
    rows = q_ref.shape[0]
    tile = 256
    query, grad = q_ref[...], do_ref[...]
    place = lane_in_head(query.shape)
    first = lax.broadcasted_iota(jnp.int32, query.shape, 1) < HEAD_DIM
    tile_first = first[:tile]
    product = grad.astype(F32) * att_ref[...]
    lse = pltpu.roll(lse_ref[...], HEAD_DIM, 1)
    mask_q = mq_ref[...].astype(F32)
    zero = jnp.zeros_like(mask_q)
    q_both, g_both = [], []
    for head in range(2):
        side = first if head == 0 else jnp.logical_not(first)
        delta = jnp.sum(jnp.where(side, product, 0.0), axis=-1, keepdims=True)
        q_both.append(jnp.where(side, query, place_three(lse, place, mask_q).astype(BF16)))
        wide = jnp.broadcast_to(delta, product.shape)
        g_both.append(jnp.where(side, grad, place_three(wide, place, zero).astype(BF16)))
    d_query = [jnp.zeros((rows, LANES), F32) for _ in range(2)]
    for source in range(2):
        k_ref, v_ref, out_ref = ((ko_ref, vo_ref, own_ref), (kp_ref, vp_ref, peer_ref))[source]
        for t in range(rows // tile):
            part = pl.ds(t * tile, tile)
            keys, values = k_ref[0, part, :], v_ref[0, part, :]
            marks = mk_ref[pl.ds(source * rows + t * tile, tile), :]
            d_keys, d_values = [], []
            for head in range(2):
                side = tile_first if head == 0 else jnp.logical_not(tile_first)
                probs = jnp.exp(mm(jnp.where(side, keys, marks), q_both[head], NT))
                d_probs = mm(jnp.where(side, values, marks), g_both[head], NT)
                d_scores = (probs * d_probs).astype(BF16)
                d_values.append(mm(probs.astype(BF16), grad))
                d_keys.append(mm(d_scores, query))
                d_query[head] = d_query[head] + mm(d_scores, keys, TN)
            out_ref[0, part, :] = jnp.where(tile_first, d_keys[0], d_keys[1]).astype(BF16)
            out_ref[1, part, :] = jnp.where(tile_first, d_values[0], d_values[1]).astype(BF16)
    d_q = jnp.where(first, d_query[0], d_query[1]) * HEAD_DIM**-0.5
    dq_ref[...] = (d_q * cos_ref[...] - swap_halves(d_q) * sin_ref[...]).astype(BF16)


def attend_back(query, kv_own, kv_peer, mask_q, mask_k, grad, att, lse, cosine, sine):
    rows = query.shape[0]
    keys = mask_k.shape[0]
    pair = pl.BlockSpec((rows, LANES), lambda i: (0, i))
    both = pl.BlockSpec((2, rows, LANES), lambda i: (0, 0, i))
    whole = lambda n: pl.BlockSpec((n, LANES), lambda i: (0, 0))
    return pl.pallas_call(
        attend_back_kernel,
        grid=(PAIRS,),
        out_shape=(
            jax.ShapeDtypeStruct((rows, D), BF16),
            jax.ShapeDtypeStruct((2, rows, D), BF16),
            jax.ShapeDtypeStruct((2, rows, D), BF16),
        ),
        in_specs=[pair] + kv_specs(rows) + kv_specs(rows)
        + [whole(rows), whole(keys), pair, pair, pair, whole(rows), whole(rows)],
        out_specs=(pair, both, both),
        compiler_params=params(40),
        cost_estimate=cost(40 * rows * keys * D, 12 * MIB),
        name="attend_back",
    )(query, kv_own, kv_own, kv_peer, kv_peer, mask_q, mask_k, grad, att, lse, cosine, sine)


def qkv_terms_kernel(core_ref, n1_ref, dq_ref, own_ref, got_ref, cos_ref, sin_ref, peer_ref, dqkv_ref):
    rows = n1_ref.shape[0]
    cosine, sine = cos_ref[...], sin_ref[...]
    other = pl.ds(pl.multiple_of((1 - core_ref[0]) * HALF, LANES), HALF)
    n1 = n1_ref[:, other]
    dqkv_ref[:, :D] = dq_ref[...]
    for pair in range(PAIRS):
        cols = slice(pair * LANES, (pair + 1) * LANES)
        d_key = own_ref[0, :, cols].astype(F32) + got_ref[0, :, cols].astype(F32)
        d_value = own_ref[1, :, cols].astype(F32) + got_ref[1, :, cols].astype(F32)
        d_key = d_key * cosine - swap_halves(d_key) * sine
        dqkv_ref[:, D + pair * LANES : D + (pair + 1) * LANES] = d_key.astype(BF16)
        dqkv_ref[:, 2 * D + pair * LANES : 2 * D + (pair + 1) * LANES] = d_value.astype(BF16)
    for b in range(QKV // 384):
        cols = slice(b * 384, (b + 1) * 384)
        peer_ref[:, cols] = mm(n1, dqkv_ref[:, cols], TN).astype(BF16)


def qkv_terms(core, n1, dq, own, got, cosine, sine):
    rows = n1.shape[0]
    return pl.pallas_call(
        qkv_terms_kernel,
        out_shape=(jax.ShapeDtypeStruct((HALF, QKV), BF16), jax.ShapeDtypeStruct((rows, QKV), BF16)),
        in_specs=[smem()] + [vmem()] * 6,
        out_specs=(vmem(), vmem()),
        compiler_params=params(40),
        cost_estimate=cost(rows * D * QKV, 10 * MIB),
        name="qkv_terms",
    )(core, n1, dq, own, got, cosine, sine)


def qkv_own_kernel(core_ref, n1_ref, dqkv_ref, own_ref):
    mine = pl.ds(pl.multiple_of(core_ref[0] * HALF, LANES), HALF)
    n1 = n1_ref[:, mine]
    for b in range(QKV // 384):
        cols = slice(b * 384, (b + 1) * 384)
        own_ref[:, cols] = mm(n1, dqkv_ref[:, cols], TN).astype(BF16)


def qkv_own(core, n1, dqkv):
    rows = n1.shape[0]
    return pl.pallas_call(
        qkv_own_kernel,
        out_shape=jax.ShapeDtypeStruct((HALF, QKV), BF16),
        in_specs=[smem()] + [vmem()] * 2,
        out_specs=vmem(),
        compiler_params=params(40),
        cost_estimate=cost(rows * D * QKV, 6 * MIB),
        name="qkv_own",
    )(core, n1, dqkv)


def input_kernel(core_ref, x_ref, gain_ref, dqkv_ref, own_ref, peer_ref, dres_ref, dx_ref, dgain_ref, w_ref, sems):
    copies = halves_in(own_ref, peer_ref, w_ref, sems, 0, core_ref[0])
    for copy in copies:
        copy.start()
    for copy in copies:
        copy.wait()
    gain = gain_ref[...]
    rows = 256
    total = jnp.zeros((1, D), F32)
    for r in range(x_ref.shape[0] // rows):
        part = pl.ds(r * rows, rows)
        hat, inverse = normalize(x_ref[part, :].astype(F32))
        d_normed = mm(dqkv_ref[part, :], w_ref[...], NT)
        total = total + jnp.sum(d_normed * hat, axis=0, keepdims=True)
        d_hat = d_normed * gain
        back = inverse * (
            d_hat
            - jnp.mean(d_hat, axis=-1, keepdims=True)
            - hat * jnp.mean(d_hat * hat, axis=-1, keepdims=True)
        )
        dx_ref[part, :] = (dres_ref[part, :] + back).astype(BF16)
    dgain_ref[...] = total


def input_grad(core, x, gain, dqkv, own, peer, dres):
    rows = x.shape[0]
    return pl.pallas_call(
        input_kernel,
        out_shape=(jax.ShapeDtypeStruct((rows, D), BF16), jax.ShapeDtypeStruct((1, D), F32)),
        in_specs=[smem()] + [vmem()] * 3 + [anywhere()] * 2 + [vmem()],
        out_specs=(vmem(), vmem()),
        scratch_shapes=[pltpu.VMEM((D, QKV), BF16), pltpu.SemaphoreType.DMA((2,))],
        compiler_params=params(40),
        cost_estimate=cost(2 * rows * D * QKV, 10 * MIB),
        name="input_grad",
    )(core, x, gain, dqkv, own, peer, dres)


BITS = {"x": 1, "y": 2, "near": 4, "far": 8}
ORDERS = (("x", "y", "near", "far"), ("y", "near", "x", "far"), ("near", "x", "y", "far"))


def trade(values, axis):
    return lax.ppermute(values, "rep", [(i, i ^ BITS[axis]) for i in range(16)])


def bit_of(axis):
    return (lax.axis_index("rep") // BITS[axis]) % 2


def scatter_sum(values, order):
    for axis in order:
        rows = values.shape[0] // 2
        bit = bit_of(axis)
        keep = lax.dynamic_slice_in_dim(values, bit * rows, rows, 0)
        got = trade(lax.dynamic_slice_in_dim(values, (1 - bit) * rows, rows, 0), axis)
        values = (keep.astype(F32) + got.astype(F32)).astype(BF16)
    return values


def gather_back(values, order):
    for axis in reversed(order):
        got = trade(values, axis)
        values = jnp.where(
            bit_of(axis) == 0, jnp.concatenate([values, got], 0), jnp.concatenate([got, values], 0)
        )
    return values


def sum_groups(values):
    if lax.axis_size("rep") != 16:
        return lax.psum(values.astype(F32), "rep")
    width = values.shape[1] // 3
    parts = [values[:, i * width : (i + 1) * width] for i in range(3)]
    parts = [scatter_sum(part, order) for part, order in zip(parts, ORDERS)]
    return jnp.concatenate([gather_back(part, order) for part, order in zip(parts, ORDERS)], axis=1)


def swap_cores(values):
    return lax.ppermute(values, "fsdp", [(0, 1), (1, 0)])


def layout(lengths, slot_count):
    slots = jnp.arange(slot_count, dtype=jnp.int32)
    ends = jnp.cumsum(lengths)
    segment = jnp.sum((slots[:, None] >= ends[None, :]).astype(jnp.int32), axis=1)
    begins = jnp.max(jnp.where(ends[None, :] <= slots[:, None], ends[None, :], 0), axis=1)
    return (segment, slots - begins)


def on_device(
    tokens, attn_gain, qkv_weight, out_weight, mlp_gain, in_weight, down_weight, seq_len, cotangent
):
    row_count = tokens.shape[0]
    core = lax.axis_index("fsdp")
    core_arg = core.astype(jnp.int32).reshape(1)
    both_gains = jnp.stack([attn_gain, mlp_gain])
    peer_qkv = swap_cores(qkv_weight)
    peer_gains = swap_cores(both_gains)
    peer_out = swap_cores(out_weight)
    peer_in = swap_cores(in_weight)
    peer_down = swap_cores(down_weight)
    gains = jnp.where(
        core == 0,
        jnp.concatenate([both_gains, peer_gains], axis=1),
        jnp.concatenate([peer_gains, both_gains], axis=1),
    ).astype(F32)
    gain_one, gain_two = gains[0:1], gains[1:2]

    key_seg, key_pos = layout(seq_len[0], 2 * row_count)
    own_seg = lax.dynamic_slice_in_dim(key_seg, core * row_count, row_count)
    peer_seg = lax.dynamic_slice_in_dim(key_seg, (1 - core) * row_count, row_count)
    own_pos = lax.dynamic_slice_in_dim(key_pos, core * row_count, row_count)
    place = jnp.arange(LANES, dtype=jnp.int32) % HEAD_DIM
    half_dim = HEAD_DIM // 2
    freq = jnp.exp(-jnp.log(rope_base) * (2.0 * (place % half_dim).astype(F32) / HEAD_DIM))
    angles = own_pos.astype(F32)[:, None] * freq[None, :]
    cosine = jnp.cos(angles)
    sine = jnp.sin(angles) * jnp.where(place < half_dim, -1.0, 1.0)[None, :]
    marks = place < half_dim
    mask_q = jnp.where(marks[None, :] & (own_seg[:, None] != place[None, :]), BLOCKED, 0.0).astype(BF16)
    both_seg = jnp.concatenate([own_seg, peer_seg])
    mask_k = jnp.where(
        marks[None, :], both_seg[:, None] == place[None, :], (place < half_dim + 3)[None, :]
    ).astype(BF16)

    n1, query, kv_own = project(core_arg, tokens, gain_one, qkv_weight, peer_qkv, cosine, sine)
    kv_peer = swap_cores(kv_own)
    att, low, lse = attend(query, kv_own, kv_peer, mask_q, mask_k)
    result, n2, act, dl, dres, dproj, datt, dgain_two = middle(
        core_arg, tokens, low, cotangent, gain_two,
        (out_weight, peer_out), (in_weight, peer_in), (down_weight, peer_down),
    )
    for_peer, down_own = terms_peer(core_arg, n2, dl, act, cotangent, low, dproj)
    from_peer = swap_cores(for_peer)
    own_terms = terms_own(core_arg, n2, dl, low, dproj, down_own)
    mlp_sum = sum_groups((own_terms.astype(F32) + from_peer.astype(F32)).astype(BF16))

    dq, dkv_own, dkv_peer = attend_back(
        query, kv_own, kv_peer, mask_q, mask_k, datt, att, lse, cosine, sine
    )
    dkv_got = swap_cores(dkv_peer)
    qkv_for_peer, dqkv = qkv_terms(core_arg, n1, dq, dkv_own, dkv_got, cosine, sine)
    qkv_from_peer = swap_cores(qkv_for_peer)
    qkv_mine = qkv_own(core_arg, n1, dqkv)
    qkv_sum = sum_groups((qkv_mine.astype(F32) + qkv_from_peer.astype(F32)).astype(BF16))
    grad_tokens, dgain_one = input_grad(
        core_arg, tokens, gain_one, dqkv, qkv_weight, peer_qkv, dres
    )
    gain_terms = lax.all_gather(
        jnp.concatenate([dgain_one, dgain_two], axis=1), ("rep", "fsdp"), axis=0, tiled=True
    )
    gain_sum = jnp.sum(gain_terms, axis=0)
    grad_gain_one = lax.dynamic_slice_in_dim(gain_sum, core * HALF, HALF)
    grad_gain_two = lax.dynamic_slice_in_dim(gain_sum, D + core * HALF, HALF)

    grad_in = mlp_sum[:, : 2 * FF].astype(F32)
    grad_out = mlp_sum[:, 3 * FF :].astype(F32)
    folded = mlp_sum[:, 2 * FF + D : 3 * FF]
    rest = FF // 2 - HALF
    grad_down = jnp.concatenate(
        [mlp_sum[:, 2 * FF : 2 * FF + D], jnp.concatenate([folded[:rest], folded[rest:]], axis=1)],
        axis=0,
    ).astype(F32)
    return (
        result,
        grad_tokens,
        grad_gain_one,
        qkv_sum.astype(F32),
        grad_out,
        grad_gain_two,
        grad_in,
        grad_down,
    )


def solution(mesh):
    rows = P(("rep", "fsdp"), None)
    vector, matrix = P("fsdp"), P("fsdp", None)
    in_specs = (rows, vector, matrix, matrix, vector, matrix, matrix, P("rep", None), rows)
    out_specs = (rows, rows, vector, matrix, matrix, vector, matrix, matrix)
    return jax.shard_map(
        on_device, mesh=mesh, in_specs=in_specs, out_specs=out_specs, check_vma=False
    )
```

```python
import functools

import jax
import jax.numpy as jnp
from jax import lax
from jax.experimental import pallas as pl
from jax.experimental.pallas import tpu as pltpu
from jax.sharding import PartitionSpec as P

D = 768
HEADS = 12
HEAD_DIM = 64
FF = 1152
HALF = D // 2
LANES = 128
PAIRS = D // LANES
QKV = 3 * D
WIDE = 2 * FF + D
PACK = WIDE + FF
FLOW = 2816
WIDE_SLOT, NARROW_SLOT, QUERY_SLOT, KEY_SLOT = 1, 5, 9, 13

epsilon = 1e-05
rope_base = 160000.0
BLOCKED = -(2.0**100)
F32 = jnp.float32
BF16 = jnp.bfloat16
MIB = 1 << 20

NN = (((1,), (0,)), ((), ()))
NT = (((1,), (1,)), ((), ()))
TN = (((0,), (0,)), ((), ()))


def mm(a, b, dims=NN):
    return lax.dot_general(a, b, dims, preferred_element_type=F32)


def vmem():
    return pl.BlockSpec(memory_space=pltpu.VMEM)


def anywhere():
    return pl.BlockSpec(memory_space=pl.ANY)


def in_hbm():
    return pl.BlockSpec(memory_space=pltpu.HBM)


def after(kernel, count, deps):
    def body(*refs):
        kernel(*refs[:count], *refs[count + len(deps) :])

    return body


def smem():
    return pl.BlockSpec(memory_space=pltpu.SMEM)


def params(mib):
    return pltpu.CompilerParams(vmem_limit_bytes=mib * MIB)


def cost(flops, nbytes):
    return pl.CostEstimate(flops=int(flops) >> 10, bytes_accessed=int(nbytes) >> 10, transcendentals=0)


def halves_in(own_ref, peer_ref, whole, sems, slot, core):
    rows = own_ref.shape[0]
    mine = pl.multiple_of(core * rows, 16)
    other = pl.multiple_of((1 - core) * rows, 16)
    return (
        pltpu.make_async_copy(own_ref, whole.at[pl.ds(mine, rows), :], sems.at[slot]),
        pltpu.make_async_copy(peer_ref, whole.at[pl.ds(other, rows), :], sems.at[slot + 1]),
    )


def lane_in_head(shape):
    return lax.broadcasted_iota(jnp.int32, shape, 1) % HEAD_DIM


def swap_halves(values):
    place = lane_in_head(values.shape)
    return jnp.where(
        place < HEAD_DIM // 2,
        pltpu.roll(values, LANES - HEAD_DIM // 2, 1),
        pltpu.roll(values, HEAD_DIM // 2, 1),
    )


def normalize(values):
    row_mean = jnp.mean(values, axis=-1, keepdims=True)
    centred = values - row_mean
    row_var = jnp.mean(centred * centred, axis=-1, keepdims=True)
    inverse = lax.rsqrt(row_var + epsilon)
    return centred * inverse, inverse


def project_kernel(core_ref, x_ref, gain_ref, own_ref, peer_ref, cos_ref, sin_ref, n_ref, q_ref, kv_ref, w_ref, sems):
    core = core_ref[0]
    copies = halves_in(own_ref, peer_ref, w_ref, sems, 0, core)
    for copy in copies:
        copy.start()
    rows = 256
    for r in range(x_ref.shape[0] // rows):
        part = pl.ds(r * rows, rows)
        hat, _ = normalize(x_ref[part, :].astype(F32))
        n_ref[part, :] = (hat * gain_ref[...]).astype(BF16)
    for copy in copies:
        copy.wait()
    scale = HEAD_DIM**-0.5
    for r in range(x_ref.shape[0] // rows):
        part = pl.ds(r * rows, rows)
        normed = n_ref[part, :]
        cosine, sine = cos_ref[part, :], sin_ref[part, :]
        for which in range(3):
            for half in range(2):
                at = which * D + half * HALF
                out = mm(normed, w_ref[:, at : at + HALF])
                for tile in range(HALF // LANES):
                    piece = out[:, tile * LANES : (tile + 1) * LANES]
                    cols = pl.ds(half * HALF + tile * LANES, LANES)
                    if which < 2:
                        piece = piece * cosine + swap_halves(piece) * sine
                    if which == 0:
                        q_ref[part, cols] = (piece * scale).astype(BF16)
                    else:
                        kv_ref[which - 1, part, cols] = piece.astype(BF16)


def project(core, x, gain, own, peer, cosine, sine):
    rows = x.shape[0]
    return pl.pallas_call(
        project_kernel,
        out_shape=(
            jax.ShapeDtypeStruct((rows, D), BF16),
            jax.ShapeDtypeStruct((rows, D), BF16),
            jax.ShapeDtypeStruct((2, rows, D), BF16),
        ),
        in_specs=[smem(), vmem(), vmem(), in_hbm(), in_hbm(), vmem(), vmem()],
        out_specs=(vmem(), vmem(), vmem()),
        scratch_shapes=[pltpu.VMEM((D, QKV), BF16), pltpu.SemaphoreType.DMA((2,))],
        compiler_params=params(20),
        cost_estimate=cost(2 * rows * D * QKV, 8 * MIB),
        name="project",
    )(core, x, gain, own, peer, cosine, sine)


def attend_kernel(q_ref, ko_ref, vo_ref, kp_ref, vp_ref, mq_ref, mk_ref, att_ref, low_ref, lse_ref):
    rows = q_ref.shape[0]
    tile = 256
    keys = jnp.concatenate([ko_ref[0], kp_ref[0]], axis=0)
    values = jnp.concatenate([vo_ref[0], vp_ref[0]], axis=0)
    key_first = lax.broadcasted_iota(jnp.int32, keys.shape, 1) < HEAD_DIM
    one = jnp.ones_like(values)
    mask_keys = mk_ref[...]
    k_both = (jnp.where(key_first, keys, mask_keys), jnp.where(key_first, mask_keys, keys))
    v_both = (jnp.where(key_first, values, one), jnp.where(key_first, one, values))
    first = lax.broadcasted_iota(jnp.int32, (tile, LANES), 1) < HEAD_DIM
    for t in range(rows // tile):
        part = pl.ds(t * tile, tile)
        query, mask_q = q_ref[part, :], mq_ref[part, :]
        sums, peaks = [], []
        for head in range(2):
            side = first if head == 0 else jnp.logical_not(first)
            scores = mm(jnp.where(side, query, mask_q), k_both[head], NT)
            peak = jnp.max(scores, axis=-1, keepdims=True)
            weights = jnp.exp(scores - peak).astype(BF16)
            sums.append(mm(weights, v_both[head]))
            peaks.append(peak)
        numer = jnp.where(first, sums[0], sums[1])
        denom = jnp.where(first, pltpu.roll(sums[0], HEAD_DIM, 1), pltpu.roll(sums[1], HEAD_DIM, 1))
        out = numer / denom
        att_ref[part, :] = out
        low_ref[part, :] = out.astype(BF16)
        lse_ref[part, :] = jnp.where(first, peaks[0], peaks[1]) + jnp.log(denom)


def kv_specs(rows):
    return [
        pl.BlockSpec((1, rows, LANES), lambda i: (0, 0, i)),
        pl.BlockSpec((1, rows, LANES), lambda i: (1, 0, i)),
    ]


def attend(query, kv_own, kv_peer, mask_q, mask_k):
    rows = query.shape[0]
    keys = mask_k.shape[0]
    pair = pl.BlockSpec((rows, LANES), lambda i: (0, i))
    whole = lambda n: pl.BlockSpec((n, LANES), lambda i: (0, 0))
    return pl.pallas_call(
        attend_kernel,
        grid=(PAIRS,),
        out_shape=(
            jax.ShapeDtypeStruct((rows, D), F32),
            jax.ShapeDtypeStruct((rows, D), BF16),
            jax.ShapeDtypeStruct((rows, D), F32),
        ),
        in_specs=[pair] + kv_specs(rows) + kv_specs(rows) + [whole(rows), whole(keys)],
        out_specs=(pair, pair, pair),
        compiler_params=params(16),
        cost_estimate=cost(16 * rows * keys * D, 8 * MIB),
        name="attend",
    )(query, kv_own, kv_own, kv_peer, kv_peer, mask_q, mask_k)


def middle_kernel(
    core_ref, x_ref, low_ref, dy_ref, gain_ref,
    oo_ref, op_ref, io_ref, ip_ref, do_ref, dp_ref,
    result_ref, n2_ref, act_ref, dl_ref, dres_ref, dproj_ref, datt_ref,
    wo_ref, wi_ref, wd_ref, sems,
):
    core = core_ref[0]
    copies = (
        halves_in(oo_ref, op_ref, wo_ref, sems, 0, core),
        halves_in(io_ref, ip_ref, wi_ref, sems, 2, core),
        halves_in(do_ref, dp_ref, wd_ref, sems, 4, core),
    )
    for pair in copies:
        for copy in pair:
            copy.start()
    for pair in copies:
        for copy in pair:
            copy.wait()
    gain = gain_ref[...]
    rows = 256
    block = 384
    for r in range(x_ref.shape[0] // rows):
        part = pl.ds(r * rows, rows)
        resid = x_ref[part, :].astype(F32) + mm(low_ref[part, :], wo_ref[...])
        hat, inverse = normalize(resid)
        n2 = (hat * gain).astype(BF16)
        n2_ref[part, :] = n2
        dy = dy_ref[part, :]
        for b in range(FF // block):
            cols = slice(b * block, (b + 1) * block)
            gate_cols = slice(FF + b * block, FF + (b + 1) * block)
            lift = mm(n2, wi_ref[:, cols])
            gate = mm(n2, wi_ref[:, gate_cols])
            d_act = mm(dy, wd_ref[cols, :], NT)
            cdf = 0.5 + 0.5 * lax.erf(lift * (0.5**0.5))
            bell = jnp.exp(-0.5 * lift * lift) * 0.3989422804014327
            gelu = lift * cdf
            act_ref[part, cols] = (gelu * gate).astype(BF16)
            dl_ref[part, cols] = (d_act * gate * (cdf + lift * bell)).astype(BF16)
            dl_ref[part, gate_cols] = (d_act * gelu).astype(BF16)
        result_ref[part, :] = (resid + mm(act_ref[part, :], wd_ref[...])).astype(BF16)
        d_normed = mm(dl_ref[part, :], wi_ref[...], NT)
        d_hat = d_normed * gain
        d_resid = dy.astype(F32) + inverse * (
            d_hat
            - jnp.mean(d_hat, axis=-1, keepdims=True)
            - hat * jnp.mean(d_hat * hat, axis=-1, keepdims=True)
        )
        dres_ref[part, :] = d_resid
        d_proj = d_resid.astype(BF16)
        dproj_ref[part, :] = d_proj
        datt_ref[part, :] = mm(d_proj, wo_ref[...], NT).astype(BF16)


def middle(core, x, low, dy, gain, w_out, w_in, w_down):
    rows = x.shape[0]
    low_shape = lambda n: jax.ShapeDtypeStruct((rows, n), BF16)
    return pl.pallas_call(
        middle_kernel,
        out_shape=(
            low_shape(D), low_shape(D), low_shape(FF), low_shape(2 * FF),
            jax.ShapeDtypeStruct((rows, D), F32), low_shape(D), low_shape(D),
        ),
        in_specs=[smem()] + [vmem()] * 4 + [in_hbm()] * 6,
        out_specs=(vmem(),) * 7,
        scratch_shapes=[
            pltpu.VMEM((D, D), BF16),
            pltpu.VMEM((D, 2 * FF), BF16),
            pltpu.VMEM((FF, D), BF16),
            pltpu.SemaphoreType.DMA((6,)),
        ],
        compiler_params=params(32),
        cost_estimate=cost(2 * rows * D * (2 * D + 6 * FF), 16 * MIB),
        name="middle",
    )(core, x, low, dy, gain, *w_out, *w_in, *w_down)


def fold_down(ref, block):
    rest = block.shape[0] - HALF
    ref[:, :D] = block[:HALF]
    ref[0:rest, D:FF] = block[HALF:, :HALF]
    ref[rest : 2 * rest, D:FF] = block[HALF:, HALF:]


def narrow_kernel(core_ref, act_ref, dy_ref, peer_ref, own_ref, whole):
    core = core_ref[0]
    for b in range(FF // 384):
        rows = slice(b * 384, (b + 1) * 384)
        whole[rows, :] = mm(act_ref[:, rows], dy_ref[...], TN).astype(BF16)
    size = FF // 2
    for ref, side in ((peer_ref, 1 - core), (own_ref, core)):
        fold_down(ref, whole[pl.ds(pl.multiple_of(side * size, 16), size), :])


def narrow_terms(core, act, dy):
    rows = act.shape[0]
    half = jax.ShapeDtypeStruct((HALF, FF), BF16)
    return pl.pallas_call(
        narrow_kernel,
        out_shape=(half, half),
        in_specs=[smem()] + [vmem()] * 2,
        out_specs=(vmem(), vmem()),
        scratch_shapes=[pltpu.VMEM((FF, D), BF16)],
        compiler_params=params(14),
        cost_estimate=cost(2 * rows * D * FF, 8 * MIB),
        name="narrow_terms",
    )(core, act, dy)


def wide_block(side, n2_ref, dl_ref, low_ref, dproj_ref, store):
    cols = pl.ds(pl.multiple_of(side * HALF, LANES), HALF)
    n2 = n2_ref[:, cols]
    for b in range(2 * FF // 384):
        at = slice(b * 384, (b + 1) * 384)
        store(at, mm(n2, dl_ref[:, at], TN))
    low = low_ref[:, cols]
    cut = FLOW - 2 * FF
    store(slice(2 * FF, FLOW), mm(low, dproj_ref[:, :cut], TN))
    store(slice(FLOW, WIDE), mm(low, dproj_ref[:, cut:], TN))


def wide_peer_kernel(core_ref, n2_ref, dl_ref, low_ref, dproj_ref, peer_ref):
    def store(at, block):
        peer_ref[:, at] = block.astype(BF16)

    wide_block(1 - core_ref[0], n2_ref, dl_ref, low_ref, dproj_ref, store)


def wide_peer(core, n2, dl, low, dproj):
    rows = n2.shape[0]
    return pl.pallas_call(
        wide_peer_kernel,
        out_shape=jax.ShapeDtypeStruct((HALF, WIDE), BF16),
        in_specs=[smem()] + [vmem()] * 4,
        out_specs=vmem(),
        compiler_params=params(14),
        cost_estimate=cost(2 * rows * HALF * WIDE, 6 * MIB),
        name="wide_peer",
    )(core, n2, dl, low, dproj)


def split_rows(bit, block, at, keep_ref, send_ref):
    rows = block.shape[0] // 2
    keep_ref[:, at] = jnp.where(bit == 0, block[:rows], block[rows:]).astype(BF16)
    send_ref[:, at] = jnp.where(bit == 0, block[rows:], block[:rows]).astype(BF16)


def first_kernel(
    place_ref, n2_ref, dl_ref, low_ref, dproj_ref, got_ref, down_ref, down_got_ref,
    keep_ref, send_ref, narrow_keep, narrow_send,
):
    def store(at, block):
        block = block + got_ref[:, at].astype(F32)
        if at.start < FLOW:
            split_rows(place_ref[WIDE_SLOT], block, at, keep_ref, send_ref)
        else:
            split_rows(place_ref[NARROW_SLOT], block, slice(0, WIDE - FLOW), narrow_keep, narrow_send)

    wide_block(place_ref[0], n2_ref, dl_ref, low_ref, dproj_ref, store)
    total = down_ref[...].astype(F32) + down_got_ref[...].astype(F32)
    split_rows(place_ref[NARROW_SLOT], total, slice(WIDE - FLOW, PACK - FLOW), narrow_keep, narrow_send)


def first_sums(place, n2, dl, low, dproj, got, down, down_got, deps):
    rows = n2.shape[0]
    half = jax.ShapeDtypeStruct((HALF // 2, FLOW), BF16)
    narrow = jax.ShapeDtypeStruct((HALF // 2, PACK - FLOW), BF16)
    return pl.pallas_call(
        after(first_kernel, 8, deps),
        out_shape=(half, half, narrow, narrow),
        in_specs=[smem()] + [vmem()] * 7 + [anywhere()] * len(deps),
        out_specs=(vmem(),) * 4,
        compiler_params=params(16),
        cost_estimate=cost(2 * rows * HALF * WIDE, 8 * MIB),
        name="first_sums",
    )(place, n2, dl, low, dproj, got, down, down_got, *deps)


def split_three(values):
    high = values.astype(BF16)
    rest = values - high.astype(F32)
    mid = rest.astype(BF16)
    return high, mid, (rest - mid.astype(F32)).astype(BF16)


def place_three(values, place, others):
    high, mid, tail = split_three(-values)
    at = HEAD_DIM // 2
    out = jnp.where(place == at, high.astype(F32), others)
    out = jnp.where(place == at + 1, mid.astype(F32), out)
    return jnp.where(place == at + 2, tail.astype(F32), out)


def attend_back_kernel(
    q_ref, ko_ref, vo_ref, kp_ref, vp_ref, mq_ref, mk_ref, do_ref, att_ref, lse_ref, cos_ref, sin_ref,
    dq_ref, own_ref, peer_ref,
):
    rows = q_ref.shape[0]
    tile = 256
    query, grad = q_ref[...], do_ref[...]
    place = lane_in_head(query.shape)
    first = lax.broadcasted_iota(jnp.int32, query.shape, 1) < HEAD_DIM
    tile_first = first[:tile]
    product = grad.astype(F32) * att_ref[...]
    lse = pltpu.roll(lse_ref[...], HEAD_DIM, 1)
    mask_q = mq_ref[...].astype(F32)
    zero = jnp.zeros_like(mask_q)
    q_both, g_both = [], []
    for head in range(2):
        side = first if head == 0 else jnp.logical_not(first)
        delta = jnp.sum(jnp.where(side, product, 0.0), axis=-1, keepdims=True)
        q_both.append(jnp.where(side, query, place_three(lse, place, mask_q).astype(BF16)))
        wide = jnp.broadcast_to(delta, product.shape)
        g_both.append(jnp.where(side, grad, place_three(wide, place, zero).astype(BF16)))
    d_query = [jnp.zeros((rows, LANES), F32) for _ in range(2)]
    for source in range(2):
        k_ref, v_ref, out_ref = ((ko_ref, vo_ref, own_ref), (kp_ref, vp_ref, peer_ref))[source]
        for t in range(rows // tile):
            part = pl.ds(t * tile, tile)
            keys, values = k_ref[0, part, :], v_ref[0, part, :]
            marks = mk_ref[pl.ds(source * rows + t * tile, tile), :]
            d_keys, d_values = [], []
            for head in range(2):
                side = tile_first if head == 0 else jnp.logical_not(tile_first)
                probs = jnp.exp(mm(jnp.where(side, keys, marks), q_both[head], NT))
                d_probs = mm(jnp.where(side, values, marks), g_both[head], NT)
                d_scores = (probs * d_probs).astype(BF16)
                d_values.append(mm(probs.astype(BF16), grad))
                d_keys.append(mm(d_scores, query))
                d_query[head] = d_query[head] + mm(d_scores, keys, TN)
            out_ref[0, part, :] = jnp.where(tile_first, d_keys[0], d_keys[1]).astype(BF16)
            out_ref[1, part, :] = jnp.where(tile_first, d_values[0], d_values[1]).astype(BF16)
    d_q = jnp.where(first, d_query[0], d_query[1]) * HEAD_DIM**-0.5
    dq_ref[...] = (d_q * cos_ref[...] - swap_halves(d_q) * sin_ref[...]).astype(BF16)


def attend_back(first, count, so_far, deps, query, kv_own, kv_peer, mask_q, mask_k, grad, att, lse, cosine, sine):
    rows = query.shape[0]
    keys = mask_k.shape[0]
    pair = pl.BlockSpec((rows, LANES), lambda i: (0, first + i))
    both = pl.BlockSpec((2, rows, LANES), lambda i: (0, 0, first + i))
    whole = lambda n: pl.BlockSpec((n, LANES), lambda i: (0, 0))
    kv = [
        pl.BlockSpec((1, rows, LANES), lambda i: (0, 0, first + i)),
        pl.BlockSpec((1, rows, LANES), lambda i: (1, 0, first + i)),
    ]
    extra = tuple(so_far) + tuple(deps)
    return pl.pallas_call(
        after(attend_back_kernel, 12, extra),
        grid=(count,),
        out_shape=(
            jax.ShapeDtypeStruct((rows, D), BF16),
            jax.ShapeDtypeStruct((2, rows, D), BF16),
            jax.ShapeDtypeStruct((2, rows, D), BF16),
        ),
        in_specs=[pair] + kv + kv
        + [whole(rows), whole(keys), pair, pair, pair, whole(rows), whole(rows)]
        + [anywhere()] * len(extra),
        out_specs=(pair, both, both),
        input_output_aliases={12 + i: i for i in range(len(so_far))},
        compiler_params=params(18),
        cost_estimate=cost(40 * rows * keys * LANES * count, 2 * MIB * count),
        name="attend_back",
    )(query, kv_own, kv_own, kv_peer, kv_peer, mask_q, mask_k, grad, att, lse, cosine, sine, *extra)


def query_terms_kernel(core_ref, n1_ref, dq_ref, peer_ref, own_ref):
    for ref, side in ((peer_ref, 1 - core_ref[0]), (own_ref, core_ref[0])):
        cols = pl.ds(pl.multiple_of(side * HALF, LANES), HALF)
        ref[...] = mm(n1_ref[:, cols], dq_ref[...], TN).astype(BF16)


def query_terms(core, n1, dq, deps):
    rows = n1.shape[0]
    half = jax.ShapeDtypeStruct((HALF, D), BF16)
    return pl.pallas_call(
        after(query_terms_kernel, 3, deps),
        out_shape=(half, half),
        in_specs=[smem()] + [vmem()] * 2 + [anywhere()] * len(deps),
        out_specs=(vmem(), vmem()),
        compiler_params=params(12),
        cost_estimate=cost(2 * rows * D * D, 3 * MIB),
        name="query_terms",
    )(core, n1, dq, *deps)


def key_terms_kernel(core_ref, n1_ref, own_ref, got_ref, cos_ref, sin_ref, peer_ref, dkv_ref):
    cosine, sine = cos_ref[...], sin_ref[...]
    cols = pl.ds(pl.multiple_of((1 - core_ref[0]) * HALF, LANES), HALF)
    n1 = n1_ref[:, cols]
    for pair in range(PAIRS):
        at = slice(pair * LANES, (pair + 1) * LANES)
        d_key = own_ref[0, :, at].astype(F32) + got_ref[0, :, at].astype(F32)
        d_value = own_ref[1, :, at].astype(F32) + got_ref[1, :, at].astype(F32)
        d_key = d_key * cosine - swap_halves(d_key) * sine
        dkv_ref[:, at] = d_key.astype(BF16)
        dkv_ref[:, D + pair * LANES : D + (pair + 1) * LANES] = d_value.astype(BF16)
    for b in range(2 * D // 384):
        at = slice(b * 384, (b + 1) * 384)
        peer_ref[:, at] = mm(n1, dkv_ref[:, at], TN).astype(BF16)


def key_terms(core, n1, own, got, cosine, sine, deps):
    rows = n1.shape[0]
    return pl.pallas_call(
        after(key_terms_kernel, 6, deps),
        out_shape=(jax.ShapeDtypeStruct((HALF, 2 * D), BF16), jax.ShapeDtypeStruct((rows, 2 * D), BF16)),
        in_specs=[smem()] + [vmem()] * 5 + [anywhere()] * len(deps),
        out_specs=(vmem(), vmem()),
        compiler_params=params(16),
        cost_estimate=cost(2 * rows * D * D, 6 * MIB),
        name="key_terms",
    )(core, n1, own, got, cosine, sine, *deps)


def key_own_kernel(place_ref, n1_ref, dkv_ref, got_ref, q_own_ref, q_got_ref, q_keep, q_send, kv_keep, kv_send):
    total = q_own_ref[...].astype(F32) + q_got_ref[...].astype(F32)
    split_rows(place_ref[QUERY_SLOT], total, slice(0, D), q_keep, q_send)
    n1 = n1_ref[:, pl.ds(pl.multiple_of(place_ref[0] * HALF, LANES), HALF)]
    for b in range(2 * D // 384):
        at = slice(b * 384, (b + 1) * 384)
        block = mm(n1, dkv_ref[:, at], TN) + got_ref[:, at].astype(F32)
        split_rows(place_ref[KEY_SLOT], block, at, kv_keep, kv_send)


def key_own(place, n1, dkv, got, q_own, q_got, deps):
    rows = n1.shape[0]
    part = jax.ShapeDtypeStruct((HALF // 2, D), BF16)
    both = jax.ShapeDtypeStruct((HALF // 2, 2 * D), BF16)
    return pl.pallas_call(
        after(key_own_kernel, 6, deps),
        out_shape=(part, part, both, both),
        in_specs=[smem()] + [vmem()] * 5 + [anywhere()] * len(deps),
        out_specs=(vmem(),) * 4,
        compiler_params=params(14),
        cost_estimate=cost(2 * rows * D * D, 6 * MIB),
        name="key_own",
    )(place, n1, dkv, got, q_own, q_got, *deps)


def input_kernel(
    core_ref, x_ref, gain_ref, dq_ref, dkv_ref, own_ref, peer_ref, dres_ref, dx_ref, w_ref, sems
):
    copies = halves_in(own_ref, peer_ref, w_ref, sems, 0, core_ref[0])
    for copy in copies:
        copy.start()
    for copy in copies:
        copy.wait()
    gain = gain_ref[...]
    rows = 256
    for r in range(x_ref.shape[0] // rows):
        part = pl.ds(r * rows, rows)
        hat, inverse = normalize(x_ref[part, :].astype(F32))
        d_normed = mm(dq_ref[part, :], w_ref[:, :D], NT) + mm(dkv_ref[part, :], w_ref[:, D:], NT)
        d_hat = d_normed * gain
        back = inverse * (
            d_hat
            - jnp.mean(d_hat, axis=-1, keepdims=True)
            - hat * jnp.mean(d_hat * hat, axis=-1, keepdims=True)
        )
        dx_ref[part, :] = (dres_ref[part, :] + back).astype(BF16)


def input_grad(core, x, gain, dq, dkv, own, peer, dres, deps):
    rows = x.shape[0]
    return pl.pallas_call(
        after(input_kernel, 8, deps),
        out_shape=jax.ShapeDtypeStruct((rows, D), BF16),
        in_specs=[smem()] + [vmem()] * 4 + [in_hbm()] * 2 + [vmem()] + [anywhere()] * len(deps),
        out_specs=vmem(),
        scratch_shapes=[pltpu.VMEM((D, QKV), BF16), pltpu.SemaphoreType.DMA((2,))],
        compiler_params=params(16),
        cost_estimate=cost(2 * rows * D * QKV, 10 * MIB),
        name="input_grad",
    )(core, x, gain, dq, dkv, own, peer, dres, *deps)


BITS = {"x": 1, "y": 2, "n": 4, "f": 8}
WIDE_ORDER = ("xy", "yx", "nf", "fn")
NARROW_ORDER = ("nf", "fn", "xy", "yx")
KEY_ORDER = ("xy", "yx", "nf", "fn")
QUERY_ORDER = ("nf", "fn", "xy", "yx")
ALL_ORDERS = WIDE_ORDER + NARROW_ORDER + QUERY_ORDER + KEY_ORDER


def trade(values, axes):
    pairs = []
    for group in range(16):
        for core in range(2):
            pairs.append((2 * group + core, 2 * (group ^ BITS[axes[core]]) + core))
    return lax.ppermute(values, ("rep", "fsdp"), pairs)


def bit_of(axes):
    step = jnp.where(lax.axis_index("fsdp") == 0, BITS[axes[0]], BITS[axes[1]])
    return (lax.axis_index("rep") // step) % 2


def advance_kernel(plan, place_ref, *refs):
    ins, outs = refs[: 2 * len(plan)], list(refs[2 * len(plan) :])
    for i, (mode, slot) in enumerate(plan):
        kept, got = ins[2 * i][...].astype(F32), ins[2 * i + 1][...].astype(F32)
        if mode == "split":
            split_rows(place_ref[slot], kept + got, slice(0, kept.shape[1]), outs.pop(0), outs.pop(0))
        elif mode == "add":
            outs.pop(0)[...] = (kept + got).astype(BF16)
        else:
            bit = place_ref[slot]
            both = [jnp.where(bit == 0, kept, got), jnp.where(bit == 0, got, kept)]
            outs.pop(0)[...] = jnp.concatenate(both, axis=0).astype(BF16)


def advance(place, flows, deps, carried):
    plan, arrays, shapes = [], [], []
    for mode, slot, kept, got in flows:
        rows, cols = kept.shape
        plan.append((mode, slot))
        arrays += [kept, got]
        sizes = {"split": [rows // 2, rows // 2], "add": [rows], "join": [2 * rows]}[mode]
        shapes += [jax.ShapeDtypeStruct((size, cols), BF16) for size in sizes]
    count, made = 1 + len(arrays), len(shapes)
    extra = tuple(carried) + tuple(deps)
    kernel = functools.partial(advance_kernel, plan)

    def body(*refs):
        outs = refs[count + len(extra) :]
        kernel(*refs[:count], *outs[:made])

    outs = pl.pallas_call(
        body,
        out_shape=tuple(shapes) + tuple(jax.ShapeDtypeStruct(a.shape, a.dtype) for a in carried),
        in_specs=[smem()] + [vmem()] * len(arrays) + [anywhere()] * len(extra),
        out_specs=(vmem(),) * made + (anywhere(),) * len(carried),
        input_output_aliases={count + i: made + i for i in range(len(carried))},
        compiler_params=params(12),
        cost_estimate=cost(MIB, 2 * MIB),
        name="advance",
    )(place, *arrays, *extra)
    return outs[:made], outs[made:]


class Chain:
    def __init__(self, place, flows):
        self.place, self.step = place, 0
        self.orders = [order for order, *_ in flows]
        self.slots = [slot for _, slot, *_ in flows]
        self.kept = [kept for *_, kept, _ in flows]
        self.exchange([send for *_, send in flows])

    def exchange(self, sends):
        axis = self.step if self.step < 4 else 7 - self.step
        self.sent = tuple(sends)
        self.got = [trade(send, order[axis]) for send, order in zip(sends, self.orders)]

    def flows(self):
        modes = [("split", self.step + 1), ("add", 0), ("join", 7 - self.step)]
        mode, bit = modes[(self.step >= 3) + (self.step > 3)]
        return [(mode, slot + bit, *pair) for slot, *pair in zip(self.slots, self.kept, self.got)]

    def take(self, parts):
        if self.step < 3:
            self.kept, sends = parts[0::2], parts[1::2]
        else:
            self.kept = sends = parts
        self.step += 1
        self.exchange(sends)

    def advance(self, deps, carried=()):
        parts, carried = advance(self.place, self.flows(), deps, carried)
        self.take(parts)
        return carried


def advance_both(one, two):
    flows = one.flows()
    parts, _ = advance(one.place, flows + two.flows(), (), ())
    count = sum(2 if mode == "split" else 1 for mode, *_ in flows)
    one.take(parts[:count])
    two.take(parts[count:])


def weighted_sum(total, weight):
    sums = jnp.sum(total * weight.astype(F32), axis=-1, keepdims=True)
    return jnp.broadcast_to(sums, (total.shape[0], LANES))


def finish_mlp_kernel(
    place_ref, mine, theirs, narrow_mine, narrow_theirs, weight_ref, in_ref, out_ref, down_ref, sum_ref
):
    rows = HALF // 2
    rest = FF // 2 - HALF
    cut = FLOW - 2 * FF
    down = WIDE - FLOW
    bit, narrow_bit = place_ref[WIDE_SLOT], place_ref[NARROW_SLOT]
    for half in range(2):
        at = slice(half * rows, (half + 1) * rows)

        def pick(start, stop):
            cols = slice(start, stop)
            return jnp.where(bit == half, mine[:, cols].astype(F32), theirs[:, cols].astype(F32))

        def pick_narrow(start, stop):
            cols = slice(start, stop)
            return jnp.where(
                narrow_bit == half, narrow_mine[:, cols].astype(F32), narrow_theirs[:, cols].astype(F32)
            )

        total = pick(0, 2 * FF)
        in_ref[at, :] = total
        sum_ref[at, :] = weighted_sum(total, weight_ref[at, :])
        out_ref[at, :cut] = pick(2 * FF, FLOW)
        out_ref[at, cut:] = pick_narrow(0, down)
        down_ref[at, :] = pick_narrow(down, down + D)
        down_ref[HALF : HALF + rest, half * HALF : (half + 1) * HALF] = pick_narrow(down + D, down + FF)


def mlp_outputs():
    return (
        jax.ShapeDtypeStruct((HALF, 2 * FF), F32),
        jax.ShapeDtypeStruct((HALF, D), F32),
        jax.ShapeDtypeStruct((FF // 2, D), F32),
        jax.ShapeDtypeStruct((HALF, LANES), F32),
    )


def finish_mlp(place, mine, theirs, narrow_mine, narrow_theirs, weight, deps):
    return pl.pallas_call(
        after(finish_mlp_kernel, 6, deps),
        out_shape=mlp_outputs(),
        in_specs=[smem()] + [vmem()] * 5 + [anywhere()] * len(deps),
        out_specs=(vmem(),) * 4,
        compiler_params=params(20),
        cost_estimate=cost(MIB, 10 * MIB),
        name="finish_mlp",
    )(place, mine, theirs, narrow_mine, narrow_theirs, weight, *deps)


def finish_qkv_kernel(place_ref, q_ref, q_got, kv_ref, kv_got, weight_ref, out_ref, sum_ref):
    step = out_ref.shape[0]
    half = pl.program_id(0) * step // (HALF // 2)
    at = pl.ds(pl.multiple_of(pl.program_id(0) * step - half * (HALF // 2), step), step)
    sums = jnp.zeros((step, LANES), F32)
    for slot, mine, theirs, start in ((QUERY_SLOT, q_ref, q_got, 0), (KEY_SLOT, kv_ref, kv_got, D)):
        cols = slice(start, start + mine.shape[1])
        total = jnp.where(place_ref[slot] == half, mine[at, :].astype(F32), theirs[at, :].astype(F32))
        out_ref[:, cols] = total
        sums = sums + weighted_sum(total, weight_ref[:, cols])
    sum_ref[...] = sums


def finish_qkv(place, q_mine, q_theirs, kv_mine, kv_theirs, weight, deps):
    step = 96
    whole = lambda array: pl.BlockSpec(array.shape, lambda i: (0, 0))
    arrays = (q_mine, q_theirs, kv_mine, kv_theirs)
    return pl.pallas_call(
        after(finish_qkv_kernel, 6, deps),
        grid=(HALF // step,),
        out_shape=(jax.ShapeDtypeStruct((HALF, QKV), F32), jax.ShapeDtypeStruct((HALF, LANES), F32)),
        in_specs=[smem()] + [whole(array) for array in arrays] + [pl.BlockSpec((step, QKV), lambda i: (i, 0))]
        + [anywhere()] * len(deps),
        out_specs=(
            pl.BlockSpec((step, QKV), lambda i: (i, 0)),
            pl.BlockSpec((step, LANES), lambda i: (i, 0)),
        ),
        compiler_params=params(14),
        cost_estimate=cost(MIB, 7 * MIB),
        name="finish_qkv",
    )(place, *arrays, weight, *deps)


def swap_cores(values):
    return lax.ppermute(values, "fsdp", [(0, 1), (1, 0)])


def layout(lengths, slot_count):
    slots = jnp.arange(slot_count, dtype=jnp.int32)
    ends = jnp.cumsum(lengths)
    segment = jnp.sum((slots[:, None] >= ends[None, :]).astype(jnp.int32), axis=1)
    begins = jnp.max(jnp.where(ends[None, :] <= slots[:, None], ends[None, :], 0), axis=1)
    return (segment, slots - begins)


def on_device(
    tokens, attn_gain, qkv_weight, out_weight, mlp_gain, in_weight, down_weight, seq_len, cotangent
):
    row_count = tokens.shape[0]
    core = lax.axis_index("fsdp")
    paired = lax.axis_size("rep") == 16
    bits = [bit_of(axes) if paired else 0 * core for axes in ALL_ORDERS]
    place = jnp.stack([core] + bits).astype(jnp.int32)
    both_gains = jnp.stack([attn_gain, mlp_gain])
    peer_qkv = swap_cores(qkv_weight)
    peer_gains = swap_cores(both_gains)
    peer_out = swap_cores(out_weight)
    peer_in = swap_cores(in_weight)
    peer_down = swap_cores(down_weight)
    gains = jnp.where(
        core == 0,
        jnp.concatenate([both_gains, peer_gains], axis=1),
        jnp.concatenate([peer_gains, both_gains], axis=1),
    ).astype(F32)
    gain_one, gain_two = gains[0:1], gains[1:2]

    key_seg, key_pos = layout(seq_len[0], 2 * row_count)
    own_seg = lax.dynamic_slice_in_dim(key_seg, core * row_count, row_count)
    peer_seg = lax.dynamic_slice_in_dim(key_seg, (1 - core) * row_count, row_count)
    own_pos = lax.dynamic_slice_in_dim(key_pos, core * row_count, row_count)
    lane = jnp.arange(LANES, dtype=jnp.int32) % HEAD_DIM
    half_dim = HEAD_DIM // 2
    freq = jnp.exp(-jnp.log(rope_base) * (2.0 * (lane % half_dim).astype(F32) / HEAD_DIM))
    angles = own_pos.astype(F32)[:, None] * freq[None, :]
    cosine = jnp.cos(angles)
    sine = jnp.sin(angles) * jnp.where(lane < half_dim, -1.0, 1.0)[None, :]
    marks = lane < half_dim
    mask_q = jnp.where(marks[None, :] & (own_seg[:, None] != lane[None, :]), BLOCKED, 0.0).astype(BF16)
    both_seg = jnp.concatenate([own_seg, peer_seg])
    mask_k = jnp.where(
        marks[None, :], both_seg[:, None] == lane[None, :], (lane < half_dim + 3)[None, :]
    ).astype(BF16)

    n1, query, kv_own = project(place, tokens, gain_one, qkv_weight, peer_qkv, cosine, sine)
    kv_peer = swap_cores(kv_own)
    att, low, lse = attend(query, kv_own, kv_peer, mask_q, mask_k)
    result, n2, act, dl, dres, dproj, datt = middle(
        place, tokens, low, cotangent, gain_two,
        (out_weight, peer_out), (in_weight, peer_in), (down_weight, peer_down),
    )
    wide_for_peer = wide_peer(place, n2, dl, low, dproj)
    wide_got = swap_cores(wide_for_peer)
    narrow_for_peer, narrow_own = narrow_terms(place, act, cotangent)
    narrow_got = swap_cores(narrow_for_peer)
    back_args = (query, kv_own, kv_peer, mask_q, mask_k, datt, att, lse, cosine, sine)
    grads = attend_back(0, 1, (), (wide_for_peer, narrow_own), *back_args)
    wide_keep, wide_send, narrow_keep, narrow_send = first_sums(place, n2, dl, low, dproj, wide_got, narrow_own, narrow_got, grads[:1])

    def input_part(deps):
        return input_grad(place, tokens, gain_one, dq, dkv, qkv_weight, peer_qkv, dres, deps)

    if paired:
        mlp = Chain(
            place,
            [
                (WIDE_ORDER, WIDE_SLOT, wide_keep, wide_send),
                (NARROW_ORDER, NARROW_SLOT, narrow_keep, narrow_send),
            ],
        )
        grads = attend_back(1, 3, grads, mlp.sent, *back_args)
        mlp.advance(grads[:1])
        dq, dkv_own, dkv_peer = attend_back(4, 2, grads, mlp.sent, *back_args)
        (dkv_peer,) = mlp.advance((dq,), (dkv_peer,))
        dkv_got = swap_cores(dkv_peer)
        query_for_peer, query_own = query_terms(place, n1, dq, mlp.sent)
        key_for_peer, dkv = key_terms(place, n1, dkv_own, dkv_got, cosine, sine, (query_own,))
        query_for_peer, key_for_peer = mlp.advance((dkv,), (query_for_peer, key_for_peer))
        key_got, query_got = swap_cores(key_for_peer), swap_cores(query_for_peer)
        grad_tokens = input_part(mlp.sent)
        mlp.advance((grad_tokens,))
        q_keep, q_send, kv_keep, kv_send = key_own(
            place, n1, dkv, key_got, query_own, query_got, mlp.sent
        )
        qkv = Chain(
            place,
            [(KEY_ORDER, KEY_SLOT, kv_keep, kv_send), (QUERY_ORDER, QUERY_SLOT, q_keep, q_send)],
        )
        for _ in range(3):
            advance_both(qkv, mlp)
        for step in range(4):
            qkv.advance(mlp.got[1:] if step == 1 else ())
        grad_in, grad_out, grad_down, in_sums = finish_mlp(
            place, mlp.kept[0], mlp.got[0], mlp.kept[1], mlp.got[1], in_weight, qkv.sent
        )
        grad_qkv, qkv_sums = finish_qkv(
            place, qkv.kept[1], qkv.got[1], qkv.kept[0], qkv.got[0], qkv_weight, (in_sums,)
        )
    else:
        grads = attend_back(1, PAIRS - 1, grads, (), *back_args)
        dq, dkv_own, dkv_peer = grads
        query_for_peer, query_own = query_terms(place, n1, dq, ())
        key_for_peer, dkv = key_terms(place, n1, dkv_own, swap_cores(dkv_peer), cosine, sine, ())
        query_got, key_got = swap_cores(query_for_peer), swap_cores(key_for_peer)
        parts = key_own(place, n1, dkv, key_got, query_own, query_got, ())
        grad_tokens = input_part(())
        total = lambda values: lax.psum(values.astype(F32), "rep")
        grad_qkv, qkv_sums = finish_qkv(place, *[total(part) for part in parts], qkv_weight, ())
        grad_in, grad_out, grad_down, in_sums = finish_mlp(
            place, *[total(part) for part in (wide_keep, wide_send, narrow_keep, narrow_send)], in_weight, ()
        )
    grad_gain_one = qkv_sums[:, 0] / attn_gain.astype(F32)
    grad_gain_two = in_sums[:, 0] / mlp_gain.astype(F32)
    return (
        result,
        grad_tokens,
        grad_gain_one,
        grad_qkv,
        grad_out,
        grad_gain_two,
        grad_in,
        grad_down,
    )


def solution(mesh):
    rows = P(("rep", "fsdp"), None)
    vector, matrix = P("fsdp"), P("fsdp", None)
    in_specs = (rows, vector, matrix, matrix, vector, matrix, matrix, P("rep", None), rows)
    out_specs = (rows, rows, vector, matrix, matrix, vector, matrix, matrix)
    return jax.shard_map(
        on_device, mesh=mesh, in_specs=in_specs, out_specs=out_specs, check_vma=False
    )
```

```python
import functools

import jax
import jax.numpy as jnp
from jax import lax
from jax.experimental import pallas as pl
from jax.experimental.pallas import tpu as pltpu
from jax.sharding import PartitionSpec as P

D = 768
HEADS = 12
HEAD_DIM = 64
FF = 1152
HALF = D // 2
LANES = 128
PAIRS = D // LANES
QKV = 3 * D
WIDE = 2 * FF + D
PACK = WIDE + FF
FLOW = 3200
WIDE_SLOT, NARROW_SLOT, QUERY_SLOT, KEY_SLOT = 1, 5, 9, 13

epsilon = 1e-05
rope_base = 160000.0
BLOCKED = -(2.0**100)
F32 = jnp.float32
BF16 = jnp.bfloat16
MIB = 1 << 20

NN = (((1,), (0,)), ((), ()))
NT = (((1,), (1,)), ((), ()))
TN = (((0,), (0,)), ((), ()))


def mm(a, b, dims=NN):
    return lax.dot_general(a, b, dims, preferred_element_type=F32)


def vmem():
    return pl.BlockSpec(memory_space=pltpu.VMEM)


def anywhere():
    return pl.BlockSpec(memory_space=pl.ANY)


def in_hbm():
    return pl.BlockSpec(memory_space=pltpu.HBM)


def after(kernel, count, deps):
    def body(*refs):
        kernel(*refs[:count], *refs[count + len(deps) :])

    return body


def smem():
    return pl.BlockSpec(memory_space=pltpu.SMEM)


def params(mib):
    return pltpu.CompilerParams(vmem_limit_bytes=mib * MIB)


def cost(flops, nbytes):
    return pl.CostEstimate(flops=int(flops) >> 10, bytes_accessed=int(nbytes) >> 10, transcendentals=0)


def halves_in(own_ref, peer_ref, whole, sems, slot, core):
    rows = own_ref.shape[0]
    mine = pl.multiple_of(core * rows, 16)
    other = pl.multiple_of((1 - core) * rows, 16)
    return (
        pltpu.make_async_copy(own_ref, whole.at[pl.ds(mine, rows), :], sems.at[slot]),
        pltpu.make_async_copy(peer_ref, whole.at[pl.ds(other, rows), :], sems.at[slot + 1]),
    )


def lane_in_head(shape):
    return lax.broadcasted_iota(jnp.int32, shape, 1) % HEAD_DIM


def swap_halves(values):
    place = lane_in_head(values.shape)
    return jnp.where(
        place < HEAD_DIM // 2,
        pltpu.roll(values, LANES - HEAD_DIM // 2, 1),
        pltpu.roll(values, HEAD_DIM // 2, 1),
    )


def normalize(values):
    row_mean = jnp.mean(values, axis=-1, keepdims=True)
    centred = values - row_mean
    row_var = jnp.mean(centred * centred, axis=-1, keepdims=True)
    inverse = lax.rsqrt(row_var + epsilon)
    return centred * inverse, inverse


def whole_gain(place_ref, own_ref, peer_ref):
    own, peer = own_ref[...].astype(F32), peer_ref[...].astype(F32)
    first = place_ref[0] == 0
    return jnp.concatenate([jnp.where(first, own, peer), jnp.where(first, peer, own)], axis=1)


def norm_kernel(place_ref, x_ref, own_ref, peer_ref, n_ref):
    hat, _ = normalize(x_ref[...].astype(F32))
    n_ref[...] = (hat * whole_gain(place_ref, own_ref, peer_ref)).astype(BF16)


def first_norm(place, x, gain):
    rows = 128
    block = pl.BlockSpec((rows, D), lambda i: (i, 0))
    return pl.pallas_call(
        norm_kernel,
        grid=(x.shape[0] // rows,),
        out_shape=jax.ShapeDtypeStruct(x.shape, BF16),
        in_specs=[smem(), block] + [pl.BlockSpec((1, HALF), lambda i: (0, 0))] * 2,
        out_specs=block,
        compiler_params=params(8),
        cost_estimate=cost(MIB, 2 * MIB),
        name="first_norm",
    )(place, x, *gain)


def project_kernel(parts, scale, place_ref, n_ref, own_ref, peer_ref, cos_ref, sin_ref, out_ref):
    core = place_ref[0]
    mine = pl.ds(pl.multiple_of(core * HALF, LANES), HALF)
    other = pl.ds(pl.multiple_of((1 - core) * HALF, LANES), HALF)
    rows = 256
    for r in range(n_ref.shape[0] // rows):
        part = pl.ds(r * rows, rows)
        left, right = n_ref[part, mine], n_ref[part, other]
        cosine, sine = cos_ref[part, :], sin_ref[part, :]
        for i, which in enumerate(parts):
            for half in range(2):
                at = slice(which * D + half * HALF, which * D + (half + 1) * HALF)
                out = mm(left, own_ref[:, at]) + mm(right, peer_ref[:, at])
                for tile in range(HALF // LANES):
                    piece = out[:, tile * LANES : (tile + 1) * LANES]
                    if which < 2:
                        piece = piece * cosine + swap_halves(piece) * sine
                    cols = pl.ds(half * HALF + tile * LANES, LANES)
                    out_ref[i, part, cols] = (piece * scale).astype(BF16)


def project(parts, scale, place, normed, own, peer, cosine, sine, deps):
    rows = normed.shape[0]
    return pl.pallas_call(
        after(functools.partial(project_kernel, parts, scale), 6, deps),
        out_shape=jax.ShapeDtypeStruct((len(parts), rows, D), BF16),
        in_specs=[smem()] + [vmem()] * 5 + [anywhere()] * len(deps),
        out_specs=vmem(),
        compiler_params=params(12),
        cost_estimate=cost(2 * rows * D * D * len(parts), 8 * MIB),
        name="project",
    )(place, normed, own, peer, cosine, sine, *deps)


def attend_kernel(q_ref, ko_ref, vo_ref, kp_ref, vp_ref, mq_ref, mk_ref, att_ref, low_ref, lse_ref):
    rows = q_ref.shape[0]
    tile = min(512, rows)
    keys = jnp.concatenate([ko_ref[0], kp_ref[0]], axis=0)
    values = jnp.concatenate([vo_ref[0], vp_ref[0]], axis=0)
    key_first = lax.broadcasted_iota(jnp.int32, keys.shape, 1) < HEAD_DIM
    one = jnp.ones_like(values)
    mask_keys = mk_ref[...]
    k_both = (jnp.where(key_first, keys, mask_keys), jnp.where(key_first, mask_keys, keys))
    v_both = (jnp.where(key_first, values, one), jnp.where(key_first, one, values))
    first = lax.broadcasted_iota(jnp.int32, (tile, LANES), 1) < HEAD_DIM
    for t in range(rows // tile):
        part = pl.ds(t * tile, tile)
        query, mask_q = q_ref[part, :], mq_ref[part, :]
        sums, peaks = [], []
        for head in range(2):
            side = first if head == 0 else jnp.logical_not(first)
            scores = mm(jnp.where(side, query, mask_q), k_both[head], NT)
            peak = jnp.max(scores, axis=-1, keepdims=True)
            weights = jnp.exp(scores - peak).astype(BF16)
            sums.append(mm(weights, v_both[head]))
            peaks.append(peak)
        numer = jnp.where(first, sums[0], sums[1])
        denom = jnp.where(first, pltpu.roll(sums[0], HEAD_DIM, 1), pltpu.roll(sums[1], HEAD_DIM, 1))
        out = numer / denom
        att_ref[part, :] = out
        low_ref[part, :] = out.astype(BF16)
        lse_ref[part, :] = jnp.where(first, peaks[0], peaks[1]) + jnp.log(denom)


def kv_specs(rows):
    return [
        pl.BlockSpec((1, rows, LANES), lambda i: (0, 0, i)),
        pl.BlockSpec((1, rows, LANES), lambda i: (1, 0, i)),
    ]


def attend(query, kv_own, kv_peer, mask_q, mask_k):
    rows = query.shape[0]
    keys = mask_k.shape[0]
    pair = pl.BlockSpec((rows, LANES), lambda i: (0, i))
    whole = lambda n: pl.BlockSpec((n, LANES), lambda i: (0, 0))
    return pl.pallas_call(
        attend_kernel,
        grid=(PAIRS,),
        out_shape=(
            jax.ShapeDtypeStruct((rows, D), F32),
            jax.ShapeDtypeStruct((rows, D), BF16),
            jax.ShapeDtypeStruct((rows, D), F32),
        ),
        in_specs=[pair] + kv_specs(rows) + kv_specs(rows) + [whole(rows), whole(keys)],
        out_specs=(pair, pair, pair),
        compiler_params=params(16),
        cost_estimate=cost(16 * rows * keys * D, 8 * MIB),
        name="attend",
    )(query, kv_own, kv_own, kv_peer, kv_peer, mask_q, mask_k)


def middle_kernel(
    core_ref, x_ref, low_ref, dy_ref, gain_ref, gain_peer_ref,
    oo_ref, op_ref, io_ref, ip_ref, do_ref, dp_ref,
    result_ref, n2_ref, act_ref, dl_ref, dres_ref, dproj_ref, datt_ref,
    wo_ref, wi_ref, wd_ref, sems,
):
    core = core_ref[0]
    copies = (
        halves_in(oo_ref, op_ref, wo_ref, sems, 0, core),
        halves_in(io_ref, ip_ref, wi_ref, sems, 2, core),
        halves_in(do_ref, dp_ref, wd_ref, sems, 4, core),
    )
    for pair in copies:
        for copy in pair:
            copy.start()

    def arrived(which):
        for copy in copies[which]:
            copy.wait()

    gain = whole_gain(core_ref, gain_ref, gain_peer_ref)
    rows = 256
    block = 384
    for r in range(x_ref.shape[0] // rows):
        part = pl.ds(r * rows, rows)
        if r == 0:
            arrived(0)
        resid = x_ref[part, :].astype(F32) + mm(low_ref[part, :], wo_ref[...])
        hat, inverse = normalize(resid)
        n2 = (hat * gain).astype(BF16)
        n2_ref[part, :] = n2
        dy = dy_ref[part, :]
        if r == 0:
            arrived(1)
            arrived(2)
        for b in range(FF // block):
            cols = slice(b * block, (b + 1) * block)
            gate_cols = slice(FF + b * block, FF + (b + 1) * block)
            lift = mm(n2, wi_ref[:, cols])
            gate = mm(n2, wi_ref[:, gate_cols])
            d_act = mm(dy, wd_ref[cols, :], NT)
            cdf = 0.5 + 0.5 * lax.erf(lift * (0.5**0.5))
            bell = jnp.exp(-0.5 * lift * lift) * 0.3989422804014327
            gelu = lift * cdf
            act_ref[part, cols] = (gelu * gate).astype(BF16)
            dl_ref[part, cols] = (d_act * gate * (cdf + lift * bell)).astype(BF16)
            dl_ref[part, gate_cols] = (d_act * gelu).astype(BF16)
        result_ref[part, :] = (resid + mm(act_ref[part, :], wd_ref[...])).astype(BF16)
        d_normed = mm(dl_ref[part, :], wi_ref[...], NT)
        d_hat = d_normed * gain
        d_resid = dy.astype(F32) + inverse * (
            d_hat
            - jnp.mean(d_hat, axis=-1, keepdims=True)
            - hat * jnp.mean(d_hat * hat, axis=-1, keepdims=True)
        )
        dres_ref[part, :] = d_resid
        d_proj = d_resid.astype(BF16)
        dproj_ref[part, :] = d_proj
        datt_ref[part, :] = mm(d_proj, wo_ref[...], NT).astype(BF16)


def middle(core, x, low, dy, gain, w_out, w_in, w_down):
    rows = x.shape[0]
    low_shape = lambda n: jax.ShapeDtypeStruct((rows, n), BF16)
    return pl.pallas_call(
        middle_kernel,
        out_shape=(
            low_shape(D), low_shape(D), low_shape(FF), low_shape(2 * FF),
            jax.ShapeDtypeStruct((rows, D), F32), low_shape(D), low_shape(D),
        ),
        in_specs=[smem()] + [vmem()] * 5 + [in_hbm()] * 6,
        out_specs=(vmem(),) * 7,
        scratch_shapes=[
            pltpu.VMEM((D, D), BF16),
            pltpu.VMEM((D, 2 * FF), BF16),
            pltpu.VMEM((FF, D), BF16),
            pltpu.SemaphoreType.DMA((6,)),
        ],
        compiler_params=params(32),
        cost_estimate=cost(2 * rows * D * (2 * D + 6 * FF), 16 * MIB),
        name="middle",
    )(core, x, low, dy, *gain, *w_out, *w_in, *w_down)


def fold_down(ref, block):
    rest = block.shape[0] - HALF
    ref[:, :D] = block[:HALF]
    ref[0:rest, D:FF] = block[HALF:, :HALF]
    ref[rest : 2 * rest, D:FF] = block[HALF:, HALF:]


def narrow_kernel(core_ref, act_ref, dy_ref, peer_ref, own_ref, whole):
    core = core_ref[0]
    for b in range(FF // 384):
        rows = slice(b * 384, (b + 1) * 384)
        whole[rows, :] = mm(act_ref[:, rows], dy_ref[...], TN).astype(BF16)
    size = FF // 2
    for ref, side in ((peer_ref, 1 - core), (own_ref, core)):
        fold_down(ref, whole[pl.ds(pl.multiple_of(side * size, 16), size), :])


def narrow_terms(core, act, dy):
    rows = act.shape[0]
    half = jax.ShapeDtypeStruct((HALF, FF), BF16)
    return pl.pallas_call(
        narrow_kernel,
        out_shape=(half, half),
        in_specs=[smem()] + [vmem()] * 2,
        out_specs=(vmem(), vmem()),
        scratch_shapes=[pltpu.VMEM((FF, D), BF16)],
        compiler_params=params(14),
        cost_estimate=cost(2 * rows * D * FF, 8 * MIB),
        name="narrow_terms",
    )(core, act, dy)


def wide_block(side, n2_ref, dl_ref, low_ref, dproj_ref, store):
    cols = pl.ds(pl.multiple_of(side * HALF, LANES), HALF)
    n2 = n2_ref[:, cols]
    for b in range(2 * FF // 384):
        at = slice(b * 384, (b + 1) * 384)
        store(at, mm(n2, dl_ref[:, at], TN))
    store(slice(2 * FF, WIDE), mm(low_ref[:, cols], dproj_ref[...], TN))


def wide_peer_kernel(core_ref, n2_ref, dl_ref, low_ref, dproj_ref, peer_ref):
    def store(at, block):
        peer_ref[:, at] = block.astype(BF16)

    wide_block(1 - core_ref[0], n2_ref, dl_ref, low_ref, dproj_ref, store)


def wide_peer(core, n2, dl, low, dproj):
    rows = n2.shape[0]
    return pl.pallas_call(
        wide_peer_kernel,
        out_shape=jax.ShapeDtypeStruct((HALF, WIDE), BF16),
        in_specs=[smem()] + [vmem()] * 4,
        out_specs=vmem(),
        compiler_params=params(14),
        cost_estimate=cost(2 * rows * HALF * WIDE, 6 * MIB),
        name="wide_peer",
    )(core, n2, dl, low, dproj)


def split_rows(bit, block, at, keep_ref, send_ref):
    rows = block.shape[0] // 2
    keep_ref[:, at] = jnp.where(bit == 0, block[:rows], block[rows:]).astype(BF16)
    send_ref[:, at] = jnp.where(bit == 0, block[rows:], block[:rows]).astype(BF16)


def first_kernel(
    place_ref, n2_ref, dl_ref, low_ref, dproj_ref, got_ref, down_ref, down_got_ref,
    keep_ref, send_ref, narrow_keep, narrow_send,
):
    def store(at, block):
        split_rows(place_ref[WIDE_SLOT], block + got_ref[:, at].astype(F32), at, keep_ref, send_ref)

    wide_block(place_ref[0], n2_ref, dl_ref, low_ref, dproj_ref, store)
    total = down_ref[...].astype(F32) + down_got_ref[...].astype(F32)
    cut = FLOW - WIDE
    split_rows(place_ref[WIDE_SLOT], total[:, :cut], slice(WIDE, FLOW), keep_ref, send_ref)
    split_rows(place_ref[NARROW_SLOT], total[:, cut:], slice(0, PACK - FLOW), narrow_keep, narrow_send)


def first_sums(place, n2, dl, low, dproj, got, down, down_got, deps):
    rows = n2.shape[0]
    half = jax.ShapeDtypeStruct((HALF // 2, FLOW), BF16)
    narrow = jax.ShapeDtypeStruct((HALF // 2, PACK - FLOW), BF16)
    return pl.pallas_call(
        after(first_kernel, 8, deps),
        out_shape=(half, half, narrow, narrow),
        in_specs=[smem()] + [vmem()] * 7 + [anywhere()] * len(deps),
        out_specs=(vmem(),) * 4,
        compiler_params=params(16),
        cost_estimate=cost(2 * rows * HALF * WIDE, 8 * MIB),
        name="first_sums",
    )(place, n2, dl, low, dproj, got, down, down_got, *deps)


def split_three(values):
    high = values.astype(BF16)
    rest = values - high.astype(F32)
    mid = rest.astype(BF16)
    return high, mid, (rest - mid.astype(F32)).astype(BF16)


def place_three(values, place, others):
    high, mid, tail = split_three(-values)
    at = HEAD_DIM // 2
    out = jnp.where(place == at, high.astype(F32), others)
    out = jnp.where(place == at + 1, mid.astype(F32), out)
    return jnp.where(place == at + 2, tail.astype(F32), out)


def attend_back_kernel(
    q_ref, ko_ref, vo_ref, kp_ref, vp_ref, mq_ref, mk_ref, do_ref, att_ref, lse_ref, cos_ref, sin_ref,
    dq_ref, own_ref, peer_ref,
):
    rows = q_ref.shape[0]
    tile = 256
    query, grad = q_ref[...], do_ref[...]
    place = lane_in_head(query.shape)
    first = lax.broadcasted_iota(jnp.int32, query.shape, 1) < HEAD_DIM
    tile_first = first[:tile]
    product = grad.astype(F32) * att_ref[...]
    lse = pltpu.roll(lse_ref[...], HEAD_DIM, 1)
    mask_q = mq_ref[...].astype(F32)
    zero = jnp.zeros_like(mask_q)
    q_both, g_both = [], []
    for head in range(2):
        side = first if head == 0 else jnp.logical_not(first)
        delta = jnp.sum(jnp.where(side, product, 0.0), axis=-1, keepdims=True)
        q_both.append(jnp.where(side, query, place_three(lse, place, mask_q).astype(BF16)))
        wide = jnp.broadcast_to(delta, product.shape)
        g_both.append(jnp.where(side, grad, place_three(wide, place, zero).astype(BF16)))
    d_query = [jnp.zeros((LANES, rows), F32) for _ in range(2)]
    for source in range(2):
        k_ref, v_ref, out_ref = ((ko_ref, vo_ref, own_ref), (kp_ref, vp_ref, peer_ref))[source]
        for t in range(rows // tile):
            part = pl.ds(t * tile, tile)
            keys, values = k_ref[0, part, :], v_ref[0, part, :]
            keys_across = keys.T
            marks = mk_ref[pl.ds(source * rows + t * tile, tile), :]
            d_keys, d_values = [], []
            for head in range(2):
                side = tile_first if head == 0 else jnp.logical_not(tile_first)
                probs = jnp.exp(mm(jnp.where(side, keys, marks), q_both[head], NT))
                d_probs = mm(jnp.where(side, values, marks), g_both[head], NT)
                d_scores = (probs * d_probs).astype(BF16)
                d_values.append(mm(probs.astype(BF16), grad))
                d_keys.append(mm(d_scores, query))
                d_query[head] = d_query[head] + mm(keys_across, d_scores)
            out_ref[0, part, :] = jnp.where(tile_first, d_keys[0], d_keys[1]).astype(BF16)
            out_ref[1, part, :] = jnp.where(tile_first, d_values[0], d_values[1]).astype(BF16)
    d_q = jnp.concatenate([d_query[0][:HEAD_DIM], d_query[1][HEAD_DIM:]], axis=0).T * HEAD_DIM**-0.5
    dq_ref[...] = (d_q * cos_ref[...] - swap_halves(d_q) * sin_ref[...]).astype(BF16)


def attend_back(first, count, so_far, deps, query, kv_own, kv_peer, mask_q, mask_k, grad, att, lse, cosine, sine):
    rows = query.shape[0]
    keys = mask_k.shape[0]
    pair = pl.BlockSpec((rows, LANES), lambda i: (0, first + i))
    both = pl.BlockSpec((2, rows, LANES), lambda i: (0, 0, first + i))
    whole = lambda n: pl.BlockSpec((n, LANES), lambda i: (0, 0))
    kv = [
        pl.BlockSpec((1, rows, LANES), lambda i: (0, 0, first + i)),
        pl.BlockSpec((1, rows, LANES), lambda i: (1, 0, first + i)),
    ]
    extra = tuple(so_far) + tuple(deps)
    return pl.pallas_call(
        after(attend_back_kernel, 12, extra),
        grid=(count,),
        out_shape=(
            jax.ShapeDtypeStruct((rows, D), BF16),
            jax.ShapeDtypeStruct((2, rows, D), BF16),
            jax.ShapeDtypeStruct((2, rows, D), BF16),
        ),
        in_specs=[pair] + kv + kv
        + [whole(rows), whole(keys), pair, pair, pair, whole(rows), whole(rows)]
        + [anywhere()] * len(extra),
        out_specs=(pair, both, both),
        input_output_aliases={12 + i: i for i in range(len(so_far))},
        compiler_params=params(18),
        cost_estimate=cost(40 * rows * keys * LANES * count, 2 * MIB * count),
        name="attend_back",
    )(query, kv_own, kv_own, kv_peer, kv_peer, mask_q, mask_k, grad, att, lse, cosine, sine, *extra)


def query_terms_kernel(core_ref, n1_ref, dq_ref, peer_ref, own_ref):
    for ref, side in ((peer_ref, 1 - core_ref[0]), (own_ref, core_ref[0])):
        cols = pl.ds(pl.multiple_of(side * HALF, LANES), HALF)
        ref[...] = mm(n1_ref[:, cols], dq_ref[...], TN).astype(BF16)


def query_terms(core, n1, dq, deps):
    rows = n1.shape[0]
    half = jax.ShapeDtypeStruct((HALF, D), BF16)
    return pl.pallas_call(
        after(query_terms_kernel, 3, deps),
        out_shape=(half, half),
        in_specs=[smem()] + [vmem()] * 2 + [anywhere()] * len(deps),
        out_specs=(vmem(), vmem()),
        compiler_params=params(12),
        cost_estimate=cost(2 * rows * D * D, 3 * MIB),
        name="query_terms",
    )(core, n1, dq, *deps)


def key_terms_kernel(core_ref, n1_ref, own_ref, got_ref, cos_ref, sin_ref, peer_ref, dkv_ref):
    cosine, sine = cos_ref[...], sin_ref[...]
    cols = pl.ds(pl.multiple_of((1 - core_ref[0]) * HALF, LANES), HALF)
    n1 = n1_ref[:, cols]
    for pair in range(PAIRS):
        at = slice(pair * LANES, (pair + 1) * LANES)
        d_key = own_ref[0, :, at].astype(F32) + got_ref[0, :, at].astype(F32)
        d_value = own_ref[1, :, at].astype(F32) + got_ref[1, :, at].astype(F32)
        d_key = d_key * cosine - swap_halves(d_key) * sine
        dkv_ref[:, at] = d_key.astype(BF16)
        dkv_ref[:, D + pair * LANES : D + (pair + 1) * LANES] = d_value.astype(BF16)
    for b in range(2 * D // 384):
        at = slice(b * 384, (b + 1) * 384)
        peer_ref[:, at] = mm(n1, dkv_ref[:, at], TN).astype(BF16)


def key_terms(core, n1, own, got, cosine, sine, deps):
    rows = n1.shape[0]
    return pl.pallas_call(
        after(key_terms_kernel, 6, deps),
        out_shape=(jax.ShapeDtypeStruct((HALF, 2 * D), BF16), jax.ShapeDtypeStruct((rows, 2 * D), BF16)),
        in_specs=[smem()] + [vmem()] * 5 + [anywhere()] * len(deps),
        out_specs=(vmem(), vmem()),
        compiler_params=params(16),
        cost_estimate=cost(2 * rows * D * D, 6 * MIB),
        name="key_terms",
    )(core, n1, own, got, cosine, sine, *deps)


def key_own_kernel(place_ref, n1_ref, dkv_ref, own_ref):
    n1 = n1_ref[:, pl.ds(pl.multiple_of(place_ref[0] * HALF, LANES), HALF)]
    for b in range(2 * D // 384):
        at = slice(b * 384, (b + 1) * 384)
        own_ref[:, at] = mm(n1, dkv_ref[:, at], TN).astype(BF16)


def key_own(place, n1, dkv, deps):
    rows = n1.shape[0]
    return pl.pallas_call(
        after(key_own_kernel, 3, deps),
        out_shape=jax.ShapeDtypeStruct((HALF, 2 * D), BF16),
        in_specs=[smem()] + [vmem()] * 2 + [anywhere()] * len(deps),
        out_specs=vmem(),
        compiler_params=params(12),
        cost_estimate=cost(2 * rows * D * D, 6 * MIB),
        name="key_own",
    )(place, n1, dkv, *deps)


def input_kernel(
    core_ref, x_ref, gain_ref, gain_peer_ref, dq_ref, dkv_ref, own_ref, peer_ref, dres_ref, dx_ref, w_ref, sems
):
    copies = halves_in(own_ref, peer_ref, w_ref, sems, 0, core_ref[0])
    for copy in copies:
        copy.start()
    for copy in copies:
        copy.wait()
    gain = whole_gain(core_ref, gain_ref, gain_peer_ref)
    rows = 256
    for r in range(x_ref.shape[0] // rows):
        part = pl.ds(r * rows, rows)
        hat, inverse = normalize(x_ref[part, :].astype(F32))
        d_normed = mm(dq_ref[part, :], w_ref[:, :D], NT) + mm(dkv_ref[part, :], w_ref[:, D:], NT)
        d_hat = d_normed * gain
        back = inverse * (
            d_hat
            - jnp.mean(d_hat, axis=-1, keepdims=True)
            - hat * jnp.mean(d_hat * hat, axis=-1, keepdims=True)
        )
        dx_ref[part, :] = (dres_ref[part, :] + back).astype(BF16)


def input_grad(core, x, gain, dq, dkv, own, peer, dres, deps):
    rows = x.shape[0]
    return pl.pallas_call(
        after(input_kernel, 9, deps),
        out_shape=jax.ShapeDtypeStruct((rows, D), BF16),
        in_specs=[smem()] + [vmem()] * 5 + [in_hbm()] * 2 + [vmem()] + [anywhere()] * len(deps),
        out_specs=vmem(),
        scratch_shapes=[pltpu.VMEM((D, QKV), BF16), pltpu.SemaphoreType.DMA((2,))],
        compiler_params=params(16),
        cost_estimate=cost(2 * rows * D * QKV, 10 * MIB),
        name="input_grad",
    )(core, x, *gain, dq, dkv, own, peer, dres, *deps)


BITS = {"x": 1, "y": 2, "n": 4, "f": 8}
WIDE_ORDER = ("xy", "yx", "nf", "fn")
NARROW_ORDER = ("nf", "fn", "xy", "yx")
KEY_ORDER = ("xy", "yx", "nf", "fn")
QUERY_ORDER = ("nf", "fn", "xy", "yx")
PATTERN = (1, 1, 1, 0, 0, 0, 0)
ALL_ORDERS = WIDE_ORDER + NARROW_ORDER + QUERY_ORDER + KEY_ORDER


def trade(values, axes):
    pairs = []
    for group in range(16):
        for core in range(2):
            pairs.append((2 * group + core, 2 * (group ^ BITS[axes[core]]) + core))
    return lax.ppermute(values, ("rep", "fsdp"), pairs)


def bit_of(axes):
    step = jnp.where(lax.axis_index("fsdp") == 0, BITS[axes[0]], BITS[axes[1]])
    return (lax.axis_index("rep") // step) % 2


def advance_kernel(plan, place_ref, *refs):
    ins, outs = refs[: 2 * len(plan)], list(refs[2 * len(plan) :])
    for i, (mode, slot) in enumerate(plan):
        kept, got = ins[2 * i][...].astype(F32), ins[2 * i + 1][...].astype(F32)
        if mode == "split":
            split_rows(place_ref[slot], kept + got, slice(0, kept.shape[1]), outs.pop(0), outs.pop(0))
        elif mode == "add":
            outs.pop(0)[...] = (kept + got).astype(BF16)
        else:
            bit = place_ref[slot]
            both = [jnp.where(bit == 0, kept, got), jnp.where(bit == 0, got, kept)]
            outs.pop(0)[...] = jnp.concatenate(both, axis=0).astype(BF16)


def advance(place, flows, deps, carried):
    plan, arrays, shapes = [], [], []
    for mode, slot, kept, got in flows:
        rows, cols = kept.shape
        plan.append((mode, slot))
        arrays += [kept, got]
        sizes = {"split": [rows // 2, rows // 2], "add": [rows], "join": [2 * rows]}[mode]
        shapes += [jax.ShapeDtypeStruct((size, cols), BF16) for size in sizes]
    count, made = 1 + len(arrays), len(shapes)
    extra = tuple(carried) + tuple(deps)
    kernel = functools.partial(advance_kernel, plan)

    def body(*refs):
        outs = refs[count + len(extra) :]
        kernel(*refs[:count], *outs[:made])

    outs = pl.pallas_call(
        body,
        out_shape=tuple(shapes) + tuple(jax.ShapeDtypeStruct(a.shape, a.dtype) for a in carried),
        in_specs=[smem()] + [vmem()] * len(arrays) + [anywhere()] * len(extra),
        out_specs=(vmem(),) * made + (anywhere(),) * len(carried),
        input_output_aliases={count + i: made + i for i in range(len(carried))},
        compiler_params=params(12),
        cost_estimate=cost(MIB, 2 * MIB),
        name="advance",
    )(place, *arrays, *extra)
    return outs[:made], outs[made:]


class Chain:
    def __init__(self, place, flows):
        self.place, self.step = place, 0
        self.orders = [order for order, *_ in flows]
        self.slots = [slot for _, slot, *_ in flows]
        self.kept = [kept for *_, kept, _ in flows]
        self.exchange([send for *_, send in flows])

    def exchange(self, sends):
        axis = self.step if self.step < 4 else 7 - self.step
        self.sent = tuple(sends)
        self.got = [trade(send, order[axis]) for send, order in zip(sends, self.orders)]

    def flows(self):
        modes = [("split", self.step + 1), ("add", 0), ("join", 7 - self.step)]
        mode, bit = modes[(self.step >= 3) + (self.step > 3)]
        return [(mode, slot + bit, *pair) for slot, *pair in zip(self.slots, self.kept, self.got)]

    def take(self, parts):
        if self.step < 3:
            self.kept, sends = parts[0::2], parts[1::2]
        else:
            self.kept = sends = parts
        self.step += 1
        self.exchange(sends)

    def advance(self, deps, carried=()):
        parts, carried = advance(self.place, self.flows(), deps, carried)
        self.take(parts)
        return carried


def advance_both(one, two, deps):
    flows = one.flows()
    parts, _ = advance(one.place, flows + two.flows(), deps, ())
    count = sum(2 if mode == "split" else 1 for mode, *_ in flows)
    one.take(parts[:count])
    two.take(parts[count:])


def weighted_sum(total, weight):
    sums = jnp.sum(total * weight.astype(F32), axis=-1, keepdims=True)
    return jnp.broadcast_to(sums, (total.shape[0], LANES))


def finish_mlp_kernel(
    place_ref, mine, theirs, narrow_mine, narrow_theirs, weight_ref, in_ref, out_ref, down_ref, sum_ref
):
    rows = HALF // 2
    rest = FF // 2 - HALF
    cut = FLOW - WIDE
    bit, narrow_bit = place_ref[WIDE_SLOT], place_ref[NARROW_SLOT]
    for half in range(2):
        at = slice(half * rows, (half + 1) * rows)

        def pick(start, stop):
            cols = slice(start, stop)
            return jnp.where(bit == half, mine[:, cols].astype(F32), theirs[:, cols].astype(F32))

        def pick_narrow(start, stop):
            cols = slice(start, stop)
            return jnp.where(
                narrow_bit == half, narrow_mine[:, cols].astype(F32), narrow_theirs[:, cols].astype(F32)
            )

        total = pick(0, 2 * FF)
        in_ref[at, :] = total
        sum_ref[at, :] = weighted_sum(total, weight_ref[at, :])
        out_ref[at, :] = pick(2 * FF, WIDE)
        down_ref[at, :cut] = pick(WIDE, FLOW)
        down_ref[at, cut:] = pick_narrow(0, D - cut)
        down_ref[HALF : HALF + rest, half * HALF : (half + 1) * HALF] = pick_narrow(D - cut, FF - cut)


def mlp_outputs():
    return (
        jax.ShapeDtypeStruct((HALF, 2 * FF), F32),
        jax.ShapeDtypeStruct((HALF, D), F32),
        jax.ShapeDtypeStruct((FF // 2, D), F32),
        jax.ShapeDtypeStruct((HALF, LANES), F32),
    )


def finish_mlp(place, mine, theirs, narrow_mine, narrow_theirs, weight, deps):
    return pl.pallas_call(
        after(finish_mlp_kernel, 6, deps),
        out_shape=mlp_outputs(),
        in_specs=[smem()] + [vmem()] * 5 + [anywhere()] * len(deps),
        out_specs=(vmem(),) * 4,
        compiler_params=params(20),
        cost_estimate=cost(MIB, 10 * MIB),
        name="finish_mlp",
    )(place, mine, theirs, narrow_mine, narrow_theirs, weight, *deps)


def finish_qkv_kernel(place_ref, q_ref, q_got, kv_ref, kv_got, weight_ref, out_ref, sum_ref):
    step = out_ref.shape[0]
    half = pl.program_id(0) * step // (HALF // 2)
    at = pl.ds(pl.multiple_of(pl.program_id(0) * step - half * (HALF // 2), step), step)
    sums = jnp.zeros((step, LANES), F32)
    for slot, mine, theirs, start in ((QUERY_SLOT, q_ref, q_got, 0), (KEY_SLOT, kv_ref, kv_got, D)):
        cols = slice(start, start + mine.shape[1])
        total = jnp.where(place_ref[slot] == half, mine[at, :].astype(F32), theirs[at, :].astype(F32))
        out_ref[:, cols] = total
        sums = sums + weighted_sum(total, weight_ref[:, cols])
    sum_ref[...] = sums


def finish_qkv(place, q_mine, q_theirs, kv_mine, kv_theirs, weight, deps):
    step = 96
    whole = lambda array: pl.BlockSpec(array.shape, lambda i: (0, 0))
    arrays = (q_mine, q_theirs, kv_mine, kv_theirs)
    return pl.pallas_call(
        after(finish_qkv_kernel, 6, deps),
        grid=(HALF // step,),
        out_shape=(jax.ShapeDtypeStruct((HALF, QKV), F32), jax.ShapeDtypeStruct((HALF, LANES), F32)),
        in_specs=[smem()] + [whole(array) for array in arrays] + [pl.BlockSpec((step, QKV), lambda i: (i, 0))]
        + [anywhere()] * len(deps),
        out_specs=(
            pl.BlockSpec((step, QKV), lambda i: (i, 0)),
            pl.BlockSpec((step, LANES), lambda i: (i, 0)),
        ),
        compiler_params=params(14),
        cost_estimate=cost(MIB, 7 * MIB),
        name="finish_qkv",
    )(place, *arrays, weight, *deps)


def add(left, right):
    return (left.astype(F32) + right.astype(F32)).astype(BF16)


def swap_cores(values):
    return lax.ppermute(values, "fsdp", [(0, 1), (1, 0)])


def layout(lengths, slot_count):
    slots = jnp.arange(slot_count, dtype=jnp.int32)
    order = jnp.arange(lengths.shape[0])
    ends = jnp.sum(jnp.where(order[None, :] <= order[:, None], lengths[None, :], 0), axis=1)
    segment = jnp.sum((slots[:, None] >= ends[None, :]).astype(jnp.int32), axis=1)
    begins = jnp.max(jnp.where(ends[None, :] <= slots[:, None], ends[None, :], 0), axis=1)
    return (segment, slots - begins)


def on_device(
    tokens, attn_gain, qkv_weight, out_weight, mlp_gain, in_weight, down_weight, seq_len, cotangent
):
    row_count = tokens.shape[0]
    core = lax.axis_index("fsdp")
    paired = lax.axis_size("rep") == 16
    bits = [bit_of(axes) if paired else 0 * core for axes in ALL_ORDERS]
    place = jnp.stack([core] + bits).astype(jnp.int32)
    peer_qkv = swap_cores(qkv_weight)
    own_gains = (attn_gain.reshape(1, HALF), mlp_gain.reshape(1, HALF))
    gain_one, gain_two = [(own, swap_cores(own)) for own in own_gains]
    peer_out = swap_cores(out_weight)
    peer_in = swap_cores(in_weight)
    peer_down = swap_cores(down_weight)
    key_seg, key_pos = layout(seq_len[0], 2 * row_count)
    own_seg = lax.dynamic_slice_in_dim(key_seg, core * row_count, row_count)
    peer_seg = lax.dynamic_slice_in_dim(key_seg, (1 - core) * row_count, row_count)
    own_pos = lax.dynamic_slice_in_dim(key_pos, core * row_count, row_count)
    lane = jnp.arange(LANES, dtype=jnp.int32) % HEAD_DIM
    half_dim = HEAD_DIM // 2
    freq = jnp.exp(-jnp.log(rope_base) * (2.0 * (lane % half_dim).astype(F32) / HEAD_DIM))
    angles = own_pos.astype(F32)[:, None] * freq[None, :]
    cosine = jnp.cos(angles)
    sine = jnp.sin(angles) * jnp.where(lane < half_dim, -1.0, 1.0)[None, :]
    marks = lane < half_dim
    mask_q = jnp.where(marks[None, :] & (own_seg[:, None] != lane[None, :]), BLOCKED, 0.0).astype(BF16)
    both_seg = jnp.concatenate([own_seg, peer_seg])
    mask_k = jnp.where(
        marks[None, :], both_seg[:, None] == lane[None, :], (lane < half_dim + 3)[None, :]
    ).astype(BF16)

    n1 = first_norm(place, tokens, gain_one)
    project_args = (place, n1, qkv_weight, peer_qkv, cosine, sine)
    kv_own = project((1, 2), 1.0, *project_args, ())
    kv_peer = swap_cores(kv_own)
    query = project((0,), HEAD_DIM**-0.5, *project_args, (kv_own,)).reshape(row_count, D)
    att, low, lse = attend(query, kv_own, kv_peer, mask_q, mask_k)
    result, n2, act, dl, dres, dproj, datt = middle(
        place, tokens, low, cotangent, gain_two,
        (out_weight, peer_out), (in_weight, peer_in), (down_weight, peer_down),
    )
    wide_for_peer = wide_peer(place, n2, dl, low, dproj)
    wide_got = swap_cores(wide_for_peer)
    narrow_for_peer, narrow_own = narrow_terms(place, act, cotangent)
    narrow_got = swap_cores(narrow_for_peer)
    back_args = (query, kv_own, kv_peer, mask_q, mask_k, datt, att, lse, cosine, sine)
    grads = attend_back(0, 1, (), (wide_for_peer, narrow_own), *back_args)
    wide_keep, wide_send, narrow_keep, narrow_send = first_sums(place, n2, dl, low, dproj, wide_got, narrow_own, narrow_got, grads[:1])

    def input_part(deps):
        return input_grad(place, tokens, gain_one, dq, dkv, qkv_weight, peer_qkv, dres, deps)

    if paired:
        mlp = Chain(
            place,
            [
                (WIDE_ORDER, WIDE_SLOT, wide_keep, wide_send),
                (NARROW_ORDER, NARROW_SLOT, narrow_keep, narrow_send),
            ],
        )
        grads = attend_back(1, 3, grads, mlp.sent, *back_args)
        mlp.advance(grads[:1])
        dq, dkv_own, dkv_peer = attend_back(4, 2, grads, mlp.sent, *back_args)
        (dkv_peer,) = mlp.advance((dq,), (dkv_peer,))
        dkv_got = swap_cores(dkv_peer)
        query_for_peer, query_own = query_terms(place, n1, dq, mlp.sent)
        key_for_peer, dkv = key_terms(place, n1, dkv_own, dkv_got, cosine, sine, (query_own,))
        query_for_peer, key_for_peer = mlp.advance((dkv,), (query_for_peer, key_for_peer))
        key_got, query_got = swap_cores(key_for_peer), swap_cores(query_for_peer)
        key_mine = key_own(place, n1, dkv, mlp.sent)
        grad_tokens = input_part((key_mine,))
        mlp.advance((grad_tokens,))
        (kv_keep, kv_send, q_keep, q_send), _ = advance(
            place,
            [("split", KEY_SLOT, key_mine, key_got), ("split", QUERY_SLOT, query_own, query_got)],
            mlp.sent,
            (),
        )
        qkv = Chain(
            place,
            [(KEY_ORDER, KEY_SLOT, kv_keep, kv_send), (QUERY_ORDER, QUERY_SLOT, q_keep, q_send)],
        )
        deps = ()
        for joint in PATTERN:
            if joint:
                advance_both(qkv, mlp, deps)
            else:
                qkv.advance(deps)
            deps = ()
        grad_in, grad_out, grad_down, in_sums = finish_mlp(
            place, mlp.kept[0], mlp.got[0], mlp.kept[1], mlp.got[1], in_weight, qkv.sent
        )
        grad_qkv, qkv_sums = finish_qkv(
            place, qkv.kept[1], qkv.got[1], qkv.kept[0], qkv.got[0], qkv_weight, (in_sums,)
        )
    else:
        grads = attend_back(1, PAIRS - 1, grads, (), *back_args)
        dq, dkv_own, dkv_peer = grads
        query_for_peer, query_own = query_terms(place, n1, dq, ())
        key_for_peer, dkv = key_terms(place, n1, dkv_own, swap_cores(dkv_peer), cosine, sine, ())
        pieces = []
        for own, for_peer in ((query_own, query_for_peer), (key_own(place, n1, dkv, ()), key_for_peer)):
            total = add(own, swap_cores(for_peer))
            pieces += [total[: HALF // 2], total[HALF // 2 :]]
        grad_tokens = input_part(())
        total = lambda part: lax.psum(part.astype(F32), "rep")
        grad_qkv, qkv_sums = finish_qkv(place, *[total(part) for part in pieces], qkv_weight, ())
        grad_in, grad_out, grad_down, in_sums = finish_mlp(
            place, *[total(part) for part in (wide_keep, wide_send, narrow_keep, narrow_send)], in_weight, ()
        )
    grad_gain_one = qkv_sums[:, 0] / attn_gain.astype(F32)
    grad_gain_two = in_sums[:, 0] / mlp_gain.astype(F32)
    return (
        result,
        grad_tokens,
        grad_gain_one,
        grad_qkv,
        grad_out,
        grad_gain_two,
        grad_in,
        grad_down,
    )


def solution(mesh):
    rows = P(("rep", "fsdp"), None)
    vector, matrix = P("fsdp"), P("fsdp", None)
    in_specs = (rows, vector, matrix, matrix, vector, matrix, matrix, P("rep", None), rows)
    out_specs = (rows, rows, vector, matrix, matrix, vector, matrix, matrix)
    return jax.shard_map(
        on_device, mesh=mesh, in_specs=in_specs, out_specs=out_specs, check_vma=False
    )
```

```python
import functools

import jax
import jax.numpy as jnp
from jax import lax
from jax.experimental import pallas as pl
from jax.experimental.pallas import tpu as pltpu
from jax.sharding import PartitionSpec as P

D = 768
HEADS = 12
HEAD_DIM = 64
FF = 1152
HALF = D // 2
LANES = 128
PAIRS = D // LANES
QKV = 3 * D
WIDE = 2 * FF + D
PACK = WIDE + FF
FLOW = 3200
LEAD = 256
KEY_FLOW = 2 * D + LEAD
WIDE_SLOT, NARROW_SLOT, QUERY_SLOT, KEY_SLOT = 1, 5, 9, 13

epsilon = 1e-05
rope_base = 160000.0
BLOCKED = -(2.0**100)
F32 = jnp.float32
BF16 = jnp.bfloat16
MIB = 1 << 20

NN = (((1,), (0,)), ((), ()))
NT = (((1,), (1,)), ((), ()))
TN = (((0,), (0,)), ((), ()))


def mm(a, b, dims=NN):
    return lax.dot_general(a, b, dims, preferred_element_type=F32)


def vmem():
    return pl.BlockSpec(memory_space=pltpu.VMEM)


def anywhere():
    return pl.BlockSpec(memory_space=pl.ANY)


def in_hbm():
    return pl.BlockSpec(memory_space=pltpu.HBM)


def after(kernel, count, deps):
    def body(*refs):
        kernel(*refs[:count], *refs[count + len(deps) :])

    return body


def smem():
    return pl.BlockSpec(memory_space=pltpu.SMEM)


def params(mib):
    return pltpu.CompilerParams(vmem_limit_bytes=mib * MIB)


def cost(flops, nbytes):
    return pl.CostEstimate(flops=int(flops) >> 10, bytes_accessed=int(nbytes) >> 10, transcendentals=0)


def halves_in(own_ref, peer_ref, whole, sems, slot, core):
    rows = own_ref.shape[0]
    mine = pl.multiple_of(core * rows, 16)
    other = pl.multiple_of((1 - core) * rows, 16)
    return (
        pltpu.make_async_copy(own_ref, whole.at[pl.ds(mine, rows), :], sems.at[slot]),
        pltpu.make_async_copy(peer_ref, whole.at[pl.ds(other, rows), :], sems.at[slot + 1]),
    )


def lane_in_head(shape):
    return lax.broadcasted_iota(jnp.int32, shape, 1) % HEAD_DIM


def swap_halves(values):
    place = lane_in_head(values.shape)
    return jnp.where(
        place < HEAD_DIM // 2,
        pltpu.roll(values, LANES - HEAD_DIM // 2, 1),
        pltpu.roll(values, HEAD_DIM // 2, 1),
    )


def normalize(values):
    row_mean = jnp.mean(values, axis=-1, keepdims=True)
    centred = values - row_mean
    row_var = jnp.mean(centred * centred, axis=-1, keepdims=True)
    inverse = lax.rsqrt(row_var + epsilon)
    return centred * inverse, inverse


def whole_gain(place_ref, own_ref, peer_ref):
    own, peer = own_ref[...].astype(F32), peer_ref[...].astype(F32)
    first = place_ref[0] == 0
    return jnp.concatenate([jnp.where(first, own, peer), jnp.where(first, peer, own)], axis=1)


def norm_kernel(place_ref, x_ref, own_ref, peer_ref, n_ref):
    hat, _ = normalize(x_ref[...].astype(F32))
    n_ref[...] = (hat * whole_gain(place_ref, own_ref, peer_ref)).astype(BF16)


def first_norm(place, x, gain):
    rows = 128
    block = pl.BlockSpec((rows, D), lambda i: (i, 0))
    return pl.pallas_call(
        norm_kernel,
        grid=(x.shape[0] // rows,),
        out_shape=jax.ShapeDtypeStruct(x.shape, BF16),
        in_specs=[smem(), block] + [pl.BlockSpec((1, HALF), lambda i: (0, 0))] * 2,
        out_specs=block,
        compiler_params=params(8),
        cost_estimate=cost(MIB, 2 * MIB),
        name="first_norm",
    )(place, x, *gain)


def project_kernel(parts, scale, place_ref, n_ref, own_ref, peer_ref, cos_ref, sin_ref, out_ref):
    core = place_ref[0]
    mine = pl.ds(pl.multiple_of(core * HALF, LANES), HALF)
    other = pl.ds(pl.multiple_of((1 - core) * HALF, LANES), HALF)
    rows = 256
    for r in range(n_ref.shape[0] // rows):
        part = pl.ds(r * rows, rows)
        left, right = n_ref[part, mine], n_ref[part, other]
        cosine, sine = cos_ref[part, :], sin_ref[part, :]
        for i, which in enumerate(parts):
            for half in range(2):
                at = slice(which * D + half * HALF, which * D + (half + 1) * HALF)
                out = mm(left, own_ref[:, at]) + mm(right, peer_ref[:, at])
                for tile in range(HALF // LANES):
                    piece = out[:, tile * LANES : (tile + 1) * LANES]
                    if which < 2:
                        piece = piece * cosine + swap_halves(piece) * sine
                    cols = pl.ds(half * HALF + tile * LANES, LANES)
                    out_ref[i, part, cols] = (piece * scale).astype(BF16)


def project(parts, scale, place, normed, own, peer, cosine, sine, deps):
    rows = normed.shape[0]
    return pl.pallas_call(
        after(functools.partial(project_kernel, parts, scale), 6, deps),
        out_shape=jax.ShapeDtypeStruct((len(parts), rows, D), BF16),
        in_specs=[smem()] + [vmem()] * 5 + [anywhere()] * len(deps),
        out_specs=vmem(),
        compiler_params=params(12),
        cost_estimate=cost(2 * rows * D * D * len(parts), 8 * MIB),
        name="project",
    )(place, normed, own, peer, cosine, sine, *deps)


def attend_kernel(q_ref, ko_ref, vo_ref, kp_ref, vp_ref, mq_ref, mk_ref, att_ref, low_ref, lse_ref):
    rows = q_ref.shape[0]
    tile = min(512, rows)
    keys = jnp.concatenate([ko_ref[0], kp_ref[0]], axis=0)
    values = jnp.concatenate([vo_ref[0], vp_ref[0]], axis=0)
    key_first = lax.broadcasted_iota(jnp.int32, keys.shape, 1) < HEAD_DIM
    one = jnp.ones_like(values)
    mask_keys = mk_ref[...]
    k_both = (jnp.where(key_first, keys, mask_keys), jnp.where(key_first, mask_keys, keys))
    v_both = (jnp.where(key_first, values, one), jnp.where(key_first, one, values))
    first = lax.broadcasted_iota(jnp.int32, (tile, LANES), 1) < HEAD_DIM
    for t in range(rows // tile):
        part = pl.ds(t * tile, tile)
        query, mask_q = q_ref[part, :], mq_ref[part, :]
        sums, peaks = [], []
        for head in range(2):
            side = first if head == 0 else jnp.logical_not(first)
            scores = mm(jnp.where(side, query, mask_q), k_both[head], NT)
            peak = jnp.max(scores, axis=-1, keepdims=True)
            weights = jnp.exp(scores - peak).astype(BF16)
            sums.append(mm(weights, v_both[head]))
            peaks.append(peak)
        numer = jnp.where(first, sums[0], sums[1])
        denom = jnp.where(first, pltpu.roll(sums[0], HEAD_DIM, 1), pltpu.roll(sums[1], HEAD_DIM, 1))
        out = numer / denom
        att_ref[part, :] = out
        low_ref[part, :] = out.astype(BF16)
        lse_ref[part, :] = jnp.where(first, peaks[0], peaks[1]) + jnp.log(denom)


def kv_specs(rows):
    return [
        pl.BlockSpec((1, rows, LANES), lambda i: (0, 0, i)),
        pl.BlockSpec((1, rows, LANES), lambda i: (1, 0, i)),
    ]


def attend(query, kv_own, kv_peer, mask_q, mask_k):
    rows = query.shape[0]
    keys = mask_k.shape[0]
    pair = pl.BlockSpec((rows, LANES), lambda i: (0, i))
    whole = lambda n: pl.BlockSpec((n, LANES), lambda i: (0, 0))
    return pl.pallas_call(
        attend_kernel,
        grid=(PAIRS,),
        out_shape=(
            jax.ShapeDtypeStruct((rows, D), F32),
            jax.ShapeDtypeStruct((rows, D), BF16),
            jax.ShapeDtypeStruct((rows, D), F32),
        ),
        in_specs=[pair] + kv_specs(rows) + kv_specs(rows) + [whole(rows), whole(keys)],
        out_specs=(pair, pair, pair),
        compiler_params=params(16),
        cost_estimate=cost(16 * rows * keys * D, 8 * MIB),
        name="attend",
    )(query, kv_own, kv_own, kv_peer, kv_peer, mask_q, mask_k)


def middle_kernel(
    core_ref, x_ref, low_ref, dy_ref, gain_ref, gain_peer_ref,
    oo_ref, op_ref, io_ref, ip_ref, do_ref, dp_ref,
    result_ref, n2_ref, act_ref, dl_ref, dres_ref, dproj_ref, datt_ref,
    wo_ref, wi_ref, wd_ref, sems,
):
    core = core_ref[0]
    copies = (
        halves_in(oo_ref, op_ref, wo_ref, sems, 0, core),
        halves_in(io_ref, ip_ref, wi_ref, sems, 2, core),
        halves_in(do_ref, dp_ref, wd_ref, sems, 4, core),
    )
    for pair in copies:
        for copy in pair:
            copy.start()

    def arrived(which):
        for copy in copies[which]:
            copy.wait()

    gain = whole_gain(core_ref, gain_ref, gain_peer_ref)
    rows = 256
    block = 384
    for r in range(x_ref.shape[0] // rows):
        part = pl.ds(r * rows, rows)
        if r == 0:
            arrived(0)
        resid = x_ref[part, :].astype(F32) + mm(low_ref[part, :], wo_ref[...])
        hat, inverse = normalize(resid)
        n2 = (hat * gain).astype(BF16)
        n2_ref[part, :] = n2
        dy = dy_ref[part, :]
        if r == 0:
            arrived(1)
            arrived(2)
        for b in range(FF // block):
            cols = slice(b * block, (b + 1) * block)
            gate_cols = slice(FF + b * block, FF + (b + 1) * block)
            lift = mm(n2, wi_ref[:, cols])
            gate = mm(n2, wi_ref[:, gate_cols])
            d_act = mm(dy, wd_ref[cols, :], NT)
            cdf = 0.5 + 0.5 * lax.erf(lift * (0.5**0.5))
            bell = jnp.exp(-0.5 * lift * lift) * 0.3989422804014327
            gelu = lift * cdf
            act_ref[part, cols] = (gelu * gate).astype(BF16)
            dl_ref[part, cols] = (d_act * gate * (cdf + lift * bell)).astype(BF16)
            dl_ref[part, gate_cols] = (d_act * gelu).astype(BF16)
        result_ref[part, :] = (resid + mm(act_ref[part, :], wd_ref[...])).astype(BF16)
        d_normed = mm(dl_ref[part, :], wi_ref[...], NT)
        d_hat = d_normed * gain
        d_resid = dy.astype(F32) + inverse * (
            d_hat
            - jnp.mean(d_hat, axis=-1, keepdims=True)
            - hat * jnp.mean(d_hat * hat, axis=-1, keepdims=True)
        )
        dres_ref[part, :] = d_resid
        d_proj = d_resid.astype(BF16)
        dproj_ref[part, :] = d_proj
        datt_ref[part, :] = mm(d_proj, wo_ref[...], NT).astype(BF16)


def middle(core, x, low, dy, gain, w_out, w_in, w_down):
    rows = x.shape[0]
    low_shape = lambda n: jax.ShapeDtypeStruct((rows, n), BF16)
    return pl.pallas_call(
        middle_kernel,
        out_shape=(
            low_shape(D), low_shape(D), low_shape(FF), low_shape(2 * FF),
            jax.ShapeDtypeStruct((rows, D), F32), low_shape(D), low_shape(D),
        ),
        in_specs=[smem()] + [vmem()] * 5 + [in_hbm()] * 6,
        out_specs=(vmem(),) * 7,
        scratch_shapes=[
            pltpu.VMEM((D, D), BF16),
            pltpu.VMEM((D, 2 * FF), BF16),
            pltpu.VMEM((FF, D), BF16),
            pltpu.SemaphoreType.DMA((6,)),
        ],
        compiler_params=params(32),
        cost_estimate=cost(2 * rows * D * (2 * D + 6 * FF), 16 * MIB),
        name="middle",
    )(core, x, low, dy, *gain, *w_out, *w_in, *w_down)


def fold_down(ref, block):
    rest = block.shape[0] - HALF
    ref[:, :D] = block[:HALF]
    ref[0:rest, D:FF] = block[HALF:, :HALF]
    ref[rest : 2 * rest, D:FF] = block[HALF:, HALF:]


def narrow_kernel(core_ref, act_ref, dy_ref, peer_ref, own_ref, whole):
    core = core_ref[0]
    for b in range(FF // 384):
        rows = slice(b * 384, (b + 1) * 384)
        whole[rows, :] = mm(act_ref[:, rows], dy_ref[...], TN).astype(BF16)
    size = FF // 2
    for ref, side in ((peer_ref, 1 - core), (own_ref, core)):
        fold_down(ref, whole[pl.ds(pl.multiple_of(side * size, 16), size), :])


def narrow_terms(core, act, dy):
    rows = act.shape[0]
    half = jax.ShapeDtypeStruct((HALF, FF), BF16)
    return pl.pallas_call(
        narrow_kernel,
        out_shape=(half, half),
        in_specs=[smem()] + [vmem()] * 2,
        out_specs=(vmem(), vmem()),
        scratch_shapes=[pltpu.VMEM((FF, D), BF16)],
        compiler_params=params(14),
        cost_estimate=cost(2 * rows * D * FF, 8 * MIB),
        name="narrow_terms",
    )(core, act, dy)


def wide_block(side, n2_ref, dl_ref, low_ref, dproj_ref, store):
    cols = pl.ds(pl.multiple_of(side * HALF, LANES), HALF)
    n2 = n2_ref[:, cols]
    for b in range(2 * FF // 384):
        at = slice(b * 384, (b + 1) * 384)
        store(at, mm(n2, dl_ref[:, at], TN))
    store(slice(2 * FF, WIDE), mm(low_ref[:, cols], dproj_ref[...], TN))


def wide_peer_kernel(core_ref, n2_ref, dl_ref, low_ref, dproj_ref, peer_ref):
    def store(at, block):
        peer_ref[:, at] = block.astype(BF16)

    wide_block(1 - core_ref[0], n2_ref, dl_ref, low_ref, dproj_ref, store)


def wide_peer(core, n2, dl, low, dproj):
    rows = n2.shape[0]
    return pl.pallas_call(
        wide_peer_kernel,
        out_shape=jax.ShapeDtypeStruct((HALF, WIDE), BF16),
        in_specs=[smem()] + [vmem()] * 4,
        out_specs=vmem(),
        compiler_params=params(14),
        cost_estimate=cost(2 * rows * HALF * WIDE, 6 * MIB),
        name="wide_peer",
    )(core, n2, dl, low, dproj)


def split_rows(bit, block, at, keep_ref, send_ref):
    rows = block.shape[0] // 2
    keep_ref[:, at] = jnp.where(bit == 0, block[:rows], block[rows:]).astype(BF16)
    send_ref[:, at] = jnp.where(bit == 0, block[rows:], block[:rows]).astype(BF16)


def first_kernel(
    place_ref, n2_ref, dl_ref, low_ref, dproj_ref, got_ref, down_ref, down_got_ref,
    keep_ref, send_ref, narrow_keep, narrow_send,
):
    def store(at, block):
        split_rows(place_ref[WIDE_SLOT], block + got_ref[:, at].astype(F32), at, keep_ref, send_ref)

    wide_block(place_ref[0], n2_ref, dl_ref, low_ref, dproj_ref, store)
    total = down_ref[...].astype(F32) + down_got_ref[...].astype(F32)
    cut = FLOW - WIDE
    split_rows(place_ref[WIDE_SLOT], total[:, :cut], slice(WIDE, FLOW), keep_ref, send_ref)
    split_rows(place_ref[NARROW_SLOT], total[:, cut:], slice(0, PACK - FLOW), narrow_keep, narrow_send)


def first_sums(place, n2, dl, low, dproj, got, down, down_got, deps):
    rows = n2.shape[0]
    half = jax.ShapeDtypeStruct((HALF // 2, FLOW), BF16)
    narrow = jax.ShapeDtypeStruct((HALF // 2, PACK - FLOW), BF16)
    return pl.pallas_call(
        after(first_kernel, 8, deps),
        out_shape=(half, half, narrow, narrow),
        in_specs=[smem()] + [vmem()] * 7 + [anywhere()] * len(deps),
        out_specs=(vmem(),) * 4,
        compiler_params=params(16),
        cost_estimate=cost(2 * rows * HALF * WIDE, 8 * MIB),
        name="first_sums",
    )(place, n2, dl, low, dproj, got, down, down_got, *deps)


def split_three(values):
    high = values.astype(BF16)
    rest = values - high.astype(F32)
    mid = rest.astype(BF16)
    return high, mid, (rest - mid.astype(F32)).astype(BF16)


def place_three(values, place, others):
    high, mid, tail = split_three(-values)
    at = HEAD_DIM // 2
    out = jnp.where(place == at, high.astype(F32), others)
    out = jnp.where(place == at + 1, mid.astype(F32), out)
    return jnp.where(place == at + 2, tail.astype(F32), out)


def attend_back_kernel(
    q_ref, ko_ref, vo_ref, kp_ref, vp_ref, mq_ref, mk_ref, do_ref, att_ref, lse_ref, cos_ref, sin_ref,
    dq_ref, own_ref, peer_ref,
):
    rows = q_ref.shape[0]
    tile = 256
    query, grad = q_ref[...], do_ref[...]
    place = lane_in_head(query.shape)
    first = lax.broadcasted_iota(jnp.int32, query.shape, 1) < HEAD_DIM
    tile_first = first[:tile]
    product = grad.astype(F32) * att_ref[...]
    lse = pltpu.roll(lse_ref[...], HEAD_DIM, 1)
    mask_q = mq_ref[...].astype(F32)
    zero = jnp.zeros_like(mask_q)
    q_both, g_both = [], []
    for head in range(2):
        side = first if head == 0 else jnp.logical_not(first)
        delta = jnp.sum(jnp.where(side, product, 0.0), axis=-1, keepdims=True)
        q_both.append(jnp.where(side, query, place_three(lse, place, mask_q).astype(BF16)))
        wide = jnp.broadcast_to(delta, product.shape)
        g_both.append(jnp.where(side, grad, place_three(wide, place, zero).astype(BF16)))
    d_query = [jnp.zeros((LANES, rows), F32) for _ in range(2)]
    for source in range(2):
        k_ref, v_ref, out_ref = ((ko_ref, vo_ref, own_ref), (kp_ref, vp_ref, peer_ref))[source]
        for t in range(rows // tile):
            part = pl.ds(t * tile, tile)
            keys, values = k_ref[0, part, :], v_ref[0, part, :]
            keys_across = keys.T
            marks = mk_ref[pl.ds(source * rows + t * tile, tile), :]
            d_keys, d_values = [], []
            for head in range(2):
                side = tile_first if head == 0 else jnp.logical_not(tile_first)
                probs = jnp.exp(mm(jnp.where(side, keys, marks), q_both[head], NT))
                d_probs = mm(jnp.where(side, values, marks), g_both[head], NT)
                d_scores = (probs * d_probs).astype(BF16)
                d_values.append(mm(probs.astype(BF16), grad))
                d_keys.append(mm(d_scores, query))
                d_query[head] = d_query[head] + mm(keys_across, d_scores)
            out_ref[0, part, :] = jnp.where(tile_first, d_keys[0], d_keys[1]).astype(BF16)
            out_ref[1, part, :] = jnp.where(tile_first, d_values[0], d_values[1]).astype(BF16)
    d_q = jnp.concatenate([d_query[0][:HEAD_DIM], d_query[1][HEAD_DIM:]], axis=0).T * HEAD_DIM**-0.5
    dq_ref[...] = (d_q * cos_ref[...] - swap_halves(d_q) * sin_ref[...]).astype(BF16)


def attend_back(first, count, so_far, deps, query, kv_own, kv_peer, mask_q, mask_k, grad, att, lse, cosine, sine):
    rows = query.shape[0]
    keys = mask_k.shape[0]
    pair = pl.BlockSpec((rows, LANES), lambda i: (0, first + i))
    both = pl.BlockSpec((2, rows, LANES), lambda i: (0, 0, first + i))
    whole = lambda n: pl.BlockSpec((n, LANES), lambda i: (0, 0))
    kv = [
        pl.BlockSpec((1, rows, LANES), lambda i: (0, 0, first + i)),
        pl.BlockSpec((1, rows, LANES), lambda i: (1, 0, first + i)),
    ]
    extra = tuple(so_far) + tuple(deps)
    return pl.pallas_call(
        after(attend_back_kernel, 12, extra),
        grid=(count,),
        out_shape=(
            jax.ShapeDtypeStruct((rows, D), BF16),
            jax.ShapeDtypeStruct((2, rows, D), BF16),
            jax.ShapeDtypeStruct((2, rows, D), BF16),
        ),
        in_specs=[pair] + kv + kv
        + [whole(rows), whole(keys), pair, pair, pair, whole(rows), whole(rows)]
        + [anywhere()] * len(extra),
        out_specs=(pair, both, both),
        input_output_aliases={12 + i: i for i in range(len(so_far))},
        compiler_params=params(18),
        cost_estimate=cost(40 * rows * keys * LANES * count, 2 * MIB * count),
        name="attend_back",
    )(query, kv_own, kv_own, kv_peer, kv_peer, mask_q, mask_k, grad, att, lse, cosine, sine, *extra)


def query_terms_kernel(core_ref, n1_ref, dq_ref, peer_ref, own_ref):
    for ref, side in ((peer_ref, 1 - core_ref[0]), (own_ref, core_ref[0])):
        cols = pl.ds(pl.multiple_of(side * HALF, LANES), HALF)
        ref[...] = mm(n1_ref[:, cols], dq_ref[:, LEAD:], TN).astype(BF16)


def query_terms(core, n1, dq, deps):
    rows = n1.shape[0]
    half = jax.ShapeDtypeStruct((HALF, D - LEAD), BF16)
    return pl.pallas_call(
        after(query_terms_kernel, 3, deps),
        out_shape=(half, half),
        in_specs=[smem()] + [vmem()] * 2 + [anywhere()] * len(deps),
        out_specs=(vmem(), vmem()),
        compiler_params=params(12),
        cost_estimate=cost(2 * rows * D * D, 3 * MIB),
        name="query_terms",
    )(core, n1, dq, *deps)


def key_terms_kernel(core_ref, n1_ref, dq_ref, own_ref, got_ref, cos_ref, sin_ref, peer_ref, dkv_ref):
    cosine, sine = cos_ref[...], sin_ref[...]
    cols = pl.ds(pl.multiple_of((1 - core_ref[0]) * HALF, LANES), HALF)
    n1 = n1_ref[:, cols]
    for pair in range(PAIRS):
        at = slice(pair * LANES, (pair + 1) * LANES)
        d_key = own_ref[0, :, at].astype(F32) + got_ref[0, :, at].astype(F32)
        d_value = own_ref[1, :, at].astype(F32) + got_ref[1, :, at].astype(F32)
        d_key = d_key * cosine - swap_halves(d_key) * sine
        dkv_ref[:, at] = d_key.astype(BF16)
        dkv_ref[:, D + pair * LANES : D + (pair + 1) * LANES] = d_value.astype(BF16)
    for b in range(2 * D // 384):
        at = slice(b * 384, (b + 1) * 384)
        peer_ref[:, at] = mm(n1, dkv_ref[:, at], TN).astype(BF16)
    peer_ref[:, 2 * D :] = mm(n1, dq_ref[:, :LEAD], TN).astype(BF16)


def key_terms(core, n1, dq, own, got, cosine, sine, deps):
    rows = n1.shape[0]
    return pl.pallas_call(
        after(key_terms_kernel, 7, deps),
        out_shape=(jax.ShapeDtypeStruct((HALF, KEY_FLOW), BF16), jax.ShapeDtypeStruct((rows, 2 * D), BF16)),
        in_specs=[smem()] + [vmem()] * 6 + [anywhere()] * len(deps),
        out_specs=(vmem(), vmem()),
        compiler_params=params(16),
        cost_estimate=cost(2 * rows * D * D, 6 * MIB),
        name="key_terms",
    )(core, n1, dq, own, got, cosine, sine, *deps)


def key_own_kernel(place_ref, n1_ref, dq_ref, dkv_ref, own_ref):
    n1 = n1_ref[:, pl.ds(pl.multiple_of(place_ref[0] * HALF, LANES), HALF)]
    for b in range(2 * D // 384):
        at = slice(b * 384, (b + 1) * 384)
        own_ref[:, at] = mm(n1, dkv_ref[:, at], TN).astype(BF16)
    own_ref[:, 2 * D :] = mm(n1, dq_ref[:, :LEAD], TN).astype(BF16)


def key_own(place, n1, dq, dkv, deps):
    rows = n1.shape[0]
    return pl.pallas_call(
        after(key_own_kernel, 4, deps),
        out_shape=jax.ShapeDtypeStruct((HALF, KEY_FLOW), BF16),
        in_specs=[smem()] + [vmem()] * 3 + [anywhere()] * len(deps),
        out_specs=vmem(),
        compiler_params=params(12),
        cost_estimate=cost(2 * rows * D * D, 6 * MIB),
        name="key_own",
    )(place, n1, dq, dkv, *deps)


def input_kernel(
    core_ref, x_ref, gain_ref, gain_peer_ref, dq_ref, dkv_ref, own_ref, peer_ref, dres_ref, dx_ref, w_ref, sems
):
    copies = halves_in(own_ref, peer_ref, w_ref, sems, 0, core_ref[0])
    for copy in copies:
        copy.start()
    for copy in copies:
        copy.wait()
    gain = whole_gain(core_ref, gain_ref, gain_peer_ref)
    rows = 256
    for r in range(x_ref.shape[0] // rows):
        part = pl.ds(r * rows, rows)
        hat, inverse = normalize(x_ref[part, :].astype(F32))
        d_normed = mm(dq_ref[part, :], w_ref[:, :D], NT) + mm(dkv_ref[part, :], w_ref[:, D:], NT)
        d_hat = d_normed * gain
        back = inverse * (
            d_hat
            - jnp.mean(d_hat, axis=-1, keepdims=True)
            - hat * jnp.mean(d_hat * hat, axis=-1, keepdims=True)
        )
        dx_ref[part, :] = (dres_ref[part, :] + back).astype(BF16)


def input_grad(core, x, gain, dq, dkv, own, peer, dres, deps):
    rows = x.shape[0]
    return pl.pallas_call(
        after(input_kernel, 9, deps),
        out_shape=jax.ShapeDtypeStruct((rows, D), BF16),
        in_specs=[smem()] + [vmem()] * 5 + [in_hbm()] * 2 + [vmem()] + [anywhere()] * len(deps),
        out_specs=vmem(),
        scratch_shapes=[pltpu.VMEM((D, QKV), BF16), pltpu.SemaphoreType.DMA((2,))],
        compiler_params=params(16),
        cost_estimate=cost(2 * rows * D * QKV, 10 * MIB),
        name="input_grad",
    )(core, x, *gain, dq, dkv, own, peer, dres, *deps)


BITS = {"x": 1, "y": 2, "n": 4, "f": 8}
WIDE_ORDER = ("xy", "yx", "nf", "fn")
NARROW_ORDER = ("nf", "fn", "xy", "yx")
KEY_ORDER = ("xy", "yx", "nf", "fn")
QUERY_ORDER = ("nf", "fn", "xy", "yx")
PATTERN = (1, 1, 1, 0, 0, 0, 0)
ALL_ORDERS = WIDE_ORDER + NARROW_ORDER + QUERY_ORDER + KEY_ORDER


def trade(values, axes):
    pairs = []
    for group in range(16):
        for core in range(2):
            pairs.append((2 * group + core, 2 * (group ^ BITS[axes[core]]) + core))
    return lax.ppermute(values, ("rep", "fsdp"), pairs)


def bit_of(axes):
    step = jnp.where(lax.axis_index("fsdp") == 0, BITS[axes[0]], BITS[axes[1]])
    return (lax.axis_index("rep") // step) % 2


def advance_kernel(plan, place_ref, *refs):
    ins, outs = refs[: 2 * len(plan)], list(refs[2 * len(plan) :])
    for i, (mode, slot) in enumerate(plan):
        kept, got = ins[2 * i][...].astype(F32), ins[2 * i + 1][...].astype(F32)
        if mode == "split":
            split_rows(place_ref[slot], kept + got, slice(0, kept.shape[1]), outs.pop(0), outs.pop(0))
        elif mode == "add":
            outs.pop(0)[...] = (kept + got).astype(BF16)
        else:
            bit = place_ref[slot]
            both = [jnp.where(bit == 0, kept, got), jnp.where(bit == 0, got, kept)]
            outs.pop(0)[...] = jnp.concatenate(both, axis=0).astype(BF16)


def advance(place, flows, deps, carried):
    plan, arrays, shapes = [], [], []
    for mode, slot, kept, got in flows:
        rows, cols = kept.shape
        plan.append((mode, slot))
        arrays += [kept, got]
        sizes = {"split": [rows // 2, rows // 2], "add": [rows], "join": [2 * rows]}[mode]
        shapes += [jax.ShapeDtypeStruct((size, cols), BF16) for size in sizes]
    count, made = 1 + len(arrays), len(shapes)
    extra = tuple(carried) + tuple(deps)
    kernel = functools.partial(advance_kernel, plan)

    def body(*refs):
        outs = refs[count + len(extra) :]
        kernel(*refs[:count], *outs[:made])

    outs = pl.pallas_call(
        body,
        out_shape=tuple(shapes) + tuple(jax.ShapeDtypeStruct(a.shape, a.dtype) for a in carried),
        in_specs=[smem()] + [vmem()] * len(arrays) + [anywhere()] * len(extra),
        out_specs=(vmem(),) * made + (anywhere(),) * len(carried),
        input_output_aliases={count + i: made + i for i in range(len(carried))},
        compiler_params=params(12),
        cost_estimate=cost(MIB, 2 * MIB),
        name="advance",
    )(place, *arrays, *extra)
    return outs[:made], outs[made:]


class Chain:
    def __init__(self, place, flows):
        self.place, self.step = place, 0
        self.orders = [order for order, *_ in flows]
        self.slots = [slot for _, slot, *_ in flows]
        self.kept = [kept for *_, kept, _ in flows]
        self.exchange([send for *_, send in flows])

    def exchange(self, sends):
        axis = self.step if self.step < 4 else 7 - self.step
        self.sent = tuple(sends)
        self.got = [trade(send, order[axis]) for send, order in zip(sends, self.orders)]

    def flows(self):
        modes = [("split", self.step + 1), ("add", 0), ("join", 7 - self.step)]
        mode, bit = modes[(self.step >= 3) + (self.step > 3)]
        return [(mode, slot + bit, *pair) for slot, *pair in zip(self.slots, self.kept, self.got)]

    def take(self, parts):
        if self.step < 3:
            self.kept, sends = parts[0::2], parts[1::2]
        else:
            self.kept = sends = parts
        self.step += 1
        self.exchange(sends)

    def advance(self, deps, carried=()):
        parts, carried = advance(self.place, self.flows(), deps, carried)
        self.take(parts)
        return carried


def advance_both(one, two, deps):
    flows = one.flows()
    parts, _ = advance(one.place, flows + two.flows(), deps, ())
    count = sum(2 if mode == "split" else 1 for mode, *_ in flows)
    one.take(parts[:count])
    two.take(parts[count:])


def weighted_sum(total, weight):
    sums = jnp.sum(total * weight.astype(F32), axis=-1, keepdims=True)
    return jnp.broadcast_to(sums, (total.shape[0], LANES))


def finish_mlp_kernel(
    place_ref, mine, theirs, narrow_mine, narrow_theirs, weight_ref, in_ref, out_ref, down_ref, sum_ref
):
    rows = HALF // 2
    rest = FF // 2 - HALF
    cut = FLOW - WIDE
    bit, narrow_bit = place_ref[WIDE_SLOT], place_ref[NARROW_SLOT]
    for half in range(2):
        at = slice(half * rows, (half + 1) * rows)

        def pick(start, stop):
            cols = slice(start, stop)
            return jnp.where(bit == half, mine[:, cols].astype(F32), theirs[:, cols].astype(F32))

        def pick_narrow(start, stop):
            cols = slice(start, stop)
            return jnp.where(
                narrow_bit == half, narrow_mine[:, cols].astype(F32), narrow_theirs[:, cols].astype(F32)
            )

        total = pick(0, 2 * FF)
        in_ref[at, :] = total
        sum_ref[at, :] = weighted_sum(total, weight_ref[at, :])
        out_ref[at, :] = pick(2 * FF, WIDE)
        down_ref[at, :cut] = pick(WIDE, FLOW)
        down_ref[at, cut:] = pick_narrow(0, D - cut)
        down_ref[HALF : HALF + rest, half * HALF : (half + 1) * HALF] = pick_narrow(D - cut, FF - cut)


def mlp_outputs():
    return (
        jax.ShapeDtypeStruct((HALF, 2 * FF), F32),
        jax.ShapeDtypeStruct((HALF, D), F32),
        jax.ShapeDtypeStruct((FF // 2, D), F32),
        jax.ShapeDtypeStruct((HALF, LANES), F32),
    )


def finish_mlp(place, mine, theirs, narrow_mine, narrow_theirs, weight, deps):
    return pl.pallas_call(
        after(finish_mlp_kernel, 6, deps),
        out_shape=mlp_outputs(),
        in_specs=[smem()] + [vmem()] * 5 + [anywhere()] * len(deps),
        out_specs=(vmem(),) * 4,
        compiler_params=params(20),
        cost_estimate=cost(MIB, 10 * MIB),
        name="finish_mlp",
    )(place, mine, theirs, narrow_mine, narrow_theirs, weight, *deps)


def finish_qkv_kernel(place_ref, q_ref, q_got, kv_ref, kv_got, weight_ref, out_ref, sum_ref):
    step = out_ref.shape[0]
    half = pl.program_id(0) * step // (HALF // 2)
    at = pl.ds(pl.multiple_of(pl.program_id(0) * step - half * (HALF // 2), step), step)
    sums = jnp.zeros((step, LANES), F32)
    key_flow, query_flow = (KEY_SLOT, kv_ref, kv_got), (QUERY_SLOT, q_ref, q_got)
    pieces = ((key_flow, 2 * D, 0, LEAD), (query_flow, 0, LEAD, D - LEAD), (key_flow, 0, D, 2 * D))
    for (slot, mine, theirs), start, to, width in pieces:
        come, cols = slice(start, start + width), slice(to, to + width)
        total = jnp.where(
            place_ref[slot] == half, mine[at, come].astype(F32), theirs[at, come].astype(F32)
        )
        out_ref[:, cols] = total
        sums = sums + weighted_sum(total, weight_ref[:, cols])
    sum_ref[...] = sums


def finish_qkv(place, q_mine, q_theirs, kv_mine, kv_theirs, weight, deps):
    step = 96
    whole = lambda array: pl.BlockSpec(array.shape, lambda i: (0, 0))
    arrays = (q_mine, q_theirs, kv_mine, kv_theirs)
    return pl.pallas_call(
        after(finish_qkv_kernel, 6, deps),
        grid=(HALF // step,),
        out_shape=(jax.ShapeDtypeStruct((HALF, QKV), F32), jax.ShapeDtypeStruct((HALF, LANES), F32)),
        in_specs=[smem()] + [whole(array) for array in arrays] + [pl.BlockSpec((step, QKV), lambda i: (i, 0))]
        + [anywhere()] * len(deps),
        out_specs=(
            pl.BlockSpec((step, QKV), lambda i: (i, 0)),
            pl.BlockSpec((step, LANES), lambda i: (i, 0)),
        ),
        compiler_params=params(14),
        cost_estimate=cost(MIB, 7 * MIB),
        name="finish_qkv",
    )(place, *arrays, weight, *deps)


def add(left, right):
    return (left.astype(F32) + right.astype(F32)).astype(BF16)


def swap_cores(values):
    return lax.ppermute(values, "fsdp", [(0, 1), (1, 0)])


def layout(lengths, slot_count):
    slots = jnp.arange(slot_count, dtype=jnp.int32)
    order = jnp.arange(lengths.shape[0])
    ends = jnp.sum(jnp.where(order[None, :] <= order[:, None], lengths[None, :], 0), axis=1)
    segment = jnp.sum((slots[:, None] >= ends[None, :]).astype(jnp.int32), axis=1)
    begins = jnp.max(jnp.where(ends[None, :] <= slots[:, None], ends[None, :], 0), axis=1)
    return (segment, slots - begins)


def on_device(
    tokens, attn_gain, qkv_weight, out_weight, mlp_gain, in_weight, down_weight, seq_len, cotangent
):
    row_count = tokens.shape[0]
    core = lax.axis_index("fsdp")
    paired = lax.axis_size("rep") == 16
    bits = [bit_of(axes) if paired else 0 * core for axes in ALL_ORDERS]
    place = jnp.stack([core] + bits).astype(jnp.int32)
    peer_qkv = swap_cores(qkv_weight)
    own_gains = (attn_gain.reshape(1, HALF), mlp_gain.reshape(1, HALF))
    gain_one, gain_two = [(own, swap_cores(own)) for own in own_gains]
    peer_out = swap_cores(out_weight)
    peer_in = swap_cores(in_weight)
    peer_down = swap_cores(down_weight)
    key_seg, key_pos = layout(seq_len[0], 2 * row_count)
    own_seg = lax.dynamic_slice_in_dim(key_seg, core * row_count, row_count)
    peer_seg = lax.dynamic_slice_in_dim(key_seg, (1 - core) * row_count, row_count)
    own_pos = lax.dynamic_slice_in_dim(key_pos, core * row_count, row_count)
    lane = jnp.arange(LANES, dtype=jnp.int32) % HEAD_DIM
    half_dim = HEAD_DIM // 2
    freq = jnp.exp(-jnp.log(rope_base) * (2.0 * (lane % half_dim).astype(F32) / HEAD_DIM))
    angles = own_pos.astype(F32)[:, None] * freq[None, :]
    cosine = jnp.cos(angles)
    sine = jnp.sin(angles) * jnp.where(lane < half_dim, -1.0, 1.0)[None, :]
    marks = lane < half_dim
    mask_q = jnp.where(marks[None, :] & (own_seg[:, None] != lane[None, :]), BLOCKED, 0.0).astype(BF16)
    both_seg = jnp.concatenate([own_seg, peer_seg])
    mask_k = jnp.where(
        marks[None, :], both_seg[:, None] == lane[None, :], (lane < half_dim + 3)[None, :]
    ).astype(BF16)

    n1 = first_norm(place, tokens, gain_one)
    project_args = (place, n1, qkv_weight, peer_qkv, cosine, sine)
    kv_own = project((1, 2), 1.0, *project_args, ())
    kv_peer = swap_cores(kv_own)
    query = project((0,), HEAD_DIM**-0.5, *project_args, (kv_own,)).reshape(row_count, D)
    att, low, lse = attend(query, kv_own, kv_peer, mask_q, mask_k)
    result, n2, act, dl, dres, dproj, datt = middle(
        place, tokens, low, cotangent, gain_two,
        (out_weight, peer_out), (in_weight, peer_in), (down_weight, peer_down),
    )
    wide_for_peer = wide_peer(place, n2, dl, low, dproj)
    wide_got = swap_cores(wide_for_peer)
    narrow_for_peer, narrow_own = narrow_terms(place, act, cotangent)
    narrow_got = swap_cores(narrow_for_peer)
    back_args = (query, kv_own, kv_peer, mask_q, mask_k, datt, att, lse, cosine, sine)
    grads = attend_back(0, 1, (), (wide_for_peer, narrow_own), *back_args)
    wide_keep, wide_send, narrow_keep, narrow_send = first_sums(place, n2, dl, low, dproj, wide_got, narrow_own, narrow_got, grads[:1])

    def input_part(deps):
        return input_grad(place, tokens, gain_one, dq, dkv, qkv_weight, peer_qkv, dres, deps)

    if paired:
        mlp = Chain(
            place,
            [
                (WIDE_ORDER, WIDE_SLOT, wide_keep, wide_send),
                (NARROW_ORDER, NARROW_SLOT, narrow_keep, narrow_send),
            ],
        )
        grads = attend_back(1, 3, grads, mlp.sent, *back_args)
        mlp.advance(grads[:1])
        dq, dkv_own, dkv_peer = attend_back(4, 2, grads, mlp.sent, *back_args)
        (dkv_peer,) = mlp.advance((dq,), (dkv_peer,))
        dkv_got = swap_cores(dkv_peer)
        query_for_peer, query_own = query_terms(place, n1, dq, mlp.sent)
        key_for_peer, dkv = key_terms(place, n1, dq, dkv_own, dkv_got, cosine, sine, (query_own,))
        query_for_peer, key_for_peer = mlp.advance((dkv,), (query_for_peer, key_for_peer))
        key_got, query_got = swap_cores(key_for_peer), swap_cores(query_for_peer)
        key_mine = key_own(place, n1, dq, dkv, mlp.sent)
        grad_tokens = input_part((key_mine,))
        mlp.advance((grad_tokens,))
        (kv_keep, kv_send, q_keep, q_send), _ = advance(
            place,
            [("split", KEY_SLOT, key_mine, key_got), ("split", QUERY_SLOT, query_own, query_got)],
            mlp.sent,
            (),
        )
        qkv = Chain(
            place,
            [(KEY_ORDER, KEY_SLOT, kv_keep, kv_send), (QUERY_ORDER, QUERY_SLOT, q_keep, q_send)],
        )
        deps = ()
        for index, joint in enumerate(PATTERN):
            if joint:
                advance_both(qkv, mlp, deps)
            else:
                qkv.advance(mlp.got[1:] if index == 4 else deps)
            deps = ()
        grad_in, grad_out, grad_down, in_sums = finish_mlp(
            place, mlp.kept[0], mlp.got[0], mlp.kept[1], mlp.got[1], in_weight, qkv.sent
        )
        grad_qkv, qkv_sums = finish_qkv(
            place, qkv.kept[1], qkv.got[1], qkv.kept[0], qkv.got[0], qkv_weight, (in_sums,)
        )
    else:
        grads = attend_back(1, PAIRS - 1, grads, (), *back_args)
        dq, dkv_own, dkv_peer = grads
        query_for_peer, query_own = query_terms(place, n1, dq, ())
        key_for_peer, dkv = key_terms(place, n1, dq, dkv_own, swap_cores(dkv_peer), cosine, sine, ())
        pieces = []
        for own, for_peer in ((query_own, query_for_peer), (key_own(place, n1, dq, dkv, ()), key_for_peer)):
            total = add(own, swap_cores(for_peer))
            pieces += [total[: HALF // 2], total[HALF // 2 :]]
        grad_tokens = input_part(())
        total = lambda part: lax.psum(part.astype(F32), "rep")
        grad_qkv, qkv_sums = finish_qkv(place, *[total(part) for part in pieces], qkv_weight, ())
        grad_in, grad_out, grad_down, in_sums = finish_mlp(
            place, *[total(part) for part in (wide_keep, wide_send, narrow_keep, narrow_send)], in_weight, ()
        )
    grad_gain_one = qkv_sums[:, 0] / attn_gain.astype(F32)
    grad_gain_two = in_sums[:, 0] / mlp_gain.astype(F32)
    return (
        result,
        grad_tokens,
        grad_gain_one,
        grad_qkv,
        grad_out,
        grad_gain_two,
        grad_in,
        grad_down,
    )


def solution(mesh):
    rows = P(("rep", "fsdp"), None)
    vector, matrix = P("fsdp"), P("fsdp", None)
    in_specs = (rows, vector, matrix, matrix, vector, matrix, matrix, P("rep", None), rows)
    out_specs = (rows, rows, vector, matrix, matrix, vector, matrix, matrix)
    return jax.shard_map(
        on_device, mesh=mesh, in_specs=in_specs, out_specs=out_specs, check_vma=False
    )
```

```python
import functools

import jax
import jax.numpy as jnp
from jax import lax
from jax.experimental import pallas as pl
from jax.experimental.pallas import tpu as pltpu
from jax.sharding import PartitionSpec as P

D = 768
HEADS = 12
HEAD_DIM = 64
FF = 1152
HALF = D // 2
LANES = 128
PAIRS = D // LANES
QKV = 3 * D
WIDE = 2 * FF + D
PACK = WIDE + FF
FLOW = 3200
LEAD = 256
KEY_FLOW = 2 * D + LEAD
WIDE_SLOT, NARROW_SLOT, QUERY_SLOT, KEY_SLOT = 1, 5, 9, 13

epsilon = 1e-05
rope_base = 160000.0
BLOCKED = -(2.0**100)
F32 = jnp.float32
BF16 = jnp.bfloat16
MIB = 1 << 20

NN = (((1,), (0,)), ((), ()))
NT = (((1,), (1,)), ((), ()))
TN = (((0,), (0,)), ((), ()))


def mm(a, b, dims=NN):
    return lax.dot_general(a, b, dims, preferred_element_type=F32)


def vmem():
    return pl.BlockSpec(memory_space=pltpu.VMEM)


def anywhere():
    return pl.BlockSpec(memory_space=pl.ANY)


def in_hbm():
    return pl.BlockSpec(memory_space=pltpu.HBM)


def after(kernel, count, deps):
    def body(*refs):
        kernel(*refs[:count], *refs[count + len(deps) :])

    return body


def smem():
    return pl.BlockSpec(memory_space=pltpu.SMEM)


def params(mib):
    return pltpu.CompilerParams(vmem_limit_bytes=mib * MIB)


def cost(flops, nbytes):
    return pl.CostEstimate(flops=int(flops) >> 10, bytes_accessed=int(nbytes) >> 10, transcendentals=0)


def halves_in(own_ref, peer_ref, whole, sems, slot, core):
    rows = own_ref.shape[0]
    mine = pl.multiple_of(core * rows, 16)
    other = pl.multiple_of((1 - core) * rows, 16)
    return (
        pltpu.make_async_copy(own_ref, whole.at[pl.ds(mine, rows), :], sems.at[slot]),
        pltpu.make_async_copy(peer_ref, whole.at[pl.ds(other, rows), :], sems.at[slot + 1]),
    )


def lane_in_head(shape):
    return lax.broadcasted_iota(jnp.int32, shape, 1) % HEAD_DIM


def swap_halves(values):
    place = lane_in_head(values.shape)
    return jnp.where(
        place < HEAD_DIM // 2,
        pltpu.roll(values, LANES - HEAD_DIM // 2, 1),
        pltpu.roll(values, HEAD_DIM // 2, 1),
    )


def normalize(values):
    row_mean = jnp.mean(values, axis=-1, keepdims=True)
    centred = values - row_mean
    row_var = jnp.mean(centred * centred, axis=-1, keepdims=True)
    inverse = lax.rsqrt(row_var + epsilon)
    return centred * inverse, inverse


def whole_gain(place_ref, own_ref, peer_ref):
    own, peer = own_ref[...].astype(F32), peer_ref[...].astype(F32)
    first = place_ref[0] == 0
    return jnp.concatenate([jnp.where(first, own, peer), jnp.where(first, peer, own)], axis=1)


def norm_kernel(place_ref, x_ref, own_ref, peer_ref, n_ref):
    hat, _ = normalize(x_ref[...].astype(F32))
    n_ref[...] = (hat * whole_gain(place_ref, own_ref, peer_ref)).astype(BF16)


def first_norm(place, x, gain):
    rows = 128
    block = pl.BlockSpec((rows, D), lambda i: (i, 0))
    return pl.pallas_call(
        norm_kernel,
        grid=(x.shape[0] // rows,),
        out_shape=jax.ShapeDtypeStruct(x.shape, BF16),
        in_specs=[smem(), block] + [pl.BlockSpec((1, HALF), lambda i: (0, 0))] * 2,
        out_specs=block,
        compiler_params=params(8),
        cost_estimate=cost(MIB, 2 * MIB),
        name="first_norm",
    )(place, x, *gain)


def project_kernel(parts, scale, place_ref, n_ref, own_ref, peer_ref, cos_ref, sin_ref, out_ref):
    core = place_ref[0]
    mine = pl.ds(pl.multiple_of(core * HALF, LANES), HALF)
    other = pl.ds(pl.multiple_of((1 - core) * HALF, LANES), HALF)
    rows = 256
    for r in range(n_ref.shape[0] // rows):
        part = pl.ds(r * rows, rows)
        left, right = n_ref[part, mine], n_ref[part, other]
        cosine, sine = cos_ref[part, :], sin_ref[part, :]
        for i, which in enumerate(parts):
            for half in range(2):
                at = slice(which * D + half * HALF, which * D + (half + 1) * HALF)
                out = mm(left, own_ref[:, at]) + mm(right, peer_ref[:, at])
                for tile in range(HALF // LANES):
                    piece = out[:, tile * LANES : (tile + 1) * LANES]
                    if which < 2:
                        piece = piece * cosine + swap_halves(piece) * sine
                    cols = pl.ds(half * HALF + tile * LANES, LANES)
                    out_ref[i, part, cols] = (piece * scale).astype(BF16)


def project(parts, scale, place, normed, own, peer, cosine, sine, deps):
    rows = normed.shape[0]
    return pl.pallas_call(
        after(functools.partial(project_kernel, parts, scale), 6, deps),
        out_shape=jax.ShapeDtypeStruct((len(parts), rows, D), BF16),
        in_specs=[smem()] + [vmem()] * 5 + [anywhere()] * len(deps),
        out_specs=vmem(),
        compiler_params=params(12),
        cost_estimate=cost(2 * rows * D * D * len(parts), 8 * MIB),
        name="project",
    )(place, normed, own, peer, cosine, sine, *deps)


def attend_kernel(q_ref, ko_ref, vo_ref, kp_ref, vp_ref, mq_ref, mk_ref, att_ref, low_ref, lse_ref):
    rows = q_ref.shape[0]
    tile = min(512, rows)
    keys = jnp.concatenate([ko_ref[0], kp_ref[0]], axis=0)
    values = jnp.concatenate([vo_ref[0], vp_ref[0]], axis=0)
    key_first = lax.broadcasted_iota(jnp.int32, keys.shape, 1) < HEAD_DIM
    one = jnp.ones_like(values)
    mask_keys = mk_ref[...]
    k_both = (jnp.where(key_first, keys, mask_keys), jnp.where(key_first, mask_keys, keys))
    v_both = (jnp.where(key_first, values, one), jnp.where(key_first, one, values))
    first = lax.broadcasted_iota(jnp.int32, (tile, LANES), 1) < HEAD_DIM
    for t in range(rows // tile):
        part = pl.ds(t * tile, tile)
        query, mask_q = q_ref[part, :], mq_ref[part, :]
        sides = (first, jnp.logical_not(first))
        scores = [mm(jnp.where(sides[head], query, mask_q), k_both[head], NT) for head in range(2)]
        peaks = [jnp.max(raw, axis=-1, keepdims=True) for raw in scores]
        sums = []
        for head in range(2):
            weights = jnp.exp(scores[head] - peaks[head]).astype(BF16)
            sums.append(mm(weights, v_both[head]))
        numer = jnp.where(first, sums[0], sums[1])
        denom = jnp.where(first, pltpu.roll(sums[0], HEAD_DIM, 1), pltpu.roll(sums[1], HEAD_DIM, 1))
        out = numer / denom
        att_ref[part, :] = out
        low_ref[part, :] = out.astype(BF16)
        lse_ref[part, :] = jnp.where(first, peaks[0], peaks[1]) + jnp.log(denom)


def kv_specs(rows):
    return [
        pl.BlockSpec((1, rows, LANES), lambda i: (0, 0, i)),
        pl.BlockSpec((1, rows, LANES), lambda i: (1, 0, i)),
    ]


def attend(query, kv_own, kv_peer, mask_q, mask_k):
    rows = query.shape[0]
    keys = mask_k.shape[0]
    pair = pl.BlockSpec((rows, LANES), lambda i: (0, i))
    whole = lambda n: pl.BlockSpec((n, LANES), lambda i: (0, 0))
    return pl.pallas_call(
        attend_kernel,
        grid=(PAIRS,),
        out_shape=(
            jax.ShapeDtypeStruct((rows, D), F32),
            jax.ShapeDtypeStruct((rows, D), BF16),
            jax.ShapeDtypeStruct((rows, D), F32),
        ),
        in_specs=[pair] + kv_specs(rows) + kv_specs(rows) + [whole(rows), whole(keys)],
        out_specs=(pair, pair, pair),
        compiler_params=params(16),
        cost_estimate=cost(16 * rows * keys * D, 8 * MIB),
        name="attend",
    )(query, kv_own, kv_own, kv_peer, kv_peer, mask_q, mask_k)


def middle_kernel(
    core_ref, x_ref, low_ref, dy_ref, gain_ref, gain_peer_ref,
    oo_ref, op_ref, io_ref, ip_ref, do_ref, dp_ref,
    result_ref, n2_ref, act_ref, dl_ref, dres_ref, dproj_ref, datt_ref,
    wo_ref, wi_ref, wd_ref, sems,
):
    core = core_ref[0]
    copies = (
        halves_in(oo_ref, op_ref, wo_ref, sems, 0, core),
        halves_in(io_ref, ip_ref, wi_ref, sems, 2, core),
        halves_in(do_ref, dp_ref, wd_ref, sems, 4, core),
    )
    for pair in copies:
        for copy in pair:
            copy.start()

    def arrived(which):
        for copy in copies[which]:
            copy.wait()

    gain = whole_gain(core_ref, gain_ref, gain_peer_ref)
    rows = 256
    block = 384
    for r in range(x_ref.shape[0] // rows):
        part = pl.ds(r * rows, rows)
        if r == 0:
            arrived(0)
        resid = x_ref[part, :].astype(F32) + mm(low_ref[part, :], wo_ref[...])
        hat, inverse = normalize(resid)
        n2 = (hat * gain).astype(BF16)
        n2_ref[part, :] = n2
        dy = dy_ref[part, :]
        if r == 0:
            arrived(1)
            arrived(2)
        for b in range(FF // block):
            cols = slice(b * block, (b + 1) * block)
            gate_cols = slice(FF + b * block, FF + (b + 1) * block)
            lift = mm(n2, wi_ref[:, cols])
            gate = mm(n2, wi_ref[:, gate_cols])
            d_act = mm(dy, wd_ref[cols, :], NT)
            cdf = 0.5 + 0.5 * lax.erf(lift * (0.5**0.5))
            bell = jnp.exp(-0.5 * lift * lift) * 0.3989422804014327
            gelu = lift * cdf
            act_ref[part, cols] = (gelu * gate).astype(BF16)
            dl_ref[part, cols] = (d_act * gate * (cdf + lift * bell)).astype(BF16)
            dl_ref[part, gate_cols] = (d_act * gelu).astype(BF16)
        result_ref[part, :] = (resid + mm(act_ref[part, :], wd_ref[...])).astype(BF16)
        d_normed = mm(dl_ref[part, :], wi_ref[...], NT)
        d_hat = d_normed * gain
        d_resid = dy.astype(F32) + inverse * (
            d_hat
            - jnp.mean(d_hat, axis=-1, keepdims=True)
            - hat * jnp.mean(d_hat * hat, axis=-1, keepdims=True)
        )
        dres_ref[part, :] = d_resid
        d_proj = d_resid.astype(BF16)
        dproj_ref[part, :] = d_proj
        datt_ref[part, :] = mm(d_proj, wo_ref[...], NT).astype(BF16)


def middle(core, x, low, dy, gain, w_out, w_in, w_down):
    rows = x.shape[0]
    low_shape = lambda n: jax.ShapeDtypeStruct((rows, n), BF16)
    return pl.pallas_call(
        middle_kernel,
        out_shape=(
            low_shape(D), low_shape(D), low_shape(FF), low_shape(2 * FF),
            jax.ShapeDtypeStruct((rows, D), F32), low_shape(D), low_shape(D),
        ),
        in_specs=[smem()] + [vmem()] * 5 + [in_hbm()] * 6,
        out_specs=(vmem(),) * 7,
        scratch_shapes=[
            pltpu.VMEM((D, D), BF16),
            pltpu.VMEM((D, 2 * FF), BF16),
            pltpu.VMEM((FF, D), BF16),
            pltpu.SemaphoreType.DMA((6,)),
        ],
        compiler_params=params(32),
        cost_estimate=cost(2 * rows * D * (2 * D + 6 * FF), 16 * MIB),
        name="middle",
    )(core, x, low, dy, *gain, *w_out, *w_in, *w_down)


def fold_down(ref, block):
    rest = block.shape[0] - HALF
    ref[:, :D] = block[:HALF]
    ref[0:rest, D:FF] = block[HALF:, :HALF]
    ref[rest : 2 * rest, D:FF] = block[HALF:, HALF:]


def narrow_kernel(core_ref, act_ref, dy_ref, peer_ref, own_ref, whole):
    core = core_ref[0]
    for b in range(FF // 384):
        rows = slice(b * 384, (b + 1) * 384)
        whole[rows, :] = mm(act_ref[:, rows], dy_ref[...], TN).astype(BF16)
    size = FF // 2
    for ref, side in ((peer_ref, 1 - core), (own_ref, core)):
        fold_down(ref, whole[pl.ds(pl.multiple_of(side * size, 16), size), :])


def narrow_terms(core, act, dy):
    rows = act.shape[0]
    half = jax.ShapeDtypeStruct((HALF, FF), BF16)
    return pl.pallas_call(
        narrow_kernel,
        out_shape=(half, half),
        in_specs=[smem()] + [vmem()] * 2,
        out_specs=(vmem(), vmem()),
        scratch_shapes=[pltpu.VMEM((FF, D), BF16)],
        compiler_params=params(14),
        cost_estimate=cost(2 * rows * D * FF, 8 * MIB),
        name="narrow_terms",
    )(core, act, dy)


def wide_block(side, n2_ref, dl_ref, low_ref, dproj_ref, store):
    cols = pl.ds(pl.multiple_of(side * HALF, LANES), HALF)
    n2 = n2_ref[:, cols]
    for b in range(2 * FF // 384):
        at = slice(b * 384, (b + 1) * 384)
        store(at, mm(n2, dl_ref[:, at], TN))
    store(slice(2 * FF, WIDE), mm(low_ref[:, cols], dproj_ref[...], TN))


def wide_peer_kernel(core_ref, n2_ref, dl_ref, low_ref, dproj_ref, peer_ref):
    def store(at, block):
        peer_ref[:, at] = block.astype(BF16)

    wide_block(1 - core_ref[0], n2_ref, dl_ref, low_ref, dproj_ref, store)


def wide_peer(core, n2, dl, low, dproj):
    rows = n2.shape[0]
    return pl.pallas_call(
        wide_peer_kernel,
        out_shape=jax.ShapeDtypeStruct((HALF, WIDE), BF16),
        in_specs=[smem()] + [vmem()] * 4,
        out_specs=vmem(),
        compiler_params=params(14),
        cost_estimate=cost(2 * rows * HALF * WIDE, 6 * MIB),
        name="wide_peer",
    )(core, n2, dl, low, dproj)


def split_rows(bit, block, at, keep_ref, send_ref):
    rows = block.shape[0] // 2
    keep_ref[:, at] = jnp.where(bit == 0, block[:rows], block[rows:]).astype(BF16)
    send_ref[:, at] = jnp.where(bit == 0, block[rows:], block[:rows]).astype(BF16)


def first_kernel(
    place_ref, n2_ref, dl_ref, low_ref, dproj_ref, got_ref, down_ref, down_got_ref,
    keep_ref, send_ref, narrow_keep, narrow_send,
):
    def store(at, block):
        split_rows(place_ref[WIDE_SLOT], block + got_ref[:, at].astype(F32), at, keep_ref, send_ref)

    wide_block(place_ref[0], n2_ref, dl_ref, low_ref, dproj_ref, store)
    total = down_ref[...].astype(F32) + down_got_ref[...].astype(F32)
    cut = FLOW - WIDE
    split_rows(place_ref[WIDE_SLOT], total[:, :cut], slice(WIDE, FLOW), keep_ref, send_ref)
    split_rows(place_ref[NARROW_SLOT], total[:, cut:], slice(0, PACK - FLOW), narrow_keep, narrow_send)


def first_sums(place, n2, dl, low, dproj, got, down, down_got, deps):
    rows = n2.shape[0]
    half = jax.ShapeDtypeStruct((HALF // 2, FLOW), BF16)
    narrow = jax.ShapeDtypeStruct((HALF // 2, PACK - FLOW), BF16)
    return pl.pallas_call(
        after(first_kernel, 8, deps),
        out_shape=(half, half, narrow, narrow),
        in_specs=[smem()] + [vmem()] * 7 + [anywhere()] * len(deps),
        out_specs=(vmem(),) * 4,
        compiler_params=params(16),
        cost_estimate=cost(2 * rows * HALF * WIDE, 8 * MIB),
        name="first_sums",
    )(place, n2, dl, low, dproj, got, down, down_got, *deps)


def split_three(values):
    high = values.astype(BF16)
    rest = values - high.astype(F32)
    mid = rest.astype(BF16)
    return high, mid, (rest - mid.astype(F32)).astype(BF16)


def place_three(values, place, others):
    high, mid, tail = split_three(-values)
    at = HEAD_DIM // 2
    out = jnp.where(place == at, high.astype(F32), others)
    out = jnp.where(place == at + 1, mid.astype(F32), out)
    return jnp.where(place == at + 2, tail.astype(F32), out)


def attend_back_kernel(
    q_ref, ko_ref, vo_ref, kp_ref, vp_ref, mq_ref, mk_ref, do_ref, att_ref, lse_ref, cos_ref, sin_ref,
    dq_ref, own_ref, peer_ref,
):
    rows = q_ref.shape[0]
    tile = min(512, rows)
    query, grad = q_ref[...], do_ref[...]
    place = lane_in_head(query.shape)
    first = lax.broadcasted_iota(jnp.int32, query.shape, 1) < HEAD_DIM
    tile_first = first[:tile]
    product = grad.astype(F32) * att_ref[...]
    lse = pltpu.roll(lse_ref[...], HEAD_DIM, 1)
    mask_q = mq_ref[...].astype(F32)
    zero = jnp.zeros_like(mask_q)
    q_both, g_both = [], []
    for head in range(2):
        side = first if head == 0 else jnp.logical_not(first)
        delta = jnp.sum(jnp.where(side, product, 0.0), axis=-1, keepdims=True)
        q_both.append(jnp.where(side, query, place_three(lse, place, mask_q).astype(BF16)))
        wide = jnp.broadcast_to(delta, product.shape)
        g_both.append(jnp.where(side, grad, place_three(wide, place, zero).astype(BF16)))
    d_query = [jnp.zeros((LANES, rows), F32) for _ in range(2)]
    for source in range(2):
        k_ref, v_ref, out_ref = ((ko_ref, vo_ref, own_ref), (kp_ref, vp_ref, peer_ref))[source]
        for t in range(rows // tile):
            part = pl.ds(t * tile, tile)
            keys, values = k_ref[0, part, :], v_ref[0, part, :]
            keys_across = keys.T
            marks = mk_ref[pl.ds(source * rows + t * tile, tile), :]
            d_keys, d_values = [], []
            for head in range(2):
                side = tile_first if head == 0 else jnp.logical_not(tile_first)
                probs = jnp.exp(mm(jnp.where(side, keys, marks), q_both[head], NT))
                d_probs = mm(jnp.where(side, values, marks), g_both[head], NT)
                d_scores = (probs * d_probs).astype(BF16)
                d_values.append(mm(probs.astype(BF16), grad))
                d_keys.append(mm(d_scores, query))
                d_query[head] = d_query[head] + mm(keys_across, d_scores)
            out_ref[0, part, :] = jnp.where(tile_first, d_keys[0], d_keys[1]).astype(BF16)
            out_ref[1, part, :] = jnp.where(tile_first, d_values[0], d_values[1]).astype(BF16)
    d_q = jnp.concatenate([d_query[0][:HEAD_DIM], d_query[1][HEAD_DIM:]], axis=0).T * HEAD_DIM**-0.5
    dq_ref[...] = (d_q * cos_ref[...] - swap_halves(d_q) * sin_ref[...]).astype(BF16)


def attend_back(first, count, so_far, deps, query, kv_own, kv_peer, mask_q, mask_k, grad, att, lse, cosine, sine):
    rows = query.shape[0]
    keys = mask_k.shape[0]
    pair = pl.BlockSpec((rows, LANES), lambda i: (0, first + i))
    both = pl.BlockSpec((2, rows, LANES), lambda i: (0, 0, first + i))
    whole = lambda n: pl.BlockSpec((n, LANES), lambda i: (0, 0))
    kv = [
        pl.BlockSpec((1, rows, LANES), lambda i: (0, 0, first + i)),
        pl.BlockSpec((1, rows, LANES), lambda i: (1, 0, first + i)),
    ]
    extra = tuple(so_far) + tuple(deps)
    return pl.pallas_call(
        after(attend_back_kernel, 12, extra),
        grid=(count,),
        out_shape=(
            jax.ShapeDtypeStruct((rows, D), BF16),
            jax.ShapeDtypeStruct((2, rows, D), BF16),
            jax.ShapeDtypeStruct((2, rows, D), BF16),
        ),
        in_specs=[pair] + kv + kv
        + [whole(rows), whole(keys), pair, pair, pair, whole(rows), whole(rows)]
        + [anywhere()] * len(extra),
        out_specs=(pair, both, both),
        input_output_aliases={12 + i: i for i in range(len(so_far))},
        compiler_params=params(18),
        cost_estimate=cost(40 * rows * keys * LANES * count, 2 * MIB * count),
        name="attend_back",
    )(query, kv_own, kv_own, kv_peer, kv_peer, mask_q, mask_k, grad, att, lse, cosine, sine, *extra)


def query_terms_kernel(core_ref, n1_ref, dq_ref, peer_ref, own_ref):
    for ref, side in ((peer_ref, 1 - core_ref[0]), (own_ref, core_ref[0])):
        cols = pl.ds(pl.multiple_of(side * HALF, LANES), HALF)
        ref[...] = mm(n1_ref[:, cols], dq_ref[:, LEAD:], TN).astype(BF16)


def query_terms(core, n1, dq, deps):
    rows = n1.shape[0]
    half = jax.ShapeDtypeStruct((HALF, D - LEAD), BF16)
    return pl.pallas_call(
        after(query_terms_kernel, 3, deps),
        out_shape=(half, half),
        in_specs=[smem()] + [vmem()] * 2 + [anywhere()] * len(deps),
        out_specs=(vmem(), vmem()),
        compiler_params=params(12),
        cost_estimate=cost(2 * rows * D * D, 3 * MIB),
        name="query_terms",
    )(core, n1, dq, *deps)


def key_terms_kernel(core_ref, n1_ref, dq_ref, own_ref, got_ref, cos_ref, sin_ref, peer_ref, dkv_ref):
    cosine, sine = cos_ref[...], sin_ref[...]
    cols = pl.ds(pl.multiple_of((1 - core_ref[0]) * HALF, LANES), HALF)
    n1 = n1_ref[:, cols]
    for pair in range(PAIRS):
        at = slice(pair * LANES, (pair + 1) * LANES)
        d_key = own_ref[0, :, at].astype(F32) + got_ref[0, :, at].astype(F32)
        d_value = own_ref[1, :, at].astype(F32) + got_ref[1, :, at].astype(F32)
        d_key = d_key * cosine - swap_halves(d_key) * sine
        dkv_ref[:, at] = d_key.astype(BF16)
        dkv_ref[:, D + pair * LANES : D + (pair + 1) * LANES] = d_value.astype(BF16)
    for b in range(2 * D // 384):
        at = slice(b * 384, (b + 1) * 384)
        peer_ref[:, at] = mm(n1, dkv_ref[:, at], TN).astype(BF16)
    peer_ref[:, 2 * D :] = mm(n1, dq_ref[:, :LEAD], TN).astype(BF16)


def key_terms(core, n1, dq, own, got, cosine, sine, deps):
    rows = n1.shape[0]
    return pl.pallas_call(
        after(key_terms_kernel, 7, deps),
        out_shape=(jax.ShapeDtypeStruct((HALF, KEY_FLOW), BF16), jax.ShapeDtypeStruct((rows, 2 * D), BF16)),
        in_specs=[smem()] + [vmem()] * 6 + [anywhere()] * len(deps),
        out_specs=(vmem(), vmem()),
        compiler_params=params(16),
        cost_estimate=cost(2 * rows * D * D, 6 * MIB),
        name="key_terms",
    )(core, n1, dq, own, got, cosine, sine, *deps)


def key_own_kernel(place_ref, n1_ref, dq_ref, dkv_ref, own_ref):
    n1 = n1_ref[:, pl.ds(pl.multiple_of(place_ref[0] * HALF, LANES), HALF)]
    for b in range(2 * D // 384):
        at = slice(b * 384, (b + 1) * 384)
        own_ref[:, at] = mm(n1, dkv_ref[:, at], TN).astype(BF16)
    own_ref[:, 2 * D :] = mm(n1, dq_ref[:, :LEAD], TN).astype(BF16)


def key_own(place, n1, dq, dkv, deps):
    rows = n1.shape[0]
    return pl.pallas_call(
        after(key_own_kernel, 4, deps),
        out_shape=jax.ShapeDtypeStruct((HALF, KEY_FLOW), BF16),
        in_specs=[smem()] + [vmem()] * 3 + [anywhere()] * len(deps),
        out_specs=vmem(),
        compiler_params=params(12),
        cost_estimate=cost(2 * rows * D * D, 6 * MIB),
        name="key_own",
    )(place, n1, dq, dkv, *deps)


def input_kernel(
    core_ref, x_ref, gain_ref, gain_peer_ref, dq_ref, dkv_ref, own_ref, peer_ref, dres_ref, dx_ref, w_ref, sems
):
    copies = halves_in(own_ref, peer_ref, w_ref, sems, 0, core_ref[0])
    for copy in copies:
        copy.start()
    for copy in copies:
        copy.wait()
    gain = whole_gain(core_ref, gain_ref, gain_peer_ref)
    rows = 256
    for r in range(x_ref.shape[0] // rows):
        part = pl.ds(r * rows, rows)
        hat, inverse = normalize(x_ref[part, :].astype(F32))
        d_normed = mm(dq_ref[part, :], w_ref[:, :D], NT) + mm(dkv_ref[part, :], w_ref[:, D:], NT)
        d_hat = d_normed * gain
        back = inverse * (
            d_hat
            - jnp.mean(d_hat, axis=-1, keepdims=True)
            - hat * jnp.mean(d_hat * hat, axis=-1, keepdims=True)
        )
        dx_ref[part, :] = (dres_ref[part, :] + back).astype(BF16)


def input_grad(core, x, gain, dq, dkv, own, peer, dres, deps):
    rows = x.shape[0]
    return pl.pallas_call(
        after(input_kernel, 9, deps),
        out_shape=jax.ShapeDtypeStruct((rows, D), BF16),
        in_specs=[smem()] + [vmem()] * 5 + [in_hbm()] * 2 + [vmem()] + [anywhere()] * len(deps),
        out_specs=vmem(),
        scratch_shapes=[pltpu.VMEM((D, QKV), BF16), pltpu.SemaphoreType.DMA((2,))],
        compiler_params=params(16),
        cost_estimate=cost(2 * rows * D * QKV, 10 * MIB),
        name="input_grad",
    )(core, x, *gain, dq, dkv, own, peer, dres, *deps)


BITS = {"x": 1, "y": 2, "n": 4, "f": 8}
WIDE_ORDER = ("xy", "yx", "nf", "fn")
NARROW_ORDER = ("nf", "fn", "xy", "yx")
KEY_ORDER = ("xy", "yx", "nf", "fn")
QUERY_ORDER = ("nf", "fn", "xy", "yx")
PATTERN = (1, 1, 1, 0, 0, 0, 0)
ALL_ORDERS = WIDE_ORDER + NARROW_ORDER + QUERY_ORDER + KEY_ORDER


def trade(values, axes):
    pairs = []
    for group in range(16):
        for core in range(2):
            pairs.append((2 * group + core, 2 * (group ^ BITS[axes[core]]) + core))
    return lax.ppermute(values, ("rep", "fsdp"), pairs)


def bit_of(axes):
    step = jnp.where(lax.axis_index("fsdp") == 0, BITS[axes[0]], BITS[axes[1]])
    return (lax.axis_index("rep") // step) % 2


def advance_kernel(plan, place_ref, *refs):
    ins, outs = refs[: 2 * len(plan)], list(refs[2 * len(plan) :])
    for i, (mode, slot) in enumerate(plan):
        kept, got = ins[2 * i][...].astype(F32), ins[2 * i + 1][...].astype(F32)
        if mode == "split":
            split_rows(place_ref[slot], kept + got, slice(0, kept.shape[1]), outs.pop(0), outs.pop(0))
        elif mode == "add":
            outs.pop(0)[...] = (kept + got).astype(BF16)
        else:
            bit = place_ref[slot]
            both = [jnp.where(bit == 0, kept, got), jnp.where(bit == 0, got, kept)]
            outs.pop(0)[...] = jnp.concatenate(both, axis=0).astype(BF16)


def advance(place, flows, deps, carried):
    plan, arrays, shapes = [], [], []
    for mode, slot, kept, got in flows:
        rows, cols = kept.shape
        plan.append((mode, slot))
        arrays += [kept, got]
        sizes = {"split": [rows // 2, rows // 2], "add": [rows], "join": [2 * rows]}[mode]
        shapes += [jax.ShapeDtypeStruct((size, cols), BF16) for size in sizes]
    count, made = 1 + len(arrays), len(shapes)
    extra = tuple(carried) + tuple(deps)
    kernel = functools.partial(advance_kernel, plan)

    def body(*refs):
        outs = refs[count + len(extra) :]
        kernel(*refs[:count], *outs[:made])

    outs = pl.pallas_call(
        body,
        out_shape=tuple(shapes) + tuple(jax.ShapeDtypeStruct(a.shape, a.dtype) for a in carried),
        in_specs=[smem()] + [vmem()] * len(arrays) + [anywhere()] * len(extra),
        out_specs=(vmem(),) * made + (anywhere(),) * len(carried),
        input_output_aliases={count + i: made + i for i in range(len(carried))},
        compiler_params=params(12),
        cost_estimate=cost(MIB, 2 * MIB),
        name="advance",
    )(place, *arrays, *extra)
    return outs[:made], outs[made:]


class Chain:
    def __init__(self, place, flows):
        self.place, self.step = place, 0
        self.orders = [order for order, *_ in flows]
        self.slots = [slot for _, slot, *_ in flows]
        self.kept = [kept for *_, kept, _ in flows]
        self.exchange([send for *_, send in flows])

    def exchange(self, sends):
        axis = self.step if self.step < 4 else 7 - self.step
        self.sent = tuple(sends)
        self.got = [trade(send, order[axis]) for send, order in zip(sends, self.orders)]

    def flows(self):
        modes = [("split", self.step + 1), ("add", 0), ("join", 7 - self.step)]
        mode, bit = modes[(self.step >= 3) + (self.step > 3)]
        return [(mode, slot + bit, *pair) for slot, *pair in zip(self.slots, self.kept, self.got)]

    def take(self, parts):
        if self.step < 3:
            self.kept, sends = parts[0::2], parts[1::2]
        else:
            self.kept = sends = parts
        self.step += 1
        self.exchange(sends)

    def advance(self, deps, carried=()):
        parts, carried = advance(self.place, self.flows(), deps, carried)
        self.take(parts)
        return carried


def advance_both(one, two, deps):
    flows = one.flows()
    parts, _ = advance(one.place, flows + two.flows(), deps, ())
    count = sum(2 if mode == "split" else 1 for mode, *_ in flows)
    one.take(parts[:count])
    two.take(parts[count:])


def weighted_sum(total, weight):
    sums = jnp.sum(total * weight.astype(F32), axis=-1, keepdims=True)
    return jnp.broadcast_to(sums, (total.shape[0], LANES))


def finish_mlp_kernel(
    place_ref, mine, theirs, narrow_mine, narrow_theirs, weight_ref, in_ref, out_ref, down_ref, sum_ref
):
    rows = HALF // 2
    rest = FF // 2 - HALF
    cut = FLOW - WIDE
    bit, narrow_bit = place_ref[WIDE_SLOT], place_ref[NARROW_SLOT]
    for half in range(2):
        at = slice(half * rows, (half + 1) * rows)

        def pick(start, stop):
            cols = slice(start, stop)
            return jnp.where(bit == half, mine[:, cols].astype(F32), theirs[:, cols].astype(F32))

        def pick_narrow(start, stop):
            cols = slice(start, stop)
            return jnp.where(
                narrow_bit == half, narrow_mine[:, cols].astype(F32), narrow_theirs[:, cols].astype(F32)
            )

        total = pick(0, 2 * FF)
        in_ref[at, :] = total
        sum_ref[at, :] = weighted_sum(total, weight_ref[at, :])
        out_ref[at, :] = pick(2 * FF, WIDE)
        down_ref[at, :cut] = pick(WIDE, FLOW)
        down_ref[at, cut:] = pick_narrow(0, D - cut)
        down_ref[HALF : HALF + rest, half * HALF : (half + 1) * HALF] = pick_narrow(D - cut, FF - cut)


def mlp_outputs():
    return (
        jax.ShapeDtypeStruct((HALF, 2 * FF), F32),
        jax.ShapeDtypeStruct((HALF, D), F32),
        jax.ShapeDtypeStruct((FF // 2, D), F32),
        jax.ShapeDtypeStruct((HALF, LANES), F32),
    )


def finish_mlp(place, mine, theirs, narrow_mine, narrow_theirs, weight, deps):
    return pl.pallas_call(
        after(finish_mlp_kernel, 6, deps),
        out_shape=mlp_outputs(),
        in_specs=[smem()] + [vmem()] * 5 + [anywhere()] * len(deps),
        out_specs=(vmem(),) * 4,
        compiler_params=params(20),
        cost_estimate=cost(MIB, 10 * MIB),
        name="finish_mlp",
    )(place, mine, theirs, narrow_mine, narrow_theirs, weight, *deps)


def finish_qkv_kernel(place_ref, q_ref, q_got, kv_ref, kv_got, weight_ref, out_ref, sum_ref):
    step = out_ref.shape[0]
    half = pl.program_id(0) * step // (HALF // 2)
    at = pl.ds(pl.multiple_of(pl.program_id(0) * step - half * (HALF // 2), step), step)
    sums = jnp.zeros((step, LANES), F32)
    key_flow, query_flow = (KEY_SLOT, kv_ref, kv_got), (QUERY_SLOT, q_ref, q_got)
    pieces = ((key_flow, 2 * D, 0, LEAD), (query_flow, 0, LEAD, D - LEAD), (key_flow, 0, D, 2 * D))
    for (slot, mine, theirs), start, to, width in pieces:
        come, cols = slice(start, start + width), slice(to, to + width)
        total = jnp.where(
            place_ref[slot] == half, mine[at, come].astype(F32), theirs[at, come].astype(F32)
        )
        out_ref[:, cols] = total
        sums = sums + weighted_sum(total, weight_ref[:, cols])
    sum_ref[...] = sums


def finish_qkv(place, q_mine, q_theirs, kv_mine, kv_theirs, weight, deps):
    step = 96
    whole = lambda array: pl.BlockSpec(array.shape, lambda i: (0, 0))
    arrays = (q_mine, q_theirs, kv_mine, kv_theirs)
    return pl.pallas_call(
        after(finish_qkv_kernel, 6, deps),
        grid=(HALF // step,),
        out_shape=(jax.ShapeDtypeStruct((HALF, QKV), F32), jax.ShapeDtypeStruct((HALF, LANES), F32)),
        in_specs=[smem()] + [whole(array) for array in arrays] + [pl.BlockSpec((step, QKV), lambda i: (i, 0))]
        + [anywhere()] * len(deps),
        out_specs=(
            pl.BlockSpec((step, QKV), lambda i: (i, 0)),
            pl.BlockSpec((step, LANES), lambda i: (i, 0)),
        ),
        compiler_params=params(14),
        cost_estimate=cost(MIB, 7 * MIB),
        name="finish_qkv",
    )(place, *arrays, weight, *deps)


def add(left, right):
    return (left.astype(F32) + right.astype(F32)).astype(BF16)


def swap_cores(values):
    return lax.ppermute(values, "fsdp", [(0, 1), (1, 0)])


def layout(lengths, slot_count):
    slots = jnp.arange(slot_count, dtype=jnp.int32)
    order = jnp.arange(lengths.shape[0])
    ends = jnp.sum(jnp.where(order[None, :] <= order[:, None], lengths[None, :], 0), axis=1)
    segment = jnp.sum((slots[:, None] >= ends[None, :]).astype(jnp.int32), axis=1)
    begins = jnp.max(jnp.where(ends[None, :] <= slots[:, None], ends[None, :], 0), axis=1)
    return (segment, slots - begins)


def on_device(
    tokens, attn_gain, qkv_weight, out_weight, mlp_gain, in_weight, down_weight, seq_len, cotangent
):
    row_count = tokens.shape[0]
    core = lax.axis_index("fsdp")
    paired = lax.axis_size("rep") == 16
    bits = [bit_of(axes) if paired else 0 * core for axes in ALL_ORDERS]
    place = jnp.stack([core] + bits).astype(jnp.int32)
    peer_qkv = swap_cores(qkv_weight)
    own_gains = (attn_gain.reshape(1, HALF), mlp_gain.reshape(1, HALF))
    gain_one, gain_two = [(own, swap_cores(own)) for own in own_gains]
    peer_out = swap_cores(out_weight)
    peer_in = swap_cores(in_weight)
    peer_down = swap_cores(down_weight)
    key_seg, key_pos = layout(seq_len[0], 2 * row_count)
    own_seg = lax.dynamic_slice_in_dim(key_seg, core * row_count, row_count)
    peer_seg = lax.dynamic_slice_in_dim(key_seg, (1 - core) * row_count, row_count)
    own_pos = lax.dynamic_slice_in_dim(key_pos, core * row_count, row_count)
    lane = jnp.arange(LANES, dtype=jnp.int32) % HEAD_DIM
    half_dim = HEAD_DIM // 2
    freq = jnp.exp(-jnp.log(rope_base) * (2.0 * (lane % half_dim).astype(F32) / HEAD_DIM))
    angles = own_pos.astype(F32)[:, None] * freq[None, :]
    cosine = jnp.cos(angles)
    sine = jnp.sin(angles) * jnp.where(lane < half_dim, -1.0, 1.0)[None, :]
    marks = lane < half_dim
    mask_q = jnp.where(marks[None, :] & (own_seg[:, None] != lane[None, :]), BLOCKED, 0.0).astype(BF16)
    both_seg = jnp.concatenate([own_seg, peer_seg])
    mask_k = jnp.where(
        marks[None, :], both_seg[:, None] == lane[None, :], (lane < half_dim + 3)[None, :]
    ).astype(BF16)

    n1 = first_norm(place, tokens, gain_one)
    project_args = (place, n1, qkv_weight, peer_qkv, cosine, sine)
    kv_own = project((1, 2), 1.0, *project_args, ())
    kv_peer = swap_cores(kv_own)
    query = project((0,), HEAD_DIM**-0.5, *project_args, (kv_own,)).reshape(row_count, D)
    att, low, lse = attend(query, kv_own, kv_peer, mask_q, mask_k)
    result, n2, act, dl, dres, dproj, datt = middle(
        place, tokens, low, cotangent, gain_two,
        (out_weight, peer_out), (in_weight, peer_in), (down_weight, peer_down),
    )
    wide_for_peer = wide_peer(place, n2, dl, low, dproj)
    wide_got = swap_cores(wide_for_peer)
    narrow_for_peer, narrow_own = narrow_terms(place, act, cotangent)
    narrow_got = swap_cores(narrow_for_peer)
    back_args = (query, kv_own, kv_peer, mask_q, mask_k, datt, att, lse, cosine, sine)
    grads = attend_back(0, 1, (), (wide_for_peer, narrow_own), *back_args)
    wide_keep, wide_send, narrow_keep, narrow_send = first_sums(place, n2, dl, low, dproj, wide_got, narrow_own, narrow_got, grads[:1])

    def input_part(deps):
        return input_grad(place, tokens, gain_one, dq, dkv, qkv_weight, peer_qkv, dres, deps)

    if paired:
        mlp = Chain(
            place,
            [
                (WIDE_ORDER, WIDE_SLOT, wide_keep, wide_send),
                (NARROW_ORDER, NARROW_SLOT, narrow_keep, narrow_send),
            ],
        )
        grads = attend_back(1, 3, grads, mlp.sent, *back_args)
        mlp.advance(grads[:1])
        dq, dkv_own, dkv_peer = attend_back(4, 2, grads, mlp.sent, *back_args)
        (dkv_peer,) = mlp.advance((dq,), (dkv_peer,))
        dkv_got = swap_cores(dkv_peer)
        query_for_peer, query_own = query_terms(place, n1, dq, mlp.sent)
        key_for_peer, dkv = key_terms(place, n1, dq, dkv_own, dkv_got, cosine, sine, (query_own,))
        query_for_peer, key_for_peer = mlp.advance((dkv,), (query_for_peer, key_for_peer))
        key_got, query_got = swap_cores(key_for_peer), swap_cores(query_for_peer)
        key_mine = key_own(place, n1, dq, dkv, mlp.sent)
        grad_tokens = input_part((key_mine,))
        mlp.advance((grad_tokens,))
        (kv_keep, kv_send, q_keep, q_send), _ = advance(
            place,
            [("split", KEY_SLOT, key_mine, key_got), ("split", QUERY_SLOT, query_own, query_got)],
            mlp.sent,
            (),
        )
        qkv = Chain(
            place,
            [(KEY_ORDER, KEY_SLOT, kv_keep, kv_send), (QUERY_ORDER, QUERY_SLOT, q_keep, q_send)],
        )
        deps = ()
        for index, joint in enumerate(PATTERN):
            if joint:
                advance_both(qkv, mlp, deps)
            else:
                qkv.advance(mlp.got[1:] if index == 4 else deps)
            deps = ()
        grad_in, grad_out, grad_down, in_sums = finish_mlp(
            place, mlp.kept[0], mlp.got[0], mlp.kept[1], mlp.got[1], in_weight, qkv.sent
        )
        grad_qkv, qkv_sums = finish_qkv(
            place, qkv.kept[1], qkv.got[1], qkv.kept[0], qkv.got[0], qkv_weight, (in_sums,)
        )
    else:
        grads = attend_back(1, PAIRS - 1, grads, (), *back_args)
        dq, dkv_own, dkv_peer = grads
        query_for_peer, query_own = query_terms(place, n1, dq, ())
        key_for_peer, dkv = key_terms(place, n1, dq, dkv_own, swap_cores(dkv_peer), cosine, sine, ())
        pieces = []
        for own, for_peer in ((query_own, query_for_peer), (key_own(place, n1, dq, dkv, ()), key_for_peer)):
            total = add(own, swap_cores(for_peer))
            pieces += [total[: HALF // 2], total[HALF // 2 :]]
        grad_tokens = input_part(())
        total = lambda part: lax.psum(part.astype(F32), "rep")
        grad_qkv, qkv_sums = finish_qkv(place, *[total(part) for part in pieces], qkv_weight, ())
        grad_in, grad_out, grad_down, in_sums = finish_mlp(
            place, *[total(part) for part in (wide_keep, wide_send, narrow_keep, narrow_send)], in_weight, ()
        )
    grad_gain_one = qkv_sums[:, 0] / attn_gain.astype(F32)
    grad_gain_two = in_sums[:, 0] / mlp_gain.astype(F32)
    return (
        result,
        grad_tokens,
        grad_gain_one,
        grad_qkv,
        grad_out,
        grad_gain_two,
        grad_in,
        grad_down,
    )


def solution(mesh):
    rows = P(("rep", "fsdp"), None)
    vector, matrix = P("fsdp"), P("fsdp", None)
    in_specs = (rows, vector, matrix, matrix, vector, matrix, matrix, P("rep", None), rows)
    out_specs = (rows, rows, vector, matrix, matrix, vector, matrix, matrix)
    return jax.shard_map(
        on_device, mesh=mesh, in_specs=in_specs, out_specs=out_specs, check_vma=False
    )
```

```python
import functools

import jax
import jax.numpy as jnp
from jax import lax
from jax.experimental import pallas as pl
from jax.experimental.pallas import tpu as pltpu
from jax.sharding import PartitionSpec as P

D = 768
HEADS = 12
HEAD_DIM = 64
FF = 1152
HALF = D // 2
LANES = 128
PAIRS = D // LANES
QKV = 3 * D
WIDE = 2 * FF + D
PACK = WIDE + FF
FLOW = 3200
LEAD = 256
KEY_FLOW = 2 * D + LEAD
WIDE_SLOT, NARROW_SLOT, QUERY_SLOT, KEY_SLOT = 1, 5, 9, 13

epsilon = 1e-05
rope_base = 160000.0
BLOCKED = -(2.0**100)
F32 = jnp.float32
BF16 = jnp.bfloat16
MIB = 1 << 20

NN = (((1,), (0,)), ((), ()))
NT = (((1,), (1,)), ((), ()))
TN = (((0,), (0,)), ((), ()))


def mm(a, b, dims=NN):
    return lax.dot_general(a, b, dims, preferred_element_type=F32)


def vmem():
    return pl.BlockSpec(memory_space=pltpu.VMEM)


def anywhere():
    return pl.BlockSpec(memory_space=pl.ANY)


def in_hbm():
    return pl.BlockSpec(memory_space=pltpu.HBM)


def after(kernel, count, deps):
    def body(*refs):
        kernel(*refs[:count], *refs[count + len(deps) :])

    return body


def smem():
    return pl.BlockSpec(memory_space=pltpu.SMEM)


def params(mib):
    return pltpu.CompilerParams(vmem_limit_bytes=mib * MIB)


def cost(flops, nbytes):
    return pl.CostEstimate(flops=int(flops) >> 10, bytes_accessed=int(nbytes) >> 10, transcendentals=0)


def halves_in(own_ref, peer_ref, whole, sems, slot, core):
    rows = own_ref.shape[0]
    mine = pl.multiple_of(core * rows, 16)
    other = pl.multiple_of((1 - core) * rows, 16)
    return (
        pltpu.make_async_copy(own_ref, whole.at[pl.ds(mine, rows), :], sems.at[slot]),
        pltpu.make_async_copy(peer_ref, whole.at[pl.ds(other, rows), :], sems.at[slot + 1]),
    )


def lane_in_head(shape):
    return lax.broadcasted_iota(jnp.int32, shape, 1) % HEAD_DIM


def swap_halves(values):
    place = lane_in_head(values.shape)
    return jnp.where(
        place < HEAD_DIM // 2,
        pltpu.roll(values, LANES - HEAD_DIM // 2, 1),
        pltpu.roll(values, HEAD_DIM // 2, 1),
    )


def normalize(values):
    row_mean = jnp.mean(values, axis=-1, keepdims=True)
    centred = values - row_mean
    row_var = jnp.mean(centred * centred, axis=-1, keepdims=True)
    inverse = lax.rsqrt(row_var + epsilon)
    return centred * inverse, inverse


def whole_gain(place_ref, own_ref, peer_ref):
    own, peer = own_ref[...].astype(F32), peer_ref[...].astype(F32)
    first = place_ref[0] == 0
    return jnp.concatenate([jnp.where(first, own, peer), jnp.where(first, peer, own)], axis=1)


def norm_kernel(place_ref, x_ref, own_ref, peer_ref, n_ref):
    hat, _ = normalize(x_ref[...].astype(F32))
    n_ref[...] = (hat * whole_gain(place_ref, own_ref, peer_ref)).astype(BF16)


def first_norm(place, x, gain):
    rows = 128
    block = pl.BlockSpec((rows, D), lambda i: (i, 0))
    return pl.pallas_call(
        norm_kernel,
        grid=(x.shape[0] // rows,),
        out_shape=jax.ShapeDtypeStruct(x.shape, BF16),
        in_specs=[smem(), block] + [pl.BlockSpec((1, HALF), lambda i: (0, 0))] * 2,
        out_specs=block,
        compiler_params=params(8),
        cost_estimate=cost(MIB, 2 * MIB),
        name="first_norm",
    )(place, x, *gain)


def project_kernel(parts, scale, place_ref, n_ref, own_ref, peer_ref, cos_ref, sin_ref, out_ref):
    core = place_ref[0]
    mine = pl.ds(pl.multiple_of(core * HALF, LANES), HALF)
    other = pl.ds(pl.multiple_of((1 - core) * HALF, LANES), HALF)
    rows = 256
    for r in range(n_ref.shape[0] // rows):
        part = pl.ds(r * rows, rows)
        left, right = n_ref[part, mine], n_ref[part, other]
        cosine, sine = cos_ref[part, :], sin_ref[part, :]
        for i, which in enumerate(parts):
            for half in range(2):
                at = slice(which * D + half * HALF, which * D + (half + 1) * HALF)
                out = mm(left, own_ref[:, at]) + mm(right, peer_ref[:, at])
                for tile in range(HALF // LANES):
                    piece = out[:, tile * LANES : (tile + 1) * LANES]
                    if which < 2:
                        piece = piece * cosine + swap_halves(piece) * sine
                    cols = pl.ds(half * HALF + tile * LANES, LANES)
                    out_ref[i, part, cols] = (piece * scale).astype(BF16)


def project(parts, scale, place, normed, own, peer, cosine, sine, deps):
    rows = normed.shape[0]
    return pl.pallas_call(
        after(functools.partial(project_kernel, parts, scale), 6, deps),
        out_shape=jax.ShapeDtypeStruct((len(parts), rows, D), BF16),
        in_specs=[smem()] + [vmem()] * 5 + [anywhere()] * len(deps),
        out_specs=vmem(),
        compiler_params=params(12),
        cost_estimate=cost(2 * rows * D * D * len(parts), 8 * MIB),
        name="project",
    )(place, normed, own, peer, cosine, sine, *deps)


def attend_kernel(q_ref, ko_ref, vo_ref, kp_ref, vp_ref, mq_ref, mk_ref, att_ref, low_ref, lse_ref):
    rows = q_ref.shape[0]
    tile = min(512, rows)
    keys = jnp.concatenate([ko_ref[0], kp_ref[0]], axis=0)
    values = jnp.concatenate([vo_ref[0], vp_ref[0]], axis=0)
    key_first = lax.broadcasted_iota(jnp.int32, keys.shape, 1) < HEAD_DIM
    one = jnp.ones_like(values)
    mask_keys = mk_ref[...]
    k_both = (jnp.where(key_first, keys, mask_keys), jnp.where(key_first, mask_keys, keys))
    v_both = (jnp.where(key_first, values, one), jnp.where(key_first, one, values))
    first = lax.broadcasted_iota(jnp.int32, (tile, LANES), 1) < HEAD_DIM
    for t in range(rows // tile):
        part = pl.ds(t * tile, tile)
        query, mask_q = q_ref[part, :], mq_ref[part, :]
        sides = (first, jnp.logical_not(first))
        scores = [mm(jnp.where(sides[head], query, mask_q), k_both[head], NT) for head in range(2)]
        peaks = [jnp.max(raw, axis=-1, keepdims=True) for raw in scores]
        sums = []
        for head in range(2):
            weights = jnp.exp(scores[head] - peaks[head]).astype(BF16)
            sums.append(mm(weights, v_both[head]))
        numer = jnp.where(first, sums[0], sums[1])
        denom = jnp.where(first, pltpu.roll(sums[0], HEAD_DIM, 1), pltpu.roll(sums[1], HEAD_DIM, 1))
        out = numer / denom
        att_ref[part, :] = out
        low_ref[part, :] = out.astype(BF16)
        lse_ref[part, :] = jnp.where(first, peaks[0], peaks[1]) + jnp.log(denom)


def kv_specs(rows):
    return [
        pl.BlockSpec((1, rows, LANES), lambda i: (0, 0, i)),
        pl.BlockSpec((1, rows, LANES), lambda i: (1, 0, i)),
    ]


def attend(query, kv_own, kv_peer, mask_q, mask_k):
    rows = query.shape[0]
    keys = mask_k.shape[0]
    pair = pl.BlockSpec((rows, LANES), lambda i: (0, i))
    whole = lambda n: pl.BlockSpec((n, LANES), lambda i: (0, 0))
    return pl.pallas_call(
        attend_kernel,
        grid=(PAIRS,),
        out_shape=(
            jax.ShapeDtypeStruct((rows, D), F32),
            jax.ShapeDtypeStruct((rows, D), BF16),
            jax.ShapeDtypeStruct((rows, D), F32),
        ),
        in_specs=[pair] + kv_specs(rows) + kv_specs(rows) + [whole(rows), whole(keys)],
        out_specs=(pair, pair, pair),
        compiler_params=params(16),
        cost_estimate=cost(16 * rows * keys * D, 8 * MIB),
        name="attend",
    )(query, kv_own, kv_own, kv_peer, kv_peer, mask_q, mask_k)


def middle_kernel(
    core_ref, x_ref, low_ref, dy_ref, gain_ref, gain_peer_ref,
    oo_ref, op_ref, io_ref, ip_ref, do_ref, dp_ref,
    result_ref, n2_ref, act_ref, dl_ref, dres_ref, dproj_ref, datt_ref,
    wo_ref, wi_ref, wd_ref, sems,
):
    core = core_ref[0]
    copies = (
        halves_in(oo_ref, op_ref, wo_ref, sems, 0, core),
        halves_in(io_ref, ip_ref, wi_ref, sems, 2, core),
        halves_in(do_ref, dp_ref, wd_ref, sems, 4, core),
    )
    for pair in copies:
        for copy in pair:
            copy.start()

    def arrived(which):
        for copy in copies[which]:
            copy.wait()

    gain = whole_gain(core_ref, gain_ref, gain_peer_ref)
    rows = 256
    block = 384
    for r in range(x_ref.shape[0] // rows):
        part = pl.ds(r * rows, rows)
        if r == 0:
            arrived(0)
        resid = x_ref[part, :].astype(F32) + mm(low_ref[part, :], wo_ref[...])
        hat, inverse = normalize(resid)
        n2 = (hat * gain).astype(BF16)
        n2_ref[part, :] = n2
        dy = dy_ref[part, :]
        if r == 0:
            arrived(1)
            arrived(2)
        for b in range(FF // block):
            cols = slice(b * block, (b + 1) * block)
            gate_cols = slice(FF + b * block, FF + (b + 1) * block)
            lift = mm(n2, wi_ref[:, cols])
            gate = mm(n2, wi_ref[:, gate_cols])
            d_act = mm(dy, wd_ref[cols, :], NT)
            cdf = 0.5 + 0.5 * lax.erf(lift * (0.5**0.5))
            bell = jnp.exp(-0.5 * lift * lift) * 0.3989422804014327
            gelu = lift * cdf
            act_ref[part, cols] = (gelu * gate).astype(BF16)
            dl_ref[part, cols] = (d_act * gate * (cdf + lift * bell)).astype(BF16)
            dl_ref[part, gate_cols] = (d_act * gelu).astype(BF16)
        result_ref[part, :] = (resid + mm(act_ref[part, :], wd_ref[...])).astype(BF16)
        d_normed = mm(dl_ref[part, :], wi_ref[...], NT)
        d_hat = d_normed * gain
        d_resid = dy.astype(F32) + inverse * (
            d_hat
            - jnp.mean(d_hat, axis=-1, keepdims=True)
            - hat * jnp.mean(d_hat * hat, axis=-1, keepdims=True)
        )
        dres_ref[part, :] = d_resid
        d_proj = d_resid.astype(BF16)
        dproj_ref[part, :] = d_proj
        datt_ref[part, :] = mm(d_proj, wo_ref[...], NT).astype(BF16)


def middle(core, x, low, dy, gain, w_out, w_in, w_down):
    rows = x.shape[0]
    low_shape = lambda n: jax.ShapeDtypeStruct((rows, n), BF16)
    return pl.pallas_call(
        middle_kernel,
        out_shape=(
            low_shape(D), low_shape(D), low_shape(FF), low_shape(2 * FF),
            jax.ShapeDtypeStruct((rows, D), F32), low_shape(D), low_shape(D),
        ),
        in_specs=[smem()] + [vmem()] * 5 + [in_hbm()] * 6,
        out_specs=(vmem(),) * 7,
        scratch_shapes=[
            pltpu.VMEM((D, D), BF16),
            pltpu.VMEM((D, 2 * FF), BF16),
            pltpu.VMEM((FF, D), BF16),
            pltpu.SemaphoreType.DMA((6,)),
        ],
        compiler_params=params(32),
        cost_estimate=cost(2 * rows * D * (2 * D + 6 * FF), 16 * MIB),
        name="middle",
    )(core, x, low, dy, *gain, *w_out, *w_in, *w_down)


def fold_down(ref, block):
    rest = block.shape[0] - HALF
    ref[:, :D] = block[:HALF]
    ref[0:rest, D:FF] = block[HALF:, :HALF]
    ref[rest : 2 * rest, D:FF] = block[HALF:, HALF:]


def narrow_kernel(core_ref, act_ref, dy_ref, peer_ref, own_ref, whole):
    core = core_ref[0]
    for b in range(FF // 384):
        rows = slice(b * 384, (b + 1) * 384)
        whole[rows, :] = mm(act_ref[:, rows], dy_ref[...], TN).astype(BF16)
    size = FF // 2
    for ref, side in ((peer_ref, 1 - core), (own_ref, core)):
        fold_down(ref, whole[pl.ds(pl.multiple_of(side * size, 16), size), :])


def narrow_terms(core, act, dy):
    rows = act.shape[0]
    half = jax.ShapeDtypeStruct((HALF, FF), BF16)
    return pl.pallas_call(
        narrow_kernel,
        out_shape=(half, half),
        in_specs=[smem()] + [vmem()] * 2,
        out_specs=(vmem(), vmem()),
        scratch_shapes=[pltpu.VMEM((FF, D), BF16)],
        compiler_params=params(14),
        cost_estimate=cost(2 * rows * D * FF, 8 * MIB),
        name="narrow_terms",
    )(core, act, dy)


def wide_block(side, n2_ref, dl_ref, low_ref, dproj_ref, store):
    cols = pl.ds(pl.multiple_of(side * HALF, LANES), HALF)
    n2 = n2_ref[:, cols]
    for b in range(2 * FF // 384):
        at = slice(b * 384, (b + 1) * 384)
        store(at, mm(n2, dl_ref[:, at], TN))
    store(slice(2 * FF, WIDE), mm(low_ref[:, cols], dproj_ref[...], TN))


def wide_peer_kernel(core_ref, n2_ref, dl_ref, low_ref, dproj_ref, peer_ref):
    def store(at, block):
        peer_ref[:, at] = block.astype(BF16)

    wide_block(1 - core_ref[0], n2_ref, dl_ref, low_ref, dproj_ref, store)


def wide_peer(core, n2, dl, low, dproj):
    rows = n2.shape[0]
    return pl.pallas_call(
        wide_peer_kernel,
        out_shape=jax.ShapeDtypeStruct((HALF, WIDE), BF16),
        in_specs=[smem()] + [vmem()] * 4,
        out_specs=vmem(),
        compiler_params=params(14),
        cost_estimate=cost(2 * rows * HALF * WIDE, 6 * MIB),
        name="wide_peer",
    )(core, n2, dl, low, dproj)


def split_rows(bit, block, at, keep_ref, send_ref):
    rows = block.shape[0] // 2
    keep_ref[:, at] = jnp.where(bit == 0, block[:rows], block[rows:]).astype(BF16)
    send_ref[:, at] = jnp.where(bit == 0, block[rows:], block[:rows]).astype(BF16)


def first_kernel(
    place_ref, n2_ref, dl_ref, low_ref, dproj_ref, got_ref, down_ref, down_got_ref,
    keep_ref, send_ref, narrow_keep, narrow_send,
):
    def store(at, block):
        split_rows(place_ref[WIDE_SLOT], block + got_ref[:, at].astype(F32), at, keep_ref, send_ref)

    wide_block(place_ref[0], n2_ref, dl_ref, low_ref, dproj_ref, store)
    total = down_ref[...].astype(F32) + down_got_ref[...].astype(F32)
    cut = FLOW - WIDE
    split_rows(place_ref[WIDE_SLOT], total[:, :cut], slice(WIDE, FLOW), keep_ref, send_ref)
    split_rows(place_ref[NARROW_SLOT], total[:, cut:], slice(0, PACK - FLOW), narrow_keep, narrow_send)


def first_sums(place, n2, dl, low, dproj, got, down, down_got, deps):
    rows = n2.shape[0]
    half = jax.ShapeDtypeStruct((HALF // 2, FLOW), BF16)
    narrow = jax.ShapeDtypeStruct((HALF // 2, PACK - FLOW), BF16)
    return pl.pallas_call(
        after(first_kernel, 8, deps),
        out_shape=(half, half, narrow, narrow),
        in_specs=[smem()] + [vmem()] * 7 + [anywhere()] * len(deps),
        out_specs=(vmem(),) * 4,
        compiler_params=params(16),
        cost_estimate=cost(2 * rows * HALF * WIDE, 8 * MIB),
        name="first_sums",
    )(place, n2, dl, low, dproj, got, down, down_got, *deps)


def split_three(values):
    high = values.astype(BF16)
    rest = values - high.astype(F32)
    mid = rest.astype(BF16)
    return high, mid, (rest - mid.astype(F32)).astype(BF16)


def place_three(values, place, others):
    high, mid, tail = split_three(-values)
    at = HEAD_DIM // 2
    out = jnp.where(place == at, high.astype(F32), others)
    out = jnp.where(place == at + 1, mid.astype(F32), out)
    return jnp.where(place == at + 2, tail.astype(F32), out)


def attend_back_kernel(
    q_ref, ko_ref, vo_ref, kp_ref, vp_ref, mq_ref, mk_ref, do_ref, att_ref, lse_ref, cos_ref, sin_ref,
    dq_ref, own_ref, peer_ref,
):
    rows = q_ref.shape[0]
    tile = min(512, rows)
    query, grad = q_ref[...], do_ref[...]
    place = lane_in_head(query.shape)
    first = lax.broadcasted_iota(jnp.int32, query.shape, 1) < HEAD_DIM
    tile_first = first[:tile]
    product = grad.astype(F32) * att_ref[...]
    lse = pltpu.roll(lse_ref[...], HEAD_DIM, 1)
    mask_q = mq_ref[...].astype(F32)
    zero = jnp.zeros_like(mask_q)
    q_both, g_both = [], []
    for head in range(2):
        side = first if head == 0 else jnp.logical_not(first)
        delta = jnp.sum(jnp.where(side, product, 0.0), axis=-1, keepdims=True)
        q_both.append(jnp.where(side, query, place_three(lse, place, mask_q).astype(BF16)))
        wide = jnp.broadcast_to(delta, product.shape)
        g_both.append(jnp.where(side, grad, place_three(wide, place, zero).astype(BF16)))
    d_query = [jnp.zeros((LANES, rows), F32) for _ in range(2)]
    for source in range(2):
        k_ref, v_ref, out_ref = ((ko_ref, vo_ref, own_ref), (kp_ref, vp_ref, peer_ref))[source]
        for t in range(rows // tile):
            part = pl.ds(t * tile, tile)
            keys, values = k_ref[0, part, :], v_ref[0, part, :]
            keys_across = keys.T
            marks = mk_ref[pl.ds(source * rows + t * tile, tile), :]
            d_keys, d_values = [], []
            for head in range(2):
                side = tile_first if head == 0 else jnp.logical_not(tile_first)
                probs = jnp.exp(mm(jnp.where(side, keys, marks), q_both[head], NT))
                d_probs = mm(jnp.where(side, values, marks), g_both[head], NT)
                d_scores = (probs * d_probs).astype(BF16)
                d_values.append(mm(probs.astype(BF16), grad))
                d_keys.append(mm(d_scores, query))
                d_query[head] = d_query[head] + mm(keys_across, d_scores)
            out_ref[0, part, :] = jnp.where(tile_first, d_keys[0], d_keys[1]).astype(BF16)
            out_ref[1, part, :] = jnp.where(tile_first, d_values[0], d_values[1]).astype(BF16)
    d_q = jnp.concatenate([d_query[0][:HEAD_DIM], d_query[1][HEAD_DIM:]], axis=0).T * HEAD_DIM**-0.5
    dq_ref[...] = (d_q * cos_ref[...] - swap_halves(d_q) * sin_ref[...]).astype(BF16)


def attend_back(first, count, so_far, deps, query, kv_own, kv_peer, mask_q, mask_k, grad, att, lse, cosine, sine):
    rows = query.shape[0]
    keys = mask_k.shape[0]
    pair = pl.BlockSpec((rows, LANES), lambda i: (0, first + i))
    both = pl.BlockSpec((2, rows, LANES), lambda i: (0, 0, first + i))
    whole = lambda n: pl.BlockSpec((n, LANES), lambda i: (0, 0))
    kv = [
        pl.BlockSpec((1, rows, LANES), lambda i: (0, 0, first + i)),
        pl.BlockSpec((1, rows, LANES), lambda i: (1, 0, first + i)),
    ]
    extra = tuple(so_far) + tuple(deps)
    return pl.pallas_call(
        after(attend_back_kernel, 12, extra),
        grid=(count,),
        out_shape=(
            jax.ShapeDtypeStruct((rows, D), BF16),
            jax.ShapeDtypeStruct((2, rows, D), BF16),
            jax.ShapeDtypeStruct((2, rows, D), BF16),
        ),
        in_specs=[pair] + kv + kv
        + [whole(rows), whole(keys), pair, pair, pair, whole(rows), whole(rows)]
        + [anywhere()] * len(extra),
        out_specs=(pair, both, both),
        input_output_aliases={12 + i: i for i in range(len(so_far))},
        compiler_params=params(18),
        cost_estimate=cost(40 * rows * keys * LANES * count, 2 * MIB * count),
        name="attend_back",
    )(query, kv_own, kv_own, kv_peer, kv_peer, mask_q, mask_k, grad, att, lse, cosine, sine, *extra)


def query_terms_kernel(core_ref, n1_ref, dq_ref, peer_ref, own_ref):
    for ref, side in ((peer_ref, 1 - core_ref[0]), (own_ref, core_ref[0])):
        cols = pl.ds(pl.multiple_of(side * HALF, LANES), HALF)
        ref[...] = mm(n1_ref[:, cols], dq_ref[:, LEAD:], TN).astype(BF16)


def query_terms(core, n1, dq, deps):
    rows = n1.shape[0]
    half = jax.ShapeDtypeStruct((HALF, D - LEAD), BF16)
    return pl.pallas_call(
        after(query_terms_kernel, 3, deps),
        out_shape=(half, half),
        in_specs=[smem()] + [vmem()] * 2 + [anywhere()] * len(deps),
        out_specs=(vmem(), vmem()),
        compiler_params=params(12),
        cost_estimate=cost(2 * rows * D * D, 3 * MIB),
        name="query_terms",
    )(core, n1, dq, *deps)


def key_terms_kernel(core_ref, n1_ref, dq_ref, own_ref, got_ref, cos_ref, sin_ref, peer_ref, dkv_ref):
    cosine, sine = cos_ref[...], sin_ref[...]
    cols = pl.ds(pl.multiple_of((1 - core_ref[0]) * HALF, LANES), HALF)
    n1 = n1_ref[:, cols]
    for pair in range(PAIRS):
        at = slice(pair * LANES, (pair + 1) * LANES)
        d_key = own_ref[0, :, at].astype(F32) + got_ref[0, :, at].astype(F32)
        d_value = own_ref[1, :, at].astype(F32) + got_ref[1, :, at].astype(F32)
        d_key = d_key * cosine - swap_halves(d_key) * sine
        dkv_ref[:, at] = d_key.astype(BF16)
        dkv_ref[:, D + pair * LANES : D + (pair + 1) * LANES] = d_value.astype(BF16)
    for b in range(2 * D // 384):
        at = slice(b * 384, (b + 1) * 384)
        peer_ref[:, at] = mm(n1, dkv_ref[:, at], TN).astype(BF16)
    peer_ref[:, 2 * D :] = mm(n1, dq_ref[:, :LEAD], TN).astype(BF16)


def key_terms(core, n1, dq, own, got, cosine, sine, deps):
    rows = n1.shape[0]
    return pl.pallas_call(
        after(key_terms_kernel, 7, deps),
        out_shape=(jax.ShapeDtypeStruct((HALF, KEY_FLOW), BF16), jax.ShapeDtypeStruct((rows, 2 * D), BF16)),
        in_specs=[smem()] + [vmem()] * 6 + [anywhere()] * len(deps),
        out_specs=(vmem(), vmem()),
        compiler_params=params(16),
        cost_estimate=cost(2 * rows * D * D, 6 * MIB),
        name="key_terms",
    )(core, n1, dq, own, got, cosine, sine, *deps)


def key_own_kernel(place_ref, n1_ref, dq_ref, dkv_ref, own_ref):
    n1 = n1_ref[:, pl.ds(pl.multiple_of(place_ref[0] * HALF, LANES), HALF)]
    for b in range(2 * D // 384):
        at = slice(b * 384, (b + 1) * 384)
        own_ref[:, at] = mm(n1, dkv_ref[:, at], TN).astype(BF16)
    own_ref[:, 2 * D :] = mm(n1, dq_ref[:, :LEAD], TN).astype(BF16)


def key_own(place, n1, dq, dkv, deps):
    rows = n1.shape[0]
    return pl.pallas_call(
        after(key_own_kernel, 4, deps),
        out_shape=jax.ShapeDtypeStruct((HALF, KEY_FLOW), BF16),
        in_specs=[smem()] + [vmem()] * 3 + [anywhere()] * len(deps),
        out_specs=vmem(),
        compiler_params=params(12),
        cost_estimate=cost(2 * rows * D * D, 6 * MIB),
        name="key_own",
    )(place, n1, dq, dkv, *deps)


def input_kernel(
    core_ref, x_ref, gain_ref, gain_peer_ref, dq_ref, dkv_ref, own_ref, peer_ref, dres_ref, dx_ref, w_ref, sems
):
    copies = halves_in(own_ref, peer_ref, w_ref, sems, 0, core_ref[0])
    for copy in copies:
        copy.start()
    for copy in copies:
        copy.wait()
    gain = whole_gain(core_ref, gain_ref, gain_peer_ref)
    rows = 256
    for r in range(x_ref.shape[0] // rows):
        part = pl.ds(r * rows, rows)
        hat, inverse = normalize(x_ref[part, :].astype(F32))
        d_normed = mm(dq_ref[part, :], w_ref[:, :D], NT) + mm(dkv_ref[part, :], w_ref[:, D:], NT)
        d_hat = d_normed * gain
        back = inverse * (
            d_hat
            - jnp.mean(d_hat, axis=-1, keepdims=True)
            - hat * jnp.mean(d_hat * hat, axis=-1, keepdims=True)
        )
        dx_ref[part, :] = (dres_ref[part, :] + back).astype(BF16)


def input_grad(core, x, gain, dq, dkv, own, peer, dres, deps):
    rows = x.shape[0]
    return pl.pallas_call(
        after(input_kernel, 9, deps),
        out_shape=jax.ShapeDtypeStruct((rows, D), BF16),
        in_specs=[smem()] + [vmem()] * 5 + [in_hbm()] * 2 + [vmem()] + [anywhere()] * len(deps),
        out_specs=vmem(),
        scratch_shapes=[pltpu.VMEM((D, QKV), BF16), pltpu.SemaphoreType.DMA((2,))],
        compiler_params=params(16),
        cost_estimate=cost(2 * rows * D * QKV, 10 * MIB),
        name="input_grad",
    )(core, x, *gain, dq, dkv, own, peer, dres, *deps)


BITS = {"x": 1, "y": 2, "n": 4, "f": 8}
WIDE_ORDER = ("xy", "yx", "nf", "fn")
NARROW_ORDER = ("nf", "fn", "xy", "yx")
KEY_ORDER = ("xy", "yx", "nf", "fn")
QUERY_ORDER = ("nf", "fn", "xy", "yx")
PATTERN = (1, 1, 1, 0, 0, 0, 0)
ALL_ORDERS = WIDE_ORDER + NARROW_ORDER + QUERY_ORDER + KEY_ORDER


def trade(values, axes):
    pairs = []
    for group in range(16):
        for core in range(2):
            pairs.append((2 * group + core, 2 * (group ^ BITS[axes[core]]) + core))
    return lax.ppermute(values, ("rep", "fsdp"), pairs)


def bit_of(axes):
    step = jnp.where(lax.axis_index("fsdp") == 0, BITS[axes[0]], BITS[axes[1]])
    return (lax.axis_index("rep") // step) % 2


def advance_kernel(plan, place_ref, *refs):
    ins, outs = refs[: 2 * len(plan)], list(refs[2 * len(plan) :])
    for i, (mode, slot) in enumerate(plan):
        kept, got = ins[2 * i][...].astype(F32), ins[2 * i + 1][...].astype(F32)
        if mode == "split":
            split_rows(place_ref[slot], kept + got, slice(0, kept.shape[1]), outs.pop(0), outs.pop(0))
        elif mode == "add":
            outs.pop(0)[...] = (kept + got).astype(BF16)
        else:
            bit = place_ref[slot]
            both = [jnp.where(bit == 0, kept, got), jnp.where(bit == 0, got, kept)]
            outs.pop(0)[...] = jnp.concatenate(both, axis=0).astype(BF16)


def advance(place, flows, deps, carried):
    plan, arrays, shapes = [], [], []
    for mode, slot, kept, got in flows:
        rows, cols = kept.shape
        plan.append((mode, slot))
        arrays += [kept, got]
        sizes = {"split": [rows // 2, rows // 2], "add": [rows], "join": [2 * rows]}[mode]
        shapes += [jax.ShapeDtypeStruct((size, cols), BF16) for size in sizes]
    count, made = 1 + len(arrays), len(shapes)
    extra = tuple(carried) + tuple(deps)
    kernel = functools.partial(advance_kernel, plan)

    def body(*refs):
        outs = refs[count + len(extra) :]
        kernel(*refs[:count], *outs[:made])

    outs = pl.pallas_call(
        body,
        out_shape=tuple(shapes) + tuple(jax.ShapeDtypeStruct(a.shape, a.dtype) for a in carried),
        in_specs=[smem()] + [vmem()] * len(arrays) + [anywhere()] * len(extra),
        out_specs=(vmem(),) * made + (anywhere(),) * len(carried),
        input_output_aliases={count + i: made + i for i in range(len(carried))},
        compiler_params=params(12),
        cost_estimate=cost(MIB, 2 * MIB),
        name="advance",
    )(place, *arrays, *extra)
    return outs[:made], outs[made:]


class Chain:
    def __init__(self, place, flows):
        self.place, self.step = place, 0
        self.orders = [order for order, *_ in flows]
        self.slots = [slot for _, slot, *_ in flows]
        self.kept = [kept for *_, kept, _ in flows]
        self.exchange([send for *_, send in flows])

    def exchange(self, sends):
        axis = self.step if self.step < 4 else 7 - self.step
        self.sent = tuple(sends)
        self.got = [trade(send, order[axis]) for send, order in zip(sends, self.orders)]

    def flows(self):
        modes = [("split", self.step + 1), ("add", 0), ("join", 7 - self.step)]
        mode, bit = modes[(self.step >= 3) + (self.step > 3)]
        return [(mode, slot + bit, *pair) for slot, *pair in zip(self.slots, self.kept, self.got)]

    def take(self, parts):
        if self.step < 3:
            self.kept, sends = parts[0::2], parts[1::2]
        else:
            self.kept = sends = parts
        self.step += 1
        self.exchange(sends)

    def advance(self, deps, carried=()):
        parts, carried = advance(self.place, self.flows(), deps, carried)
        self.take(parts)
        return carried


def advance_both(one, two, deps):
    flows = one.flows()
    parts, _ = advance(one.place, flows + two.flows(), deps, ())
    count = sum(2 if mode == "split" else 1 for mode, *_ in flows)
    one.take(parts[:count])
    two.take(parts[count:])


def weighted_sum(total, weight):
    sums = jnp.sum(total * weight.astype(F32), axis=-1, keepdims=True)
    return jnp.broadcast_to(sums, (total.shape[0], LANES))


def finish_mlp_kernel(
    place_ref, mine, theirs, narrow_mine, narrow_theirs, weight_ref, in_ref, out_ref, down_ref, sum_ref
):
    rows = HALF // 2
    rest = FF // 2 - HALF
    cut = FLOW - WIDE
    bit, narrow_bit = place_ref[WIDE_SLOT], place_ref[NARROW_SLOT]
    for half in range(2):
        at = slice(half * rows, (half + 1) * rows)

        def pick(start, stop):
            cols = slice(start, stop)
            return jnp.where(bit == half, mine[:, cols].astype(F32), theirs[:, cols].astype(F32))

        def pick_narrow(start, stop):
            cols = slice(start, stop)
            return jnp.where(
                narrow_bit == half, narrow_mine[:, cols].astype(F32), narrow_theirs[:, cols].astype(F32)
            )

        total = pick(0, 2 * FF)
        in_ref[at, :] = total
        sum_ref[at, :] = weighted_sum(total, weight_ref[at, :])
        out_ref[at, :] = pick(2 * FF, WIDE)
        down_ref[at, :cut] = pick(WIDE, FLOW)
        down_ref[at, cut:] = pick_narrow(0, D - cut)
        down_ref[HALF : HALF + rest, half * HALF : (half + 1) * HALF] = pick_narrow(D - cut, FF - cut)


def mlp_outputs():
    return (
        jax.ShapeDtypeStruct((HALF, 2 * FF), F32),
        jax.ShapeDtypeStruct((HALF, D), F32),
        jax.ShapeDtypeStruct((FF // 2, D), F32),
        jax.ShapeDtypeStruct((HALF, LANES), F32),
    )


def finish_mlp(place, mine, theirs, narrow_mine, narrow_theirs, weight, deps):
    return pl.pallas_call(
        after(finish_mlp_kernel, 6, deps),
        out_shape=mlp_outputs(),
        in_specs=[smem()] + [vmem()] * 5 + [anywhere()] * len(deps),
        out_specs=(vmem(),) * 4,
        compiler_params=params(20),
        cost_estimate=cost(MIB, 10 * MIB),
        name="finish_mlp",
    )(place, mine, theirs, narrow_mine, narrow_theirs, weight, *deps)


def finish_qkv_kernel(place_ref, q_ref, q_got, kv_ref, kv_got, weight_ref, out_ref, sum_ref):
    step = out_ref.shape[0]
    half = pl.program_id(0) * step // (HALF // 2)
    at = pl.ds(pl.multiple_of(pl.program_id(0) * step - half * (HALF // 2), step), step)
    sums = jnp.zeros((step, LANES), F32)
    key_flow, query_flow = (KEY_SLOT, kv_ref, kv_got), (QUERY_SLOT, q_ref, q_got)
    pieces = ((key_flow, 2 * D, 0, LEAD), (query_flow, 0, LEAD, D - LEAD), (key_flow, 0, D, 2 * D))
    for (slot, mine, theirs), start, to, width in pieces:
        come, cols = slice(start, start + width), slice(to, to + width)
        total = jnp.where(
            place_ref[slot] == half, mine[at, come].astype(F32), theirs[at, come].astype(F32)
        )
        out_ref[:, cols] = total
        sums = sums + weighted_sum(total, weight_ref[:, cols])
    sum_ref[...] = sums


def finish_qkv(place, q_mine, q_theirs, kv_mine, kv_theirs, weight, deps):
    step = 96
    whole = lambda array: pl.BlockSpec(array.shape, lambda i: (0, 0))
    arrays = (q_mine, q_theirs, kv_mine, kv_theirs)
    return pl.pallas_call(
        after(finish_qkv_kernel, 6, deps),
        grid=(HALF // step,),
        out_shape=(jax.ShapeDtypeStruct((HALF, QKV), F32), jax.ShapeDtypeStruct((HALF, LANES), F32)),
        in_specs=[smem()] + [whole(array) for array in arrays] + [pl.BlockSpec((step, QKV), lambda i: (i, 0))]
        + [anywhere()] * len(deps),
        out_specs=(
            pl.BlockSpec((step, QKV), lambda i: (i, 0)),
            pl.BlockSpec((step, LANES), lambda i: (i, 0)),
        ),
        compiler_params=params(14),
        cost_estimate=cost(MIB, 7 * MIB),
        name="finish_qkv",
    )(place, *arrays, weight, *deps)


def add(left, right):
    return (left.astype(F32) + right.astype(F32)).astype(BF16)


def swap_cores(values):
    return lax.ppermute(values, "fsdp", [(0, 1), (1, 0)])


def layout(lengths, slot_count):
    slots = jnp.arange(slot_count, dtype=jnp.int32)
    order = jnp.arange(lengths.shape[0])
    ends = jnp.sum(jnp.where(order[None, :] <= order[:, None], lengths[None, :], 0), axis=1)
    segment = jnp.sum((slots[:, None] >= ends[None, :]).astype(jnp.int32), axis=1)
    begins = jnp.max(jnp.where(ends[None, :] <= slots[:, None], ends[None, :], 0), axis=1)
    return (segment, slots - begins)


def on_device(
    tokens, attn_gain, qkv_weight, out_weight, mlp_gain, in_weight, down_weight, seq_len, cotangent
):
    row_count = tokens.shape[0]
    core = lax.axis_index("fsdp")
    paired = lax.axis_size("rep") == 16
    bits = [bit_of(axes) if paired else 0 * core for axes in ALL_ORDERS]
    place = jnp.stack([core] + bits).astype(jnp.int32)
    peer_qkv = swap_cores(qkv_weight)
    own_gains = (attn_gain.reshape(1, HALF), mlp_gain.reshape(1, HALF))
    gain_one, gain_two = [(own, swap_cores(own)) for own in own_gains]
    peer_out = swap_cores(out_weight)
    peer_in = swap_cores(in_weight)
    peer_down = swap_cores(down_weight)
    key_seg, key_pos = layout(seq_len[0], 2 * row_count)
    own_seg = lax.dynamic_slice_in_dim(key_seg, core * row_count, row_count)
    peer_seg = lax.dynamic_slice_in_dim(key_seg, (1 - core) * row_count, row_count)
    own_pos = lax.dynamic_slice_in_dim(key_pos, core * row_count, row_count)
    lane = jnp.arange(LANES, dtype=jnp.int32) % HEAD_DIM
    half_dim = HEAD_DIM // 2
    freq = jnp.exp(-jnp.log(rope_base) * (2.0 * (lane % half_dim).astype(F32) / HEAD_DIM))
    angles = own_pos.astype(F32)[:, None] * freq[None, :]
    cosine = jnp.cos(angles)
    sine = jnp.sin(angles) * jnp.where(lane < half_dim, -1.0, 1.0)[None, :]
    marks = lane < half_dim
    mask_q = jnp.where(marks[None, :] & (own_seg[:, None] != lane[None, :]), BLOCKED, 0.0).astype(BF16)
    both_seg = jnp.concatenate([own_seg, peer_seg])
    mask_k = jnp.where(
        marks[None, :], both_seg[:, None] == lane[None, :], (lane < half_dim + 3)[None, :]
    ).astype(BF16)

    n1 = first_norm(place, tokens, gain_one)
    project_args = (place, n1, qkv_weight, peer_qkv, cosine, sine)
    kv_own = project((1, 2), 1.0, *project_args, ())
    kv_peer = swap_cores(kv_own)
    query = project((0,), HEAD_DIM**-0.5, *project_args, (kv_own,)).reshape(row_count, D)
    att, low, lse = attend(query, kv_own, kv_peer, mask_q, mask_k)
    result, n2, act, dl, dres, dproj, datt = middle(
        place, tokens, low, cotangent, gain_two,
        (out_weight, peer_out), (in_weight, peer_in), (down_weight, peer_down),
    )
    wide_for_peer = wide_peer(place, n2, dl, low, dproj)
    wide_got = swap_cores(wide_for_peer)
    narrow_for_peer, narrow_own = narrow_terms(place, act, cotangent)
    narrow_got = swap_cores(narrow_for_peer)
    back_args = (query, kv_own, kv_peer, mask_q, mask_k, datt, att, lse, cosine, sine)
    grads = attend_back(0, 1, (), (wide_for_peer, narrow_own), *back_args)
    wide_keep, wide_send, narrow_keep, narrow_send = first_sums(place, n2, dl, low, dproj, wide_got, narrow_own, narrow_got, grads[:1])

    def input_part(deps):
        return input_grad(place, tokens, gain_one, dq, dkv, qkv_weight, peer_qkv, dres, deps)

    if paired:
        mlp = Chain(
            place,
            [
                (WIDE_ORDER, WIDE_SLOT, wide_keep, wide_send),
                (NARROW_ORDER, NARROW_SLOT, narrow_keep, narrow_send),
            ],
        )
        grads = attend_back(1, 3, grads, mlp.sent, *back_args)
        mlp.advance(grads[:1])
        dq, dkv_own, dkv_peer = attend_back(4, 2, grads, mlp.sent, *back_args)
        (dkv_peer,) = mlp.advance((dq,), (dkv_peer,))
        dkv_got = swap_cores(dkv_peer)
        query_for_peer, query_own = query_terms(place, n1, dq, mlp.sent)
        key_for_peer, dkv = key_terms(place, n1, dq, dkv_own, dkv_got, cosine, sine, (query_own,))
        query_for_peer, key_for_peer = mlp.advance((dkv,), (query_for_peer, key_for_peer))
        key_got, query_got = swap_cores(key_for_peer), swap_cores(query_for_peer)
        key_mine = key_own(place, n1, dq, dkv, mlp.sent)
        mlp.advance((key_mine,))
        (kv_keep, kv_send, q_keep, q_send), _ = advance(
            place,
            [("split", KEY_SLOT, key_mine, key_got), ("split", QUERY_SLOT, query_own, query_got)],
            mlp.sent,
            (),
        )
        qkv = Chain(
            place,
            [(KEY_ORDER, KEY_SLOT, kv_keep, kv_send), (QUERY_ORDER, QUERY_SLOT, q_keep, q_send)],
        )
        grad_tokens = input_part(qkv.sent + mlp.sent)
        deps = (grad_tokens,)
        for index, joint in enumerate(PATTERN):
            if joint:
                advance_both(qkv, mlp, deps)
            else:
                qkv.advance(mlp.got[1:] if index == 4 else deps)
            deps = ()
        grad_in, grad_out, grad_down, in_sums = finish_mlp(
            place, mlp.kept[0], mlp.got[0], mlp.kept[1], mlp.got[1], in_weight, qkv.sent
        )
        grad_qkv, qkv_sums = finish_qkv(
            place, qkv.kept[1], qkv.got[1], qkv.kept[0], qkv.got[0], qkv_weight, (in_sums,)
        )
    else:
        grads = attend_back(1, PAIRS - 1, grads, (), *back_args)
        dq, dkv_own, dkv_peer = grads
        query_for_peer, query_own = query_terms(place, n1, dq, ())
        key_for_peer, dkv = key_terms(place, n1, dq, dkv_own, swap_cores(dkv_peer), cosine, sine, ())
        pieces = []
        for own, for_peer in ((query_own, query_for_peer), (key_own(place, n1, dq, dkv, ()), key_for_peer)):
            total = add(own, swap_cores(for_peer))
            pieces += [total[: HALF // 2], total[HALF // 2 :]]
        grad_tokens = input_part(())
        total = lambda part: lax.psum(part.astype(F32), "rep")
        grad_qkv, qkv_sums = finish_qkv(place, *[total(part) for part in pieces], qkv_weight, ())
        grad_in, grad_out, grad_down, in_sums = finish_mlp(
            place, *[total(part) for part in (wide_keep, wide_send, narrow_keep, narrow_send)], in_weight, ()
        )
    grad_gain_one = qkv_sums[:, 0] / attn_gain.astype(F32)
    grad_gain_two = in_sums[:, 0] / mlp_gain.astype(F32)
    return (
        result,
        grad_tokens,
        grad_gain_one,
        grad_qkv,
        grad_out,
        grad_gain_two,
        grad_in,
        grad_down,
    )


def solution(mesh):
    rows = P(("rep", "fsdp"), None)
    vector, matrix = P("fsdp"), P("fsdp", None)
    in_specs = (rows, vector, matrix, matrix, vector, matrix, matrix, P("rep", None), rows)
    out_specs = (rows, rows, vector, matrix, matrix, vector, matrix, matrix)
    return jax.shard_map(
        on_device, mesh=mesh, in_specs=in_specs, out_specs=out_specs, check_vma=False
    )
```
